128 devices in a mesh: gx: 4 (over z), gy: 4 (over y), gz: 8 (over x, core).
Axes of the slice: x: 4, y: 4, z: 4, core: 2. Of those that a mesh axis runs over, the one named last changes fastest.
Arguments:
- source: float32 [64, 128, 1024], P('gx', 'gy', 'gz'), may hold values from -6 to 6
- conductance: float32 [64, 128, 1024], P('gx', 'gy', 'gz'), may hold values from 0.25 to 4
Outputs:
- solution_field: float32 [64, 128, 1024], P('gx', 'gy', 'gz')
- residual: float32 [64, 128, 1024], P('gx', 'gy', 'gz')
The draws below stay inside these ranges and needn't reach their ends.
All inputs are finite; a program needn't handle non-finite values.
Results may differ from the reference program's by a relative error of at most 0.0003.
Values sent between devices are 32-bit elements; how exact they have to be, the bound alone decides.
No kernel may reach another device: no remote copies, remote signals or barrier semaphores. Data moves between devices by JAX's collectives and lax.ppermute only.
A program may use at most 128 MiB of HBM per device.

```python
import math
import jax
import jax.numpy as jnp
from jax import lax

LEVELS = 4
SWEEPS = 2
COARSE_ITERS = 20
NX = 64
NY = 128
NZ = 1024


def shard_levels(key, shape, cuts, low, largest):
    factor_of, own = 1.0, jax.random.fold_in(key, 6)
    for position, blocks in cuts:
        draws = jnp.exp(jax.random.uniform(jax.random.fold_in(own, position), (blocks,), jnp.float32, low / len(cuts), largest / len(cuts)))
        factor_of = factor_of * jnp.repeat(draws, shape[position] // blocks).reshape([-1 if axis == position else 1 for axis in range(len(shape))])
    return factor_of


def scatter_about(own_key, dims, width, most, cuts=(), held_as=jnp.bfloat16):
    level = shard_levels(own_key, dims, cuts, -0.22, 0.18) if cuts else 1.0
    result = jax.random.normal(own_key, dims, jnp.float32) * width * level
    return jnp.minimum(jnp.maximum(result, -most), most).astype(held_as)


def setup_inputs(seed: int = 0) -> dict:
    splits = jax.random.split(jax.random.key(seed), 3)
    source = scatter_about(splits[0], (NX, NY, NZ), 1.0, 6.0, ((0, 4), (1, 4), (2, 8)), jnp.float32)
    conductance = jnp.clip(jnp.exp(math.log(4.0) - 2.7725887 * jax.random.uniform(splits[1], (NX, NY, NZ), jnp.float32) ** shard_levels(splits[1], (NX, NY, NZ), ((0, 4), (1, 4), (2, 8)), -0.2, 0.2)), 0.25, 4.0)
    return dict(source=source, conductance=conductance)


def coefficients(padded_b):
    center = padded_b[1:-1, 1:-1, 1:-1]
    return (0.5 * (center + padded_b[:-2, 1:-1, 1:-1]), 0.5 * (center + padded_b[2:, 1:-1, 1:-1]),
            0.5 * (center + padded_b[1:-1, :-2, 1:-1]), 0.5 * (center + padded_b[1:-1, 2:, 1:-1]),
            0.5 * (center + padded_b[1:-1, 1:-1, :-2]), 0.5 * (center + padded_b[1:-1, 1:-1, 2:]))


def operate(padded, face_coef, factor):
    center = padded[1:-1, 1:-1, 1:-1]
    beside = (padded[:-2, 1:-1, 1:-1], padded[2:, 1:-1, 1:-1], padded[1:-1, :-2, 1:-1],
              padded[1:-1, 2:, 1:-1], padded[1:-1, 1:-1, :-2], padded[1:-1, 1:-1, 2:])
    summed = face_coef[0] * (center - beside[0])
    for which in range(1, 6):
        summed = summed + face_coef[which] * (center - beside[which])
    return factor * summed


def diagonal_of(face_coef, factor):
    summed = face_coef[0]
    for which in range(1, 6):
        summed = summed + face_coef[which]
    return factor * summed


def checker(shape, offset):
    parity = (lax.broadcasted_iota(jnp.int32, shape, 0) + lax.broadcasted_iota(jnp.int32, shape, 1)
              + lax.broadcasted_iota(jnp.int32, shape, 2) + offset)
    return parity % 2 == 0


def coarsen(field):
    sx, sy, sz = field.shape
    return jnp.sum(field.reshape(sx // 2, 2, sy // 2, 2, sz // 2, 2), axis=(1, 3, 5)) * 0.125


def refine(field):
    return jnp.repeat(jnp.repeat(jnp.repeat(field, 2, 0), 2, 1), 2, 2)


def relax(field, source, face_coef, diagonal, chosen, factor):
    applied = operate(jnp.pad(field, 1), face_coef, factor)
    return jnp.where(chosen, field + (source - applied) / diagonal, field)


def sweep(field, source, face_coef, diagonal, red_cells, factor):
    field = relax(field, source, face_coef, diagonal, red_cells, factor)
    return relax(field, source, face_coef, diagonal, jnp.logical_not(red_cells), factor)


def reference(source, conductance):
    betas = [conductance]
    for level in range(LEVELS):
        betas.append(coarsen(betas[-1]))
    stored = []
    current = source
    for level in range(LEVELS):
        factor = 0.25 ** level
        face_coef = coefficients(jnp.pad(betas[level], 1))
        diagonal = diagonal_of(face_coef, factor)
        red_cells = checker(current.shape, 0)
        field = jnp.zeros_like(current)
        for count in range(SWEEPS):
            field = sweep(field, current, face_coef, diagonal, red_cells, factor)
        applied = operate(jnp.pad(field, 1), face_coef, factor)
        stored.append((field, current, face_coef, diagonal, red_cells, factor))
        current = coarsen(current - applied)
    factor = 0.25 ** LEVELS
    face_coef = coefficients(jnp.pad(betas[LEVELS], 1))
    diagonal = diagonal_of(face_coef, factor)
    red_cells = checker(current.shape, 0)

    def coarse_step(count, field):
        return sweep(field, current, face_coef, diagonal, red_cells, factor)

    coarse = lax.fori_loop(0, COARSE_ITERS, coarse_step, jnp.zeros_like(current))
    for level in range(LEVELS - 1, -1, -1):
        field, here, face_coef, diagonal, red_cells, factor = stored[level]
        field = field + refine(coarse)
        for count in range(SWEEPS):
            field = sweep(field, here, face_coef, diagonal, red_cells, factor)
        coarse = field
    face_coef = stored[0][2]
    residual = source - operate(jnp.pad(coarse, 1), face_coef, 1.0)
    return coarse, residual
```

```python
import functools

import jax
import jax.numpy as jnp
from jax import lax
from jax.experimental import pallas as pl
from jax.experimental.pallas import tpu as pltpu
from jax.sharding import PartitionSpec as P

F32 = jnp.float32
COARSE_ITERS = 20
MIB = 1 << 20


def lanes(rows):
    return lax.broadcasted_iota(jnp.int32, (rows, 128), 1)


def sublanes(rows):
    return lax.broadcasted_iota(jnp.int32, (rows, 128), 0)


def pick(x, idx):
    return jnp.take_along_axis(x, idx, axis=1, mode="promise_in_bounds")


def turn(x, shift):
    shift = shift % 128
    return pltpu.roll(x, shift, 1) if shift else x


def side_index(rows, parity, period):
    lane, row = lanes(rows), sublanes(rows)
    step = 2 * ((row + parity) % 2) - 1
    within = (lane % period + step + period) % period
    return lane - lane % period + within


def call(kernel, out, args, specs=None, scratch=(), limit=40):
    vmem = pl.BlockSpec(memory_space=pltpu.VMEM)
    return pl.pallas_call(
        kernel,
        out_shape=out[0],
        in_specs=specs or [vmem] * len(args),
        out_specs=out[1] if len(out) > 1 else jax.tree.map(lambda _: vmem, out[0]),
        scratch_shapes=scratch,
        compiler_params=pltpu.CompilerParams(vmem_limit_bytes=limit * MIB),
        name=kernel.__name__,
    )(*args)


def arr(*shape):
    return jax.ShapeDtypeStruct(shape, F32)


def split_fine(f_ref, b_ref, wf_ref, wb_ref, lo_ref, hi_ref):
    lane, row = lanes(32), sublanes(32)
    index = []
    for parity in range(2):
        odd = (row + parity) % 2
        index.append(2 * (lane % 64) + jnp.where(lane < 64, odd, 1 - odd))
    for i in range(16):
        wf = pick(f_ref[i], index[i % 2])
        wb = pick(b_ref[i], index[i % 2])
        wf_ref[i] = wf
        wb_ref[i] = wb
        if i < 8:
            lo_ref[i] = wf
        else:
            hi_ref[i - 8] = wf
        if i < 9:
            lo_ref[8 + i] = wb
        if i > 6:
            hi_ref[1 + i] = wb


def plane_f(wf, xl, xu, p):
    return xl.at[p] if p < 8 else wf.at[p - 8] if p < 24 else xu.at[p - 24]


def plane_b(wb, xl, xu, p):
    return xl.at[9 + p] if p < 8 else wb.at[p - 8] if p < 24 else xu.at[8 + p - 24]


def pack_rows(wf, wb, xl, xu, lo_ref, hi_ref):
    for p in range(32):
        f, b = plane_f(wf, xl, xu, p), plane_b(wb, xl, xu, p)
        lo_ref[p] = f[0:8]
        hi_ref[p] = f[24:32]
        lo_ref[32 + p] = b[0:8]
        hi_ref[32 + p] = b[24:32]
    for i in range(16):
        lo_ref[64 + i // 8, i % 8 : i % 8 + 1] = wb[i, 8:9]
        hi_ref[64 + i // 8, i % 8 : i % 8 + 1] = wb[i, 23:24]


def slab(plane, yl, yu, which, p):
    return jnp.concatenate([yl[32 * which + p], plane[...], yu[32 * which + p]], axis=0)


def pack_lanes(wf, wb, xl, xu, yl, yu, lo_ref, hi_ref):
    slot_of = lanes(48) % 64
    for which, width, base in ((0, 4, 0), (1, 8, 12)):
        count = 64 // width
        slot = slot_of // width
        for group in range(32 // count):
            for s in range(count):
                p = group * count + s
                plane = plane_b(wb, xl, xu, p) if which else plane_f(wf, xl, xu, p)
                v = turn(slab(plane, yl, yu, which, p), width * s)
                if s == 0:
                    low = high = v
                else:
                    low = jnp.where(slot == s, v, low)
                    high = jnp.where(slot == s - 1, v, high)
            start = base + 6 * group
            lo_ref[start : start + 6] = low.reshape(6, 8, 128)
            hi_ref[start : start + 6] = high.reshape(6, 8, 128)


def make_coefs(mine, other, f, coef, p, index, scale, rows, inside=None):
    r = slice(8, 8 + rows)
    centre = mine[p + 1, r]
    mid = other[p + 1, r]
    side = pick(mid, index)
    if inside is not None:
        side = jnp.where(inside, side, 0.0)
    beside = (other[p, r], other[p + 2, r], other[p + 1, 7 : 7 + rows], other[p + 1, 9 : 9 + rows], mid, side)
    weights = [centre + b for b in beside]
    total = weights[0]
    for w in weights[1:]:
        total = total + w
    inverse = jnp.where(centre > 0.0, 1.0 / jnp.where(centre > 0.0, total, 1.0), 0.0)
    for which in range(6):
        w = weights[which] * inverse
        if which == 5 and inside is not None:
            w = jnp.where(inside, w, 0.0)
        coef[which, p] = w
    coef[6, p] = f * (inverse * (2.0 / scale))
    coef[7, p] = total * (0.5 * scale)


def relaxed(other, coef, p, index, rows, first=0, shift=0):
    a = 8 + first
    r = slice(a, a + rows)
    c = slice(first, first + rows)
    q = p - shift
    mid = other[p + 1, r]
    out = coef[6, q, c] + coef[0, q, c] * other[p, r]
    out = out + coef[1, q, c] * other[p + 2, r]
    out = out + coef[2, q, c] * other[p + 1, a - 1 : a - 1 + rows]
    out = out + coef[3, q, c] * other[p + 1, a + 1 : a + 1 + rows]
    out = out + coef[4, q, c] * mid
    return out + coef[5, q, c] * pick(mid, index)


def pairs(start, stop, body):
    def step(t, carry):
        for parity in range(2):
            body(2 * t + parity, parity)
        return carry

    lax.fori_loop(start // 2, stop // 2, step, 0)


def update(mine, other, coef, index, start, stop, rows, flip, shift=0):
    def body(p, parity):
        mine[p + 1, 8 : 8 + rows] = relaxed(other, coef, p, index[(parity + flip) % 2], rows, 0, shift)

    pairs(start, stop, body)


def defect(red, black, cr, cb, p, parity, index, rows, first=0, shift=0):
    r = slice(8 + first, 8 + first + rows)
    c = slice(first, first + rows)
    er = cr[7, p - shift, c] * (relaxed(black, cr, p, index[parity], rows, first, shift) - red[p + 1, r])
    eb = cb[7, p - shift, c] * (relaxed(red, cb, p, index[1 - parity], rows, first, shift) - black[p + 1, r])
    return er, eb


def halve_rows(tmp, value, rows):
    tmp[0:rows] = value
    return 0.125 * (tmp[pl.ds(0, rows // 2, 2)] + tmp[pl.ds(1, rows // 2, 2)])


def double_rows(tmp, value, rows):
    tmp[pl.ds(0, rows, 2)] = value
    tmp[pl.ds(1, rows, 2)] = value


def fine_down(
    at, wf, wb, xl, xu, yl, yu, zl, zu, g_ref, cr_out, cb_out, vb_out, br, bb, fr, fb, cr, cb, vr, vb, tmp, sems
):
    gx, gy, gz = at[0], at[1], at[2]
    lane, row = lanes(48), sublanes(48)
    own = lane < 64
    keep = own | ((lane < 96) & (gz < 7)) | ((lane >= 96) & (gz > 0))
    keep = keep & ((row >= 8) | (gy > 0)) & ((row < 40) | (gy < 3))
    kept = jnp.where(keep, 1.0, 0.0).astype(F32)
    below = jnp.where(gx > 0, 1.0, 0.0).astype(F32)
    above = jnp.where(gx < 3, 1.0, 0.0).astype(F32)
    left = jnp.where(gy > 0, 1.0, 0.0).astype(F32)
    right = jnp.where(gy < 3, 1.0, 0.0).astype(F32)
    vr[...] = jnp.zeros_like(vr)
    vb[...] = jnp.zeros_like(vb)
    edge = jnp.zeros((8, 128), F32)
    for b in (br, bb):
        for q in range(34):
            b[q, 0:8] = edge
            b[q, 56:64] = edge
        for q in (0, 33):
            b[q, 8:56] = jnp.zeros((48, 128), F32)
    for which, width, base in ((0, 4, 0), (1, 8, 12)):
        count = 64 // width
        slot = (lane % 64) // width
        for p in range(32):
            plane = plane_b(wb, xl, xu, p) if which else plane_f(wf, xl, xu, p)
            w = slab(plane, yl, yu, which, p)
            s = p % count
            start = base + 6 * (p // count)
            up = zu[start : start + 6].reshape(48, 128)
            low = zl[start : start + 6].reshape(48, 128)
            both = jnp.where(slot == s, up, low)
            red = jnp.where(own, w, turn(both, 64 - width * s))
            black = jnp.where(own, turn(w, 64), turn(both, -width * s))
            if which:
                k = kept * below if p < 8 else kept * above if p >= 24 else kept
                br[p + 1, 8:56] = red * k
                bb[p + 1, 8:56] = black * k
            else:
                fr[p] = red
                fb[p] = black
    for a in range(2):
        for src, r, ok in ((yl, 7, left), (yu, 56, right)):
            v = src[64 + a] * ok
            t = turn(v, 64)
            for s in range(8):
                br[9 + 8 * a + s, r : r + 1] = v[s : s + 1]
                bb[9 + 8 * a + s, r : r + 1] = t[s : s + 1]
    for v, q in ((xl[8] * below, 0), (xu[16] * above, 33)):
        br[q, 16:48] = v
        bb[q, 16:48] = turn(v, 64)

    index = [side_index(48, parity, 128) for parity in range(2)]

    def coefs(p, parity):
        make_coefs(br, bb, fr[p], cr, p, index[parity], 1.0, 48)
        make_coefs(bb, br, fb[p], cb, p, index[1 - parity], 1.0, 48)
        vr[p + 1, 8:56] = cr[6, p]

    pairs(0, 32, coefs)
    copies = [
        pltpu.make_async_copy(cr.at[:, pl.ds(4, 24)], cr_out, sems.at[0]),
        pltpu.make_async_copy(cb.at[:, pl.ds(4, 24)], cb_out, sems.at[1]),
        pltpu.make_async_copy(vb, vb_out, sems.at[2]),
    ]
    copies[0].start()
    copies[1].start()
    update(vb, vr, cb, index, 0, 32, 48, 1)
    update(vr, vb, cr, index, 2, 30, 48, 0)
    update(vb, vr, cb, index, 2, 30, 48, 1)
    copies[2].start()

    lane, row = lanes(16), sublanes(16)
    inner = [side_index(32, parity, 128) for parity in range(2)]
    swap = jnp.where(gx >= 2, 64, 0)
    for n in range(8):
        total = coarse = None
        for parity in range(2):
            p = 8 + 2 * n + parity
            er, eb = defect(vr, vb, cr, cb, p, parity, inner, 32, 8)
            e = er + eb
            b = br[p + 1, 16:48] + bb[p + 1, 16:48]
            total = e if total is None else total + e
            coarse = b if coarse is None else coarse + b
        f1 = halve_rows(tmp, total, 32)
        b1 = halve_rows(tmp, coarse, 32)
        odd = (row + n) % 2
        idx = 64 * (lane // 64) + 2 * (lane % 32) + jnp.where(lane % 64 < 32, odd, 1 - odd)
        w1 = pick(jnp.where(lane < 64, f1, turn(b1, 64)), idx ^ swap)
        for copy in range(16):
            g_ref[copy, n] = w1
    for c in copies:
        c.wait()


def joined(g, p):
    a, i = p // 8, p % 8
    wa = jnp.concatenate([g[4 * a + y, i] for y in range(4)], axis=0)
    wb = jnp.concatenate([g[4 * (a + 2) + y, i] for y in range(4)], axis=0)
    half = lanes(64) < 64
    return jnp.where(half, wa, wb), jnp.where(half, wb, wa)


def pack_mid(g, lo_ref, hi_ref):
    slot = (lanes(64) % 32) // 8
    for group in range(4):
        low, high = [None] * 2, [None] * 2
        for s in range(4):
            for which, v in enumerate(joined(g, 4 * group + s)):
                v = turn(v, 8 * s)
                low[which] = v if s == 0 else jnp.where(slot == s, v, low[which])
                high[which] = v if s == 0 else jnp.where(slot == s - 1, v, high[which])
        for which in range(2):
            lo_ref[which, group] = low[which]
            hi_ref[which, group] = high[which]


def seam(v, rows):
    r = slice(8, 8 + rows)
    half = lanes(rows) < 64
    v[0, r] = jnp.where(half, 0.0, turn(v[16, r], 64))
    v[17, r] = jnp.where(half, turn(v[1, r], 64), 0.0)


def mid_down(at, g, zl, zu, w2_ref, cr_out, cb_out, vb_out, br, bb, fr, fb, cr, cb, vr, vb, tmp, sems):
    gy, gz = at[1], at[2]
    lane = lanes(64)
    own = lane % 64 < 32
    keep = own | ((lane % 64 < 48) & (gz < 7)) | ((lane % 64 >= 48) & (gz > 0))
    kept = jnp.where(keep, 1.0, 0.0).astype(F32)
    slot = (lane % 32) // 8
    for v in (vr, vb):
        v[...] = jnp.zeros_like(v)
    for b in (br, bb):
        b[:, 0:8] = jnp.zeros((18, 8, 128), F32)
        b[:, 72:80] = jnp.zeros((18, 8, 128), F32)
    for p in range(16):
        mf, mb = joined(g, p)
        s, group = p % 4, p // 4
        both = jnp.where(slot == s, zu[0, group], zl[0, group])
        fr[p] = jnp.where(own, mf, turn(both, 32 - 8 * s))
        fb[p] = jnp.where(own, turn(mf, 96), turn(both, -8 * s))
        both = jnp.where(slot == s, zu[1, group], zl[1, group])
        br[p + 1, 8:72] = kept * jnp.where(own, turn(mb, 64), turn(both, 96 - 8 * s))
        bb[p + 1, 8:72] = kept * jnp.where(own, turn(mb, 32), turn(both, 64 - 8 * s))
    seam(br, 64)
    seam(bb, 64)
    index = [side_index(64, parity, 64) for parity in range(2)]

    def coefs(p, parity):
        make_coefs(br, bb, fr[p], cr, p, index[parity], 0.25, 64)
        make_coefs(bb, br, fb[p], cb, p, index[1 - parity], 0.25, 64)
        vr[p + 1, 8:72] = cr[6, p]

    pairs(0, 16, coefs)
    seam(vr, 64)
    window = pl.multiple_of(jnp.clip(gy * 16 - 8, 0, 32), 8)
    copies = [
        pltpu.make_async_copy(cr.at[:, :, pl.ds(window, 32)], cr_out, sems.at[0]),
        pltpu.make_async_copy(cb.at[:, :, pl.ds(window, 32)], cb_out, sems.at[1]),
        pltpu.make_async_copy(vb.at[:, pl.ds(window + 8, 32)], vb_out, sems.at[2]),
    ]
    copies[0].start()
    copies[1].start()
    update(vb, vr, cb, index, 0, 16, 64, 1)
    seam(vb, 64)
    update(vr, vb, cr, index, 0, 16, 64, 0)
    seam(vr, 64)
    update(vb, vr, cb, index, 0, 16, 64, 1)
    seam(vb, 64)
    copies[2].start()
    lane, row = lanes(32), sublanes(32)
    for n in range(8):
        total = coarse = None
        for parity in range(2):
            p = 2 * n + parity
            er, eb = defect(vr, vb, cr, cb, p, parity, index, 64)
            e = er + eb
            b = br[p + 1, 8:72] + bb[p + 1, 8:72]
            total = e if total is None else total + e
            coarse = b if coarse is None else coarse + b
        f2 = halve_rows(tmp, total, 64)
        b2 = halve_rows(tmp, coarse, 64)
        odd = (row + n) % 2
        idx = 64 * ((lane % 64) // 32) + 2 * (lane % 16) + jnp.where(lane % 32 < 16, odd, 1 - odd)
        w2 = jnp.where(lane < 64, pick(f2, idx), pick(b2, idx))
        for copy in range(4):
            w2_ref[copy, n] = w2
    for c in copies:
        c.wait()


def transposed(blocks):
    slot = lanes(32) // 16
    for bit in (1, 2, 4):
        out = list(blocks)
        for i in range(8):
            if not i & bit:
                x, y = blocks[i], blocks[i + bit]
                out[i] = jnp.where(slot & bit == 0, x, turn(y, 16 * bit))
                out[i + bit] = jnp.where(slot & bit == 0, turn(x, -16 * bit), y)
        blocks = out
    return blocks


def level_scratch(planes, rows):
    return [pltpu.VMEM((planes + 2, rows + 16, 128), F32)] * 4 + [pltpu.VMEM((8, planes, rows, 128), F32)] * 2


def clear(refs):
    for v in refs:
        v[...] = jnp.zeros_like(v)


def smooth_down(br, bb, vr, vb, cr, cb, f_of, index, scale, planes, rows, inside):
    def coefs(p, parity):
        fr, fb = f_of(p)
        make_coefs(br, bb, fr, cr, p, index[parity], scale, rows, inside and inside[parity])
        make_coefs(bb, br, fb, cb, p, index[1 - parity], scale, rows, inside and inside[1 - parity])
        vr[p + 1, 8 : 8 + rows] = cr[6, p]

    pairs(0, planes, coefs)
    update(vb, vr, cb, index, 0, planes, rows, 1)
    update(vr, vb, cr, index, 0, planes, rows, 0)
    update(vb, vr, cb, index, 0, planes, rows, 1)


def smooth_up(vr, vb, cr, cb, index, planes, rows):
    for _ in range(2):
        update(vr, vb, cr, index, 0, planes, rows, 0)
        update(vb, vr, cb, index, 0, planes, rows, 1)


def restrict(level, tmp, index, planes, rows, cells, put):
    br, bb, vr, vb, cr, cb = level
    lane, row = lanes(rows // 2), sublanes(rows // 2)
    for n in range(planes // 2):
        total = coarse = None
        for parity in range(2):
            p = 2 * n + parity
            er, eb = defect(vr, vb, cr, cb, p, parity, index, rows)
            b = br[p + 1, 8 : 8 + rows] + bb[p + 1, 8 : 8 + rows]
            total = er + eb if total is None else total + (er + eb)
            coarse = b if coarse is None else coarse + b
        f = halve_rows(tmp, total, rows)
        b = halve_rows(tmp, coarse, rows)
        odd = (row + n) % 2
        red = 2 * (lane % 64) + odd
        black = 2 * (lane % 64) + 1 - odd
        inside = lane < cells
        put(n, *[jnp.where(inside, pick(x, i), 0.0) for x in (f, b) for i in (red, black)])


def prolong(vr, vb, out, tmp, planes, rows):
    lane, row = lanes(rows), sublanes(rows)
    r = slice(8, 8 + rows)
    for n in range(planes):
        even = (row + lane + n) % 2 == 0
        c = jnp.where(even, pick(vr[n + 1, r], lane // 2), pick(vb[n + 1, r], lane // 2))
        double_rows(tmp, c, rows)
        for p in (2 * n, 2 * n + 1):
            out[p + 1, 8 : 8 + 2 * rows] += tmp[0 : 2 * rows]


def coarse_up(
    at, mine, pair, c1r_in, c1b_in, v1b_in, c0r_in, c0b_in, v0b_in, u_ref, res_ref,
    b2r, b2b, v2r, v2b, c2r, c2b, f2,
    b3r, b3b, v3r, v3b, c3r, c3b, f3,
    b4r, b4b, v4r, v4b, c4r, c4b, f4,
    v1r, v1b, c1r, c1b, v0r, v0b, c0r, c0b, tmp, sems,
):
    gx, gy, gz = at[0], at[1], at[2]
    copies = [
        pltpu.make_async_copy(c1r_in, c1r, sems.at[0]),
        pltpu.make_async_copy(c1b_in, c1b, sems.at[1]),
        pltpu.make_async_copy(v1b_in, v1b.at[:, pl.ds(8, 32)], sems.at[2]),
        pltpu.make_async_copy(c0r_in, c0r, sems.at[3]),
        pltpu.make_async_copy(c0b_in, c0b, sems.at[4]),
        pltpu.make_async_copy(v0b_in, v0b, sems.at[5]),
    ]
    for c in copies:
        c.start()
    clear((b2r, b2b, v2r, v2b, b3r, b3b, v3r, v3b, b4r, b4b, v4r, v4b, v1r, v0r))
    v1b[:, 0:8] = jnp.zeros((18, 8, 128), F32)
    v1b[:, 40:48] = jnp.zeros((18, 8, 128), F32)

    first = gz % 2 == 0
    for n in range(8):
        blocks = []
        for chip in range(4):
            a, b = mine[chip, n], pair[chip, n]
            blocks += [jnp.where(first, a, b), jnp.where(first, b, a)]
        out = transposed(blocks)
        for h in range(2):
            p = n + 8 * h
            f2[0, p] = out[2 * h]
            f2[1, p] = out[2 * h + 1]
            b2r[p + 1, 8:40] = out[4 + 2 * h]
            b2b[p + 1, 8:40] = out[5 + 2 * h]
    lane = lanes(32)
    index2 = [side_index(32, parity, 128) for parity in range(2)]
    inside2 = [jnp.abs(index2[parity] - lane) < 64 for parity in range(2)]
    smooth_down(b2r, b2b, v2r, v2b, c2r, c2b, lambda p: (f2[0, p], f2[1, p]), index2, 0.25**2, 16, 32, inside2)

    def put3(n, fr, fb, br, bb):
        f3[0, n], f3[1, n] = fr, fb
        b3r[n + 1, 8:24], b3b[n + 1, 8:24] = br, bb

    restrict((b2r, b2b, v2r, v2b, c2r, c2b), tmp, index2, 16, 32, 64, put3)

    index3 = [side_index(16, parity, 128) for parity in range(2)]
    smooth_down(b3r, b3b, v3r, v3b, c3r, c3b, lambda p: (f3[0, p], f3[1, p]), index3, 0.25**3, 8, 16, None)

    def put4(n, fr, fb, br, bb):
        f4[0, n], f4[1, n] = fr, fb
        b4r[n + 1, 8:16], b4b[n + 1, 8:16] = br, bb

    restrict((b3r, b3b, v3r, v3b, c3r, c3b), tmp, index3, 8, 16, 32, put4)

    index4 = [side_index(8, parity, 128) for parity in range(2)]

    for p in range(4):
        make_coefs(b4r, b4b, f4[0, p], c4r, p, index4[p % 2], 0.25**4, 8)
        make_coefs(b4b, b4r, f4[1, p], c4b, p, index4[1 - p % 2], 0.25**4, 8)
    row8 = sublanes(8)
    inner = (row8 > 0, row8 < 7)
    cr4 = [[c4r[w, p] for w in range(7)] for p in range(4)]
    cb4 = [[c4b[w, p] for w in range(7)] for p in range(4)]
    for c in cr4 + cb4:
        c[2] = jnp.where(inner[0], c[2], 0.0)
        c[3] = jnp.where(inner[1], c[3], 0.0)

    def half(other, coefs, flip):
        out = []
        for p in range(4):
            c, v = coefs[p], other[p]
            w = c[6] + c[4] * v
            if p > 0:
                w = w + c[0] * other[p - 1]
            if p < 3:
                w = w + c[1] * other[p + 1]
            w = w + c[2] * pltpu.roll(v, 1, 0) + c[3] * pltpu.roll(v, 7, 0)
            out.append(w + c[5] * pick(v, index4[(p + flip) % 2]))
        return out

    def coarse_step(count, state):
        black = list(state)
        red = half(black, cr4, 0)
        return tuple(half(red, cb4, 1))

    black = lax.fori_loop(0, COARSE_ITERS - 1, coarse_step, (jnp.zeros((8, 128), F32),) * 4)
    red = half(black, cr4, 0)
    black = half(red, cb4, 1)
    for p in range(4):
        v4r[p + 1, 8:16] = red[p]
        v4b[p + 1, 8:16] = black[p]

    prolong(v4r, v4b, v3b, tmp, 4, 8)
    smooth_up(v3r, v3b, c3r, c3b, index3, 8, 16)
    prolong(v3r, v3b, v2b, tmp, 8, 16)
    smooth_up(v2r, v2b, c2r, c2b, index2, 16, 32)

    for c in copies[:3]:
        c.wait()
    lane, row = lanes(32), sublanes(32)
    near = lane % 64 - jnp.where(lane % 64 < 48, 0, 64)
    cell = gz * 32 + near
    valid = (cell >= 0) & (cell < 256)
    idx = jnp.clip(cell, 0, 255) // 2
    window = pl.multiple_of(jnp.clip(gy * 16 - 8, 0, 32), 8)
    for n in range(8):
        even = (row + lane + n) % 2 == 0
        parts = []
        for p in (n, n + 8):
            parts.append(jnp.where(even, pick(v2r[p + 1, 8:40], idx), pick(v2b[p + 1, 8:40], idx)))
        c = jnp.where(valid, jnp.where(lane < 64, parts[0], parts[1]), 0.0)
        double_rows(tmp, c, 32)
        for p in (2 * n, 2 * n + 1):
            v1b[p + 1, 8:40] += tmp[pl.ds(window, 32)]
    seam(v1b, 32)
    index1 = [side_index(32, parity, 64) for parity in range(2)]
    for _ in range(2):
        update(v1r, v1b, c1r, index1, 0, 16, 32, 0)
        seam(v1r, 32)
        update(v1b, v1r, c1b, index1, 0, 16, 32, 1)
        seam(v1b, 32)

    for c in copies[3:]:
        c.wait()
    start = pl.multiple_of(gy * 16 - window, 8)
    cell = lane - jnp.where(lane < 96, 0, 128)
    idx = (cell // 2) % 64
    for n in range(-3, 11):
        plane = gx * 8 + n
        held = jnp.clip(plane, 0, 31)
        at_half = idx + 64 * (held // 16)
        even = (row + lane + n) % 2 == 0
        red = v1r[held % 16 + 1, pl.ds(start, 32)]
        black = v1b[held % 16 + 1, pl.ds(start, 32)]
        c = jnp.where(even, pick(red, at_half), pick(black, at_half))
        c = c * jnp.where((plane >= 0) & (plane < 32), 1.0, 0.0).astype(F32)
        tmp[64:96] = c
        double_rows(tmp, tmp[68:92], 24)
        for p in (2 * n + 8, 2 * n + 9):
            v0b[p + 1, 8:56] += tmp[0:48]
    index0 = [side_index(48, parity, 128) for parity in range(2)]
    update(v0r, v0b, c0r, index0, 4, 28, 48, 0, 4)
    update(v0b, v0r, c0b, index0, 4, 28, 48, 1, 4)
    update(v0r, v0b, c0r, index0, 6, 26, 48, 0, 4)
    update(v0b, v0r, c0b, index0, 6, 26, 48, 1, 4)

    def finish(p, parity):
        even = (row + lane + parity) % 2 == 0
        er, eb = defect(v0r, v0b, c0r, c0b, p, parity, index1_0, 32, 8, 4)
        res_ref[p - 8] = jnp.where(even, pick(er, lane // 2), pick(eb, lane // 2))
        red, black = v0r[p + 1, 16:48], v0b[p + 1, 16:48]
        u_ref[p - 8] = jnp.where(even, pick(red, lane // 2), pick(black, lane // 2))

    index1_0 = [side_index(32, parity, 128) for parity in range(2)]
    pairs(8, 24, finish)


def around(lo, hi, axis):
    count = lax.axis_size(axis)
    from_above = lax.ppermute(lo, axis, [((i + 1) % count, i) for i in range(count)])
    from_below = lax.ppermute(hi, axis, [(i, (i + 1) % count) for i in range(count)])
    return from_below, from_above


def body(source, conductance):
    vmem, smem, anywhere = (pl.BlockSpec(memory_space=m) for m in (pltpu.VMEM, pltpu.SMEM, pl.ANY))
    at = jnp.stack([lax.axis_index(a) for a in ("gx", "gy", "gz")]).astype(jnp.int32)
    dma = pltpu.SemaphoreType.DMA

    block, x_slab = arr(16, 32, 128), arr(17, 32, 128)
    wf, wb, lo, hi = call(split_fine, [(block, block, x_slab, x_slab)], (source, conductance))
    xl, xu = around(lo, hi, "gx")
    lo, hi = call(pack_rows, [(arr(66, 8, 128),) * 2], (wf, wb, xl, xu))
    yl, yu = around(lo, hi, "gy")
    lo, hi = call(pack_lanes, [(arr(36, 8, 128),) * 2], (wf, wb, xl, xu, yl, yu))
    zl, zu = around(lo, hi, "gz")

    state0 = (arr(8, 24, 48, 128), arr(8, 24, 48, 128), arr(34, 64, 128))
    colour0 = pltpu.VMEM((34, 64, 128), F32)
    right0 = pltpu.VMEM((32, 48, 128), F32)
    coef0 = pltpu.VMEM((8, 32, 48, 128), F32)
    g, c0r, c0b, v0b = call(
        fine_down,
        [(arr(16, 8, 16, 128),) + state0, (vmem, anywhere, anywhere, anywhere)],
        (at, wf, wb, xl, xu, yl, yu, zl, zu),
        [smem] + [vmem] * 8,
        [colour0, colour0, right0, right0, coef0, coef0, colour0, colour0, pltpu.VMEM((32, 128), F32), dma((3,))],
    )
    g = lax.all_to_all(g, ("gx", "gy"), 0, 0, tiled=True)
    lo, hi = call(pack_mid, [(arr(2, 4, 64, 128),) * 2], (g,))
    zl, zu = around(lo, hi, "gz")

    state1 = (arr(8, 16, 32, 128), arr(8, 16, 32, 128), arr(18, 32, 128))
    colour1 = pltpu.VMEM((18, 80, 128), F32)
    right1 = pltpu.VMEM((16, 64, 128), F32)
    coef1 = pltpu.VMEM((8, 16, 64, 128), F32)
    w2, c1r, c1b, v1b = call(
        mid_down,
        [(arr(4, 8, 32, 128),) + state1, (vmem, anywhere, anywhere, anywhere)],
        (at, g, zl, zu),
        [smem] + [vmem] * 3,
        [colour1, colour1, right1, right1, coef1, coef1, colour1, colour1, pltpu.VMEM((64, 128), F32), dma((3,))],
    )
    mine = lax.all_to_all(w2, "gz", 0, 0, axis_index_groups=[[0, 2, 4, 6], [1, 3, 5, 7]], tiled=True)
    pair = lax.ppermute(mine, "gz", [(i, i ^ 1) for i in range(8)])

    scratch = []
    for planes, rows in ((16, 32), (8, 16), (4, 8)):
        scratch += level_scratch(planes, rows) + [pltpu.VMEM((2, planes, rows, 128), F32)]
    scratch += [pltpu.VMEM((18, 48, 128), F32)] * 2 + [pltpu.VMEM((8, 16, 32, 128), F32)] * 2
    scratch += [colour0] * 2 + [pltpu.VMEM((8, 24, 48, 128), F32)] * 2
    scratch += [pltpu.VMEM((96, 128), F32), dma((6,))]
    return call(
        coarse_up,
        [(block, block)],
        (at, mine, pair, c1r, c1b, v1b, c0r, c0b, v0b),
        [smem, vmem, vmem] + [anywhere] * 6,
        scratch,
    )


def solution(mesh):
    placed = (P("gx", "gy", "gz"), P("gx", "gy", "gz"))
    return jax.shard_map(body, mesh=mesh, in_specs=placed, out_specs=placed, check_vma=False)
```

```python
import functools

import jax
import jax.numpy as jnp
from jax import lax
from jax.experimental import pallas as pl
from jax.experimental.pallas import tpu as pltpu
from jax.sharding import PartitionSpec as P

F32 = jnp.float32
COARSE_ITERS = 20
MIB = 1 << 20
GROUP = 64
LIMIT = 50


def lanes(rows):
    return lax.broadcasted_iota(jnp.int32, (rows, 128), 1)


def sublanes(rows):
    return lax.broadcasted_iota(jnp.int32, (rows, 128), 0)


def pick(x, idx):
    return jnp.take_along_axis(x, idx, axis=1, mode="promise_in_bounds")


def turn(x, shift):
    shift = shift % 128
    return pltpu.roll(x, shift, 1) if shift else x


def side_index(rows, parity, period):
    lane, row = lanes(rows), sublanes(rows)
    step = 2 * ((row + parity) % 2) - 1
    within = (lane % period + step + period) % period
    return lane - lane % period + within


def call(kernel, out, args, specs=None, scratch=(), limit=40):
    vmem = pl.BlockSpec(memory_space=pltpu.VMEM)
    return pl.pallas_call(
        kernel,
        out_shape=out[0],
        in_specs=specs or [vmem] * len(args),
        out_specs=out[1] if len(out) > 1 else jax.tree.map(lambda _: vmem, out[0]),
        scratch_shapes=scratch,
        compiler_params=pltpu.CompilerParams(vmem_limit_bytes=limit * MIB),
        name=kernel.__name__,
    )(*args)


def arr(*shape):
    return jax.ShapeDtypeStruct(shape, F32)


def split_fine(f_in, b_in, wf_ref, wb_ref, lo_ref, hi_ref, b1_ref, f_ref, b_ref, tmp, sems):
    loads = [pltpu.make_async_copy(b_in, b_ref, sems.at[0]), pltpu.make_async_copy(f_in, f_ref, sems.at[1])]
    for c in loads:
        c.start()
    lane, row = lanes(32), sublanes(32)
    index = []
    for parity in range(2):
        odd = (row + parity) % 2
        index.append(2 * (lane % 64) + jnp.where(lane < 64, odd, 1 - odd))
    loads[0].wait()
    for n in range(8):
        w = [pick(b_ref[2 * n + parity], index[parity]) for parity in range(2)]
        for parity in range(2):
            i = 2 * n + parity
            wb_ref[i] = w[parity]
            if i < 9:
                lo_ref[8 + i] = w[parity]
            if i > 6:
                hi_ref[1 + i] = w[parity]
        both = w[0] + w[1]
        b1 = halve_rows(tmp, both + turn(both, 64), 32)
        b1_ref[16 * n : 16 * n + 16] = pick(b1, by_colour(n, False))
    loads[1].wait()
    for i in range(16):
        wf = pick(f_ref[i], index[i % 2])
        wf_ref[i] = wf
        if i < 8:
            lo_ref[i] = wf
        else:
            hi_ref[i - 8] = wf


def by_colour(n, swap):
    lane, row = lanes(16), sublanes(16)
    odd = (row + n) % 2
    return (2 * (lane % 64) + jnp.where((lane < 64) != swap, odd, 1 - odd)) % 128


def spared(index):
    return (index + jnp.where(lanes(16) % 64 < 48, -12, 12)) % 128


def plane_f(wf, xl, xu, p):
    return xl.at[p] if p < 8 else wf.at[p - 8] if p < 24 else xu.at[p - 24]


def plane_b(wb, xl, xu, p):
    return xl.at[9 + p] if p < 8 else wb.at[p - 8] if p < 24 else xu.at[8 + p - 24]


def pack_rows(wf, wb, xl, xu, lo_ref, hi_ref):
    for p in range(32):
        f, b = plane_f(wf, xl, xu, p), plane_b(wb, xl, xu, p)
        lo_ref[p] = f[0:8]
        hi_ref[p] = f[24:32]
        lo_ref[32 + p] = b[0:8]
        hi_ref[32 + p] = b[24:32]
    for i in range(16):
        lo_ref[64 + i // 8, i % 8 : i % 8 + 1] = wb[i, 8:9]
        hi_ref[64 + i // 8, i % 8 : i % 8 + 1] = wb[i, 23:24]


def slab(plane, yl, yu, which, p):
    return jnp.concatenate([yl[32 * which + p], plane[...], yu[32 * which + p]], axis=0)


def pack_lanes(wf, wb, xl, xu, yl, yu, lo_ref, hi_ref):
    slot_of = lanes(48) % 64
    for which, width, base in ((0, 16, 0), (1, 16, 48)):
        count = 64 // width
        slot = slot_of // width
        for group in range(32 // count):
            for s in range(count):
                p = group * count + s
                plane = plane_b(wb, xl, xu, p) if which else plane_f(wf, xl, xu, p)
                v = turn(slab(plane, yl, yu, which, p), width * s)
                if s == 0:
                    low = high = v
                else:
                    low = jnp.where(slot == s, v, low)
                    high = jnp.where(slot == s - 1, v, high)
            start = base + 6 * group
            lo_ref[start : start + 6] = low.reshape(6, 8, 128)
            hi_ref[start : start + 6] = high.reshape(6, 8, 128)


def make_coefs(mine, other, f, coef, p, index, scale, rows, inside=None):
    r = slice(8, 8 + rows)
    centre = mine[p + 1, r]
    mid = other[p + 1, r]
    side = pick(mid, index)
    if inside is not None:
        side = jnp.where(inside, side, 0.0)
    beside = (other[p, r], other[p + 2, r], other[p + 1, 7 : 7 + rows], other[p + 1, 9 : 9 + rows], mid, side)
    weights = [centre + b for b in beside]
    total = weights[0]
    for w in weights[1:]:
        total = total + w
    inverse = jnp.where(centre > 0.0, 1.0 / jnp.where(centre > 0.0, total, 1.0), 0.0)
    for which in range(6):
        w = weights[which] * inverse
        if which == 5 and inside is not None:
            w = jnp.where(inside, w, 0.0)
        coef[which, p] = w
    coef[6, p] = f * (inverse * (2.0 / scale))
    coef[7, p] = total * (0.5 * scale)


def relaxed(other, coef, p, index, rows, first=0, shift=0):
    a = 8 + first
    r = slice(a, a + rows)
    c = slice(first, first + rows)
    q = p - shift
    mid = other[p + 1, r]
    out = coef[6, q, c] + coef[0, q, c] * other[p, r]
    out = out + coef[1, q, c] * other[p + 2, r]
    out = out + coef[2, q, c] * other[p + 1, a - 1 : a - 1 + rows]
    out = out + coef[3, q, c] * other[p + 1, a + 1 : a + 1 + rows]
    out = out + coef[4, q, c] * mid
    return out + coef[5, q, c] * pick(mid, index)


def pairs(start, stop, body, rows):
    count = stop - start
    width = max(w for w in (2, 4, 8, 16) if w == 2 or (count % w == 0 and w * rows <= 8 * GROUP))

    def step(t, carry):
        for n in range(width):
            body(start + t * width + n, n % 2)
        return carry

    if count == width:
        step(0, 0)
    else:
        lax.fori_loop(0, count // width, step, 0)


def update(mine, other, coef, index, start, stop, rows, flip, shift=0):
    def body(p, parity):
        mine[p + 1, 8 : 8 + rows] = relaxed(other, coef, p, index[(parity + flip) % 2], rows, 0, shift)

    pairs(start, stop, body, rows)


def defect(red, black, cr, cb, p, parity, index, rows, first=0, shift=0):
    r = slice(8 + first, 8 + first + rows)
    c = slice(first, first + rows)
    er = cr[7, p - shift, c] * (relaxed(black, cr, p, index[parity], rows, first, shift) - red[p + 1, r])
    eb = cb[7, p - shift, c] * (relaxed(red, cb, p, index[1 - parity], rows, first, shift) - black[p + 1, r])
    return er, eb


def halve_rows(tmp, value, rows):
    tmp[0:rows] = value
    return 0.125 * (tmp[pl.ds(0, rows // 2, 2)] + tmp[pl.ds(1, rows // 2, 2)])


def double_rows(tmp, value, rows):
    tmp[pl.ds(0, rows, 2)] = value
    tmp[pl.ds(1, rows, 2)] = value


def fine_down(
    at, wf, wb, xl, xu, yl, yu, zl, zu, g_ref, cr_out, cb_out, vb_out, br, bb, fr, fb, cr, cb, vr, vb, tmp, sems
):
    gx, gy, gz = at[0], at[1], at[2]
    lane, row = lanes(48), sublanes(48)
    own = lane < 64
    keep = own | ((lane < 96) & (gz < 7)) | ((lane >= 96) & (gz > 0))
    keep = keep & ((row >= 8) | (gy > 0)) & ((row < 40) | (gy < 3))
    kept = jnp.where(keep, 1.0, 0.0).astype(F32)
    below = jnp.where(gx > 0, 1.0, 0.0).astype(F32)
    above = jnp.where(gx < 3, 1.0, 0.0).astype(F32)
    left = jnp.where(gy > 0, 1.0, 0.0).astype(F32)
    right = jnp.where(gy < 3, 1.0, 0.0).astype(F32)
    vr[...] = jnp.zeros_like(vr)
    vb[...] = jnp.zeros_like(vb)
    edge = jnp.zeros((8, 128), F32)
    for b in (br, bb):
        for q in range(34):
            b[q, 0:8] = edge
            b[q, 56:64] = edge
        for q in (0, 33):
            b[q, 8:56] = jnp.zeros((48, 128), F32)
    for which, width, base in ((0, 16, 0), (1, 16, 48)):
        count = 64 // width
        slot = (lane % 64) // width
        for p in range(32):
            plane = plane_b(wb, xl, xu, p) if which else plane_f(wf, xl, xu, p)
            w = slab(plane, yl, yu, which, p)
            s = p % count
            start = base + 6 * (p // count)
            up = zu[start : start + 6].reshape(48, 128)
            low = zl[start : start + 6].reshape(48, 128)
            both = jnp.where(slot == s, up, low)
            red = jnp.where(own, w, turn(both, 64 - width * s))
            black = jnp.where(own, turn(w, 64), turn(both, -width * s))
            if which:
                k = kept * below if p < 8 else kept * above if p >= 24 else kept
                br[p + 1, 8:56] = red * k
                bb[p + 1, 8:56] = black * k
            else:
                fr[p] = red
                fb[p] = black
    for a in range(2):
        for src, r, ok in ((yl, 7, left), (yu, 56, right)):
            v = src[64 + a] * ok
            t = turn(v, 64)
            for s in range(8):
                br[9 + 8 * a + s, r : r + 1] = v[s : s + 1]
                bb[9 + 8 * a + s, r : r + 1] = t[s : s + 1]
    for v, q in ((xl[8] * below, 0), (xu[16] * above, 33)):
        br[q, 16:48] = v
        bb[q, 16:48] = turn(v, 64)

    index = [side_index(48, parity, 128) for parity in range(2)]

    def coefs(p, parity):
        make_coefs(br, bb, fr[p], cr, p, index[parity], 1.0, 48)
        make_coefs(bb, br, fb[p], cb, p, index[1 - parity], 1.0, 48)
        vr[p + 1, 8:56] = cr[6, p]

    pairs(0, 32, coefs, 48)
    copies = [
        pltpu.make_async_copy(cr.at[:, pl.ds(4, 24)], cr_out, sems.at[0]),
        pltpu.make_async_copy(cb.at[:, pl.ds(4, 24)], cb_out, sems.at[1]),
        pltpu.make_async_copy(vb, vb_out, sems.at[2]),
    ]
    copies[0].start()
    copies[1].start()
    update(vb, vr, cb, index, 0, 32, 48, 1)
    update(vr, vb, cr, index, 2, 30, 48, 0)
    update(vb, vr, cb, index, 2, 30, 48, 1)
    copies[2].start()
    inner = [side_index(32, parity, 128) for parity in range(2)]
    swap = gx >= 2
    spare = (lanes(16) % 64 >= 38) & (lanes(16) % 64 < 58)
    for n in range(8):
        total = coarse = None
        for parity in range(2):
            p = 8 + 2 * n + parity
            er, eb = defect(vr, vb, cr, cb, p, parity, inner, 32, 8)
            b = br[p + 1, 16:48] + bb[p + 1, 16:48]
            total = er + eb if total is None else total + (er + eb)
            coarse = b if coarse is None else coarse + b
        f1 = pick(halve_rows(tmp, total, 32), by_colour(n, swap))
        b1 = pick(halve_rows(tmp, coarse, 32), spared(by_colour(n, swap)))
        w1 = jnp.where(spare, b1, f1)
        for copy in range(16):
            g_ref[copy, 16 * n : 16 * n + 16] = w1
    for c in copies:
        c.wait()


def joined(g, p, swapped):
    a, i = p // 8, p % 8
    r = slice(16 * i, 16 * i + 16)
    wa = jnp.concatenate([g[4 * a + y, r] for y in range(4)], axis=0)
    wb = jnp.concatenate([g[4 * (a + 2) + y, r] for y in range(4)], axis=0)
    half = lanes(64) < 64
    if swapped:
        return jnp.where(half, wa, wb), turn(jnp.where(half, wb, wa), 64)
    return jnp.where(half, wa, turn(wb, 64)), jnp.where(half, turn(wa, 64), wb)


def seam(v, rows):
    r = slice(8, 8 + rows)
    half = lanes(rows) < 64
    v[0, r] = jnp.where(half, 0.0, turn(v[16, r], 64))
    v[17, r] = jnp.where(half, turn(v[1, r], 64), 0.0)


def mid_down(at, g, gb, w2_ref, cr_out, cb_out, vb_out, br, bb, fr, fb, cr, cb, vr, vb, tmp, sems):
    gy, gz = at[1], at[2]
    lane = lanes(64)
    own = lane % 64 < 32
    keep = own | ((lane % 64 < 48) & (gz < 7)) | ((lane % 64 >= 48) & (gz > 0))
    kept = jnp.where(keep, 1.0, 0.0).astype(F32)
    halo = (lane + jnp.where(lane % 64 < 48, 6, -6)) % 128
    for v in (vr, vb):
        v[...] = jnp.zeros_like(v)
    for b in (br, bb):
        b[:, 0:8] = jnp.zeros((18, 8, 128), F32)
        b[:, 72:80] = jnp.zeros((18, 8, 128), F32)
    for p in range(16):
        fr[p], fb[p] = joined(g, p, True)
        red, black = joined(gb, p, False)
        br[p + 1, 8:72] = kept * jnp.where(own, red, pick(fr[p], halo))
        bb[p + 1, 8:72] = kept * jnp.where(own, black, pick(fb[p], halo))
    seam(br, 64)
    seam(bb, 64)
    index = [side_index(64, parity, 64) for parity in range(2)]

    def coefs(p, parity):
        make_coefs(br, bb, fr[p], cr, p, index[parity], 0.25, 64)
        make_coefs(bb, br, fb[p], cb, p, index[1 - parity], 0.25, 64)
        vr[p + 1, 8:72] = cr[6, p]

    pairs(0, 16, coefs, 64)
    seam(vr, 64)
    window = pl.multiple_of(jnp.clip(gy * 16 - 8, 0, 32), 8)
    copies = [
        pltpu.make_async_copy(cr.at[:, :, pl.ds(window, 32)], cr_out, sems.at[0]),
        pltpu.make_async_copy(cb.at[:, :, pl.ds(window, 32)], cb_out, sems.at[1]),
        pltpu.make_async_copy(vb.at[:, pl.ds(window + 8, 32)], vb_out, sems.at[2]),
    ]
    copies[0].start()
    copies[1].start()
    update(vb, vr, cb, index, 0, 16, 64, 1)
    seam(vb, 64)
    update(vr, vb, cr, index, 0, 16, 64, 0)
    seam(vr, 64)
    update(vb, vr, cb, index, 0, 16, 64, 1)
    seam(vb, 64)
    copies[2].start()
    lane, row = lanes(32), sublanes(32)
    for n in range(8):
        total = coarse = None
        for parity in range(2):
            p = 2 * n + parity
            er, eb = defect(vr, vb, cr, cb, p, parity, index, 64)
            e = er + eb
            b = br[p + 1, 8:72] + bb[p + 1, 8:72]
            total = e if total is None else total + e
            coarse = b if coarse is None else coarse + b
        f2 = halve_rows(tmp, total, 64)
        b2 = halve_rows(tmp, coarse, 64)
        odd = (row + n) % 2
        idx = 64 * ((lane % 64) // 32) + 2 * (lane % 16) + jnp.where(lane % 32 < 16, odd, 1 - odd)
        w2 = jnp.where(lane < 64, pick(f2, idx), pick(b2, idx))
        w2_ref[n] = w2
    for c in copies:
        c.wait()


def transposed(blocks):
    slot = lanes(32) // 16
    for bit in (1, 2, 4):
        out = list(blocks)
        for i in range(8):
            if not i & bit:
                x, y = blocks[i], blocks[i + bit]
                out[i] = jnp.where(slot & bit == 0, x, turn(y, 16 * bit))
                out[i + bit] = jnp.where(slot & bit == 0, turn(x, -16 * bit), y)
        blocks = out
    return blocks


def level_scratch(planes, rows):
    return [pltpu.VMEM((planes + 2, rows + 16, 128), F32)] * 4 + [pltpu.VMEM((8, planes, rows, 128), F32)] * 2


def clear(refs):
    for v in refs:
        v[...] = jnp.zeros_like(v)


def smooth_down(br, bb, vr, vb, cr, cb, f_of, index, scale, planes, rows, inside):
    def coefs(p, parity):
        fr, fb = f_of(p)
        make_coefs(br, bb, fr, cr, p, index[parity], scale, rows, inside and inside[parity])
        make_coefs(bb, br, fb, cb, p, index[1 - parity], scale, rows, inside and inside[1 - parity])
        vr[p + 1, 8 : 8 + rows] = cr[6, p]

    pairs(0, planes, coefs, rows)
    update(vb, vr, cb, index, 0, planes, rows, 1)
    update(vr, vb, cr, index, 0, planes, rows, 0)
    update(vb, vr, cb, index, 0, planes, rows, 1)


def smooth_up(vr, vb, cr, cb, index, planes, rows):
    for _ in range(2):
        update(vr, vb, cr, index, 0, planes, rows, 0)
        update(vb, vr, cb, index, 0, planes, rows, 1)


def restrict(level, tmp, index, planes, rows, cells, put):
    br, bb, vr, vb, cr, cb = level
    lane, row = lanes(rows // 2), sublanes(rows // 2)
    for n in range(planes // 2):
        total = coarse = None
        for parity in range(2):
            p = 2 * n + parity
            er, eb = defect(vr, vb, cr, cb, p, parity, index, rows)
            b = br[p + 1, 8 : 8 + rows] + bb[p + 1, 8 : 8 + rows]
            total = er + eb if total is None else total + (er + eb)
            coarse = b if coarse is None else coarse + b
        f = halve_rows(tmp, total, rows)
        b = halve_rows(tmp, coarse, rows)
        odd = (row + n) % 2
        red = 2 * (lane % 64) + odd
        black = 2 * (lane % 64) + 1 - odd
        inside = lane < cells
        put(n, *[jnp.where(inside, pick(x, i), 0.0) for x in (f, b) for i in (red, black)])


def prolong(vr, vb, out, tmp, planes, rows):
    lane, row = lanes(rows), sublanes(rows)
    r = slice(8, 8 + rows)
    for n in range(planes):
        even = (row + lane + n) % 2 == 0
        c = jnp.where(even, pick(vr[n + 1, r], lane // 2), pick(vb[n + 1, r], lane // 2))
        double_rows(tmp, c, rows)
        for p in (2 * n, 2 * n + 1):
            out[p + 1, 8 : 8 + 2 * rows] += tmp[0 : 2 * rows]


def coarse_up(
    at, m0, m1, m2, m3, q0, q1, q2, q3, c1r_in, c1b_in, v1b_in, c0r_in, c0b_in, v0b_in, u_ref, res_ref,
    b2r, b2b, v2r, v2b, c2r, c2b, f2,
    b3r, b3b, v3r, v3b, c3r, c3b, f3,
    b4r, b4b, v4r, v4b, c4r, c4b, f4,
    v1r, v1b, c1r, c1b, v0r, v0b, c0r, c0b, tmp, sems,
):
    gx, gy, gz = at[0], at[1], at[2]
    copies = [
        pltpu.make_async_copy(c1r_in, c1r, sems.at[0]),
        pltpu.make_async_copy(c1b_in, c1b, sems.at[1]),
        pltpu.make_async_copy(v1b_in, v1b.at[:, pl.ds(8, 32)], sems.at[2]),
        pltpu.make_async_copy(c0r_in, c0r, sems.at[3]),
        pltpu.make_async_copy(c0b_in, c0b, sems.at[4]),
        pltpu.make_async_copy(v0b_in, v0b, sems.at[5]),
    ]
    for c in copies:
        c.start()
    clear((b2r, b2b, v2r, v2b, b3r, b3b, v3r, v3b, b4r, b4b, v4r, v4b, v1r, v0r))
    v1b[:, 0:8] = jnp.zeros((18, 8, 128), F32)
    v1b[:, 40:48] = jnp.zeros((18, 8, 128), F32)

    chip = gz // 2
    first = gz % 2 == 0
    for n in range(8):
        near = [(jnp.where(first, a[n], b[n]), jnp.where(first, b[n], a[n])) for a, b in ((m0, q0), (m1, q1), (m2, q2), (m3, q3))]
        blocks = []
        for c in range(4):
            for core in range(2):
                v = near[0][core]
                for back in range(1, 4):
                    v = jnp.where(chip == (c + back) % 4, near[back][core], v)
                blocks.append(v)
        out = transposed(blocks)
        for h in range(2):
            p = n + 8 * h
            f2[0, p] = out[2 * h]
            f2[1, p] = out[2 * h + 1]
            b2r[p + 1, 8:40] = out[4 + 2 * h]
            b2b[p + 1, 8:40] = out[5 + 2 * h]
    lane = lanes(32)
    index2 = [side_index(32, parity, 128) for parity in range(2)]
    inside2 = [jnp.abs(index2[parity] - lane) < 64 for parity in range(2)]
    smooth_down(b2r, b2b, v2r, v2b, c2r, c2b, lambda p: (f2[0, p], f2[1, p]), index2, 0.25**2, 16, 32, inside2)

    def put3(n, fr, fb, br, bb):
        f3[0, n], f3[1, n] = fr, fb
        b3r[n + 1, 8:24], b3b[n + 1, 8:24] = br, bb

    restrict((b2r, b2b, v2r, v2b, c2r, c2b), tmp, index2, 16, 32, 64, put3)

    index3 = [side_index(16, parity, 128) for parity in range(2)]
    smooth_down(b3r, b3b, v3r, v3b, c3r, c3b, lambda p: (f3[0, p], f3[1, p]), index3, 0.25**3, 8, 16, None)

    def put4(n, fr, fb, br, bb):
        f4[0, n], f4[1, n] = fr, fb
        b4r[n + 1, 8:16], b4b[n + 1, 8:16] = br, bb

    restrict((b3r, b3b, v3r, v3b, c3r, c3b), tmp, index3, 8, 16, 32, put4)

    index4 = [side_index(8, parity, 128) for parity in range(2)]

    for p in range(4):
        make_coefs(b4r, b4b, f4[0, p], c4r, p, index4[p % 2], 0.25**4, 8)
        make_coefs(b4b, b4r, f4[1, p], c4b, p, index4[1 - p % 2], 0.25**4, 8)
    row8 = sublanes(8)
    inner = (row8 > 0, row8 < 7)
    cr4 = [[c4r[w, p] for w in range(7)] for p in range(4)]
    cb4 = [[c4b[w, p] for w in range(7)] for p in range(4)]
    for c in cr4 + cb4:
        c[2] = jnp.where(inner[0], c[2], 0.0)
        c[3] = jnp.where(inner[1], c[3], 0.0)

    def half(other, coefs, flip):
        out = []
        for p in range(4):
            c, v = coefs[p], other[p]
            w = c[6] + c[4] * v
            if p > 0:
                w = w + c[0] * other[p - 1]
            if p < 3:
                w = w + c[1] * other[p + 1]
            w = w + c[2] * pltpu.roll(v, 1, 0) + c[3] * pltpu.roll(v, 7, 0)
            out.append(w + c[5] * pick(v, index4[(p + flip) % 2]))
        return out

    def coarse_step(count, state):
        black = list(state)
        red = half(black, cr4, 0)
        return tuple(half(red, cb4, 1))

    black = lax.fori_loop(0, COARSE_ITERS - 1, coarse_step, (jnp.zeros((8, 128), F32),) * 4)
    red = half(black, cr4, 0)
    black = half(red, cb4, 1)
    for p in range(4):
        v4r[p + 1, 8:16] = red[p]
        v4b[p + 1, 8:16] = black[p]

    prolong(v4r, v4b, v3b, tmp, 4, 8)
    smooth_up(v3r, v3b, c3r, c3b, index3, 8, 16)
    prolong(v3r, v3b, v2b, tmp, 8, 16)
    smooth_up(v2r, v2b, c2r, c2b, index2, 16, 32)

    for c in copies[:3]:
        c.wait()
    lane, row = lanes(32), sublanes(32)
    near = lane % 64 - jnp.where(lane % 64 < 48, 0, 64)
    cell = gz * 32 + near
    valid = (cell >= 0) & (cell < 256)
    idx = jnp.clip(cell, 0, 255) // 2
    window = pl.multiple_of(jnp.clip(gy * 16 - 8, 0, 32), 8)
    for n in range(8):
        even = (row + lane + n) % 2 == 0
        parts = []
        for p in (n, n + 8):
            parts.append(jnp.where(even, pick(v2r[p + 1, 8:40], idx), pick(v2b[p + 1, 8:40], idx)))
        c = jnp.where(valid, jnp.where(lane < 64, parts[0], parts[1]), 0.0)
        double_rows(tmp, c, 32)
        for p in (2 * n, 2 * n + 1):
            v1b[p + 1, 8:40] += tmp[pl.ds(window, 32)]
    seam(v1b, 32)
    index1 = [side_index(32, parity, 64) for parity in range(2)]
    for _ in range(2):
        update(v1r, v1b, c1r, index1, 0, 16, 32, 0)
        seam(v1r, 32)
        update(v1b, v1r, c1b, index1, 0, 16, 32, 1)
        seam(v1b, 32)

    for c in copies[3:]:
        c.wait()
    start = pl.multiple_of(gy * 16 - window, 8)
    cell = lane - jnp.where(lane < 96, 0, 128)
    idx = (cell // 2) % 64
    for n in range(-3, 11):
        plane = gx * 8 + n
        held = jnp.clip(plane, 0, 31)
        at_half = idx + 64 * (held // 16)
        even = (row + lane + n) % 2 == 0
        red = v1r[held % 16 + 1, pl.ds(start, 32)]
        black = v1b[held % 16 + 1, pl.ds(start, 32)]
        c = jnp.where(even, pick(red, at_half), pick(black, at_half))
        c = c * jnp.where((plane >= 0) & (plane < 32), 1.0, 0.0).astype(F32)
        tmp[64:96] = c
        double_rows(tmp, tmp[68:92], 24)
        for p in (2 * n + 8, 2 * n + 9):
            v0b[p + 1, 8:56] += tmp[0:48]
    index0 = [side_index(48, parity, 128) for parity in range(2)]
    update(v0r, v0b, c0r, index0, 4, 28, 48, 0, 4)
    update(v0b, v0r, c0b, index0, 4, 28, 48, 1, 4)
    update(v0r, v0b, c0r, index0, 6, 26, 48, 0, 4)
    update(v0b, v0r, c0b, index0, 6, 26, 48, 1, 4)

    def finish(p, parity):
        even = (row + lane + parity) % 2 == 0
        er, eb = defect(v0r, v0b, c0r, c0b, p, parity, index1_0, 32, 8, 4)
        res_ref[p - 8] = jnp.where(even, pick(er, lane // 2), pick(eb, lane // 2))
        red, black = v0r[p + 1, 16:48], v0b[p + 1, 16:48]
        u_ref[p - 8] = jnp.where(even, pick(red, lane // 2), pick(black, lane // 2))

    index1_0 = [side_index(32, parity, 128) for parity in range(2)]
    pairs(8, 24, finish, 32)


def around(lo, hi, axis):
    count = lax.axis_size(axis)
    from_above = lax.ppermute(lo, axis, [((i + 1) % count, i) for i in range(count)])
    from_below = lax.ppermute(hi, axis, [(i, (i + 1) % count) for i in range(count)])
    return from_below, from_above


def body(source, conductance):
    vmem, smem, hbm = (pl.BlockSpec(memory_space=m) for m in (pltpu.VMEM, pltpu.SMEM, pltpu.HBM))
    at = jnp.stack([lax.axis_index(a) for a in ("gx", "gy", "gz")]).astype(jnp.int32)
    dma = pltpu.SemaphoreType.DMA

    block, x_slab = arr(16, 32, 128), arr(17, 32, 128)
    buffer = pltpu.VMEM((16, 32, 128), F32)
    wf, wb, lo, hi, b1 = call(
        split_fine,
        [(block, block, x_slab, x_slab, arr(128, 128))],
        (source, conductance),
        [hbm] * 2,
        [buffer, buffer, pltpu.VMEM((32, 128), F32), dma((2,))],
        8,
    )
    gb = lax.all_gather(b1, ("gx", "gy"))
    xl, xu = around(lo, hi, "gx")
    lo, hi = call(pack_rows, [(arr(66, 8, 128),) * 2], (wf, wb, xl, xu), limit=8)
    yl, yu = around(lo, hi, "gy")
    lo, hi = call(pack_lanes, [(arr(96, 8, 128),) * 2], (wf, wb, xl, xu, yl, yu), limit=8)
    zl, zu = around(lo, hi, "gz")

    colour0 = pltpu.VMEM((34, 64, 128), F32)
    right0 = pltpu.VMEM((32, 48, 128), F32)
    coef0 = pltpu.VMEM((8, 32, 48, 128), F32)
    state0 = (arr(8, 24, 48, 128), arr(8, 24, 48, 128), arr(34, 64, 128))
    g, c0r, c0b, v0b = call(
        fine_down,
        [(arr(16, 128, 128),) + state0, (vmem, hbm, hbm, hbm)],
        (at, wf, wb, xl, xu, yl, yu, zl, zu),
        [smem] + [vmem] * 8,
        [colour0, colour0, right0, right0, coef0, coef0, colour0, colour0, pltpu.VMEM((32, 128), F32), dma((3,))],
        LIMIT,
    )
    g = lax.all_to_all(g, ("gx", "gy"), 0, 0, tiled=True)

    state1 = (arr(8, 16, 32, 128), arr(8, 16, 32, 128), arr(18, 32, 128))
    colour1 = pltpu.VMEM((18, 80, 128), F32)
    right1 = pltpu.VMEM((16, 64, 128), F32)
    coef1 = pltpu.VMEM((8, 16, 64, 128), F32)
    w2, c1r, c1b, v1b = call(
        mid_down,
        [(arr(8, 32, 128),) + state1, (vmem, hbm, hbm, hbm)],
        (at, g, gb),
        [smem] + [vmem] * 2,
        [colour1, colour1, right1, right1, coef1, coef1, colour1, colour1, pltpu.VMEM((64, 128), F32), dma((3,))],
        LIMIT,
    )
    mine = [w2] + [lax.ppermute(w2, "gz", [(i, (i + d) % 8) for i in range(8)]) for d in (2, 4, 6)]
    pair = [lax.ppermute(w, "gz", [(i, i ^ 1) for i in range(8)]) for w in mine]

    scratch = []
    for planes, rows in ((16, 32), (8, 16), (4, 8)):
        scratch += level_scratch(planes, rows) + [pltpu.VMEM((2, planes, rows, 128), F32)]
    scratch += [pltpu.VMEM((18, 48, 128), F32)] * 2 + [pltpu.VMEM((8, 16, 32, 128), F32)] * 2
    scratch += [colour0] * 2 + [pltpu.VMEM((8, 24, 48, 128), F32)] * 2
    scratch += [pltpu.VMEM((96, 128), F32), dma((6,))]
    return call(
        coarse_up,
        [(block, block)],
        (at, *mine, *pair, c1r, c1b, v1b, c0r, c0b, v0b),
        [smem] + [vmem] * 8 + [hbm] * 6,
        scratch,
        LIMIT,
    )


def solution(mesh):
    placed = (P("gx", "gy", "gz"), P("gx", "gy", "gz"))
    return jax.shard_map(body, mesh=mesh, in_specs=placed, out_specs=placed, check_vma=False)
```

```python
import functools

import jax
import jax.numpy as jnp
from jax import lax
from jax.experimental import pallas as pl
from jax.experimental.pallas import tpu as pltpu
from jax.sharding import PartitionSpec as P

F32 = jnp.float32
COARSE_ITERS = 20
MIB = 1 << 20
GROUP = 64
LIMIT = 50


def lanes(rows):
    return lax.broadcasted_iota(jnp.int32, (rows, 128), 1)


def sublanes(rows):
    return lax.broadcasted_iota(jnp.int32, (rows, 128), 0)


def pick(x, idx):
    return jnp.take_along_axis(x, idx, axis=1, mode="promise_in_bounds")


def turn(x, shift):
    shift = shift % 128
    return pltpu.roll(x, shift, 1) if shift else x


def side_index(rows, parity, period):
    lane, row = lanes(rows), sublanes(rows)
    step = 2 * ((row + parity) % 2) - 1
    within = (lane % period + step + period) % period
    return lane - lane % period + within


def call(kernel, out, args, specs=None, scratch=(), limit=40):
    vmem = pl.BlockSpec(memory_space=pltpu.VMEM)
    return pl.pallas_call(
        kernel,
        out_shape=out[0],
        in_specs=specs or [vmem] * len(args),
        out_specs=out[1] if len(out) > 1 else jax.tree.map(lambda _: vmem, out[0]),
        scratch_shapes=scratch,
        compiler_params=pltpu.CompilerParams(vmem_limit_bytes=limit * MIB),
        name=kernel.__name__,
    )(*args)


def arr(*shape):
    return jax.ShapeDtypeStruct(shape, F32)


def split_fine(f_in, b_in, wf_ref, wb_ref, lo_ref, hi_ref, f_ref, b_ref, sems):
    loads = [pltpu.make_async_copy(b_in, b_ref, sems.at[0]), pltpu.make_async_copy(f_in, f_ref, sems.at[1])]
    for c in loads:
        c.start()
    lane, row = lanes(32), sublanes(32)
    index = []
    for parity in range(2):
        odd = (row + parity) % 2
        index.append(2 * (lane % 64) + jnp.where(lane < 64, odd, 1 - odd))
    loads[0].wait()
    for i in range(16):
        wb = pick(b_ref[i], index[i % 2])
        wb_ref[i] = wb
        if i < 9:
            lo_ref[8 + i] = wb
        if i > 6:
            hi_ref[1 + i] = wb
    loads[1].wait()
    for i in range(16):
        wf = pick(f_ref[i], index[i % 2])
        wf_ref[i] = wf
        if i < 8:
            lo_ref[i] = wf
        else:
            hi_ref[i - 8] = wf


def by_colour(n, swap):
    lane, row = lanes(16), sublanes(16)
    odd = (row + n) % 2
    return (2 * (lane % 64) + jnp.where((lane < 64) != swap, odd, 1 - odd)) % 128


def spared(index):
    return (index + jnp.where(lanes(16) % 64 < 48, -12, 12)) % 128


def plane_f(wf, xl, xu, p):
    return xl.at[p] if p < 8 else wf.at[p - 8] if p < 24 else xu.at[p - 24]


def plane_b(wb, xl, xu, p):
    return xl.at[9 + p] if p < 8 else wb.at[p - 8] if p < 24 else xu.at[8 + p - 24]


def pack_rows(wf, wb, xl, xu, lo_ref, hi_ref):
    for p in range(32):
        f, b = plane_f(wf, xl, xu, p), plane_b(wb, xl, xu, p)
        lo_ref[p] = f[0:8]
        hi_ref[p] = f[24:32]
        lo_ref[32 + p] = b[0:8]
        hi_ref[32 + p] = b[24:32]
    for i in range(16):
        lo_ref[64 + i // 8, i % 8 : i % 8 + 1] = wb[i, 8:9]
        hi_ref[64 + i // 8, i % 8 : i % 8 + 1] = wb[i, 23:24]


def slab(plane, yl, yu, which, p):
    return jnp.concatenate([yl[32 * which + p], plane[...], yu[32 * which + p]], axis=0)


def pack_lanes(wf, wb, xl, xu, yl, yu, lo_ref, hi_ref):
    slot_of = lanes(48) % 64
    for which, width, base in ((0, 16, 0), (1, 16, 48)):
        count = 64 // width
        slot = slot_of // width
        for group in range(32 // count):
            for s in range(count):
                p = group * count + s
                plane = plane_b(wb, xl, xu, p) if which else plane_f(wf, xl, xu, p)
                v = turn(slab(plane, yl, yu, which, p), width * s)
                if s == 0:
                    low = high = v
                else:
                    low = jnp.where(slot == s, v, low)
                    high = jnp.where(slot == s - 1, v, high)
            start = base + 6 * group
            lo_ref[start : start + 6] = low.reshape(6, 8, 128)
            hi_ref[start : start + 6] = high.reshape(6, 8, 128)


def make_coefs(mine, other, f, coef, p, index, scale, rows, inside=None):
    r = slice(8, 8 + rows)
    centre = mine[p + 1, r]
    mid = other[p + 1, r]
    side = pick(mid, index)
    if inside is not None:
        side = jnp.where(inside, side, 0.0)
    beside = (other[p, r], other[p + 2, r], other[p + 1, 7 : 7 + rows], other[p + 1, 9 : 9 + rows], mid, side)
    weights = [centre + b for b in beside]
    total = weights[0]
    for w in weights[1:]:
        total = total + w
    inverse = jnp.where(centre > 0.0, 1.0 / jnp.where(centre > 0.0, total, 1.0), 0.0)
    for which in range(6):
        w = weights[which] * inverse
        if which == 5 and inside is not None:
            w = jnp.where(inside, w, 0.0)
        coef[which, p] = w
    coef[6, p] = f * (inverse * (2.0 / scale))
    coef[7, p] = total * (0.5 * scale)


def relaxed(other, coef, p, index, rows, first=0, shift=0):
    a = 8 + first
    r = slice(a, a + rows)
    c = slice(first, first + rows)
    q = p - shift
    mid = other[p + 1, r]
    out = coef[6, q, c] + coef[0, q, c] * other[p, r]
    out = out + coef[1, q, c] * other[p + 2, r]
    out = out + coef[2, q, c] * other[p + 1, a - 1 : a - 1 + rows]
    out = out + coef[3, q, c] * other[p + 1, a + 1 : a + 1 + rows]
    out = out + coef[4, q, c] * mid
    return out + coef[5, q, c] * pick(mid, index)


def pairs(start, stop, body, rows):
    count = stop - start
    width = max(w for w in (2, 4, 8, 16) if w == 2 or (count % w == 0 and w * rows <= 8 * GROUP))

    def step(t, carry):
        for n in range(width):
            body(start + t * width + n, n % 2)
        return carry

    if count == width:
        step(0, 0)
    else:
        lax.fori_loop(0, count // width, step, 0)


def update(mine, other, coef, index, start, stop, rows, flip, shift=0):
    def body(p, parity):
        mine[p + 1, 8 : 8 + rows] = relaxed(other, coef, p, index[(parity + flip) % 2], rows, 0, shift)

    pairs(start, stop, body, rows)


def defect(red, black, cr, cb, p, parity, index, rows, first=0, shift=0):
    r = slice(8 + first, 8 + first + rows)
    c = slice(first, first + rows)
    er = cr[7, p - shift, c] * (relaxed(black, cr, p, index[parity], rows, first, shift) - red[p + 1, r])
    eb = cb[7, p - shift, c] * (relaxed(red, cb, p, index[1 - parity], rows, first, shift) - black[p + 1, r])
    return er, eb


def halve_rows(tmp, value, rows):
    tmp[0:rows] = value
    return 0.125 * (tmp[pl.ds(0, rows // 2, 2)] + tmp[pl.ds(1, rows // 2, 2)])


def double_rows(tmp, value, rows):
    tmp[pl.ds(0, rows, 2)] = value
    tmp[pl.ds(1, rows, 2)] = value


def fine_down(
    at, wf, wb, xl, xu, yl, yu, zl, zu, g_ref, cr_out, cb_out, vb_out, br, bb, fr, fb, cr, cb, vr, vb, tmp, sems
):
    gx, gy, gz = at[0], at[1], at[2]
    lane, row = lanes(48), sublanes(48)
    own = lane < 64
    keep = own | ((lane < 96) & (gz < 7)) | ((lane >= 96) & (gz > 0))
    keep = keep & ((row >= 8) | (gy > 0)) & ((row < 40) | (gy < 3))
    kept = jnp.where(keep, 1.0, 0.0).astype(F32)
    below = jnp.where(gx > 0, 1.0, 0.0).astype(F32)
    above = jnp.where(gx < 3, 1.0, 0.0).astype(F32)
    left = jnp.where(gy > 0, 1.0, 0.0).astype(F32)
    right = jnp.where(gy < 3, 1.0, 0.0).astype(F32)
    vr[...] = jnp.zeros_like(vr)
    vb[...] = jnp.zeros_like(vb)
    edge = jnp.zeros((8, 128), F32)
    for b in (br, bb):
        for q in range(34):
            b[q, 0:8] = edge
            b[q, 56:64] = edge
        for q in (0, 33):
            b[q, 8:56] = jnp.zeros((48, 128), F32)
    for which, width, base in ((0, 16, 0), (1, 16, 48)):
        count = 64 // width
        slot = (lane % 64) // width
        for p in range(32):
            plane = plane_b(wb, xl, xu, p) if which else plane_f(wf, xl, xu, p)
            w = slab(plane, yl, yu, which, p)
            s = p % count
            start = base + 6 * (p // count)
            up = zu[start : start + 6].reshape(48, 128)
            low = zl[start : start + 6].reshape(48, 128)
            both = jnp.where(slot == s, up, low)
            red = jnp.where(own, w, turn(both, 64 - width * s))
            black = jnp.where(own, turn(w, 64), turn(both, -width * s))
            if which:
                k = kept * below if p < 8 else kept * above if p >= 24 else kept
                br[p + 1, 8:56] = red * k
                bb[p + 1, 8:56] = black * k
            else:
                fr[p] = red
                fb[p] = black
    for a in range(2):
        for src, r, ok in ((yl, 7, left), (yu, 56, right)):
            v = src[64 + a] * ok
            t = turn(v, 64)
            for s in range(8):
                br[9 + 8 * a + s, r : r + 1] = v[s : s + 1]
                bb[9 + 8 * a + s, r : r + 1] = t[s : s + 1]
    for v, q in ((xl[8] * below, 0), (xu[16] * above, 33)):
        br[q, 16:48] = v
        bb[q, 16:48] = turn(v, 64)

    index = [side_index(48, parity, 128) for parity in range(2)]

    def coefs(p, parity):
        make_coefs(br, bb, fr[p], cr, p, index[parity], 1.0, 48)
        make_coefs(bb, br, fb[p], cb, p, index[1 - parity], 1.0, 48)
        vr[p + 1, 8:56] = cr[6, p]

    pairs(0, 32, coefs, 48)
    copies = [
        pltpu.make_async_copy(cr.at[:, pl.ds(4, 24)], cr_out, sems.at[0]),
        pltpu.make_async_copy(cb.at[:, pl.ds(4, 24)], cb_out, sems.at[1]),
        pltpu.make_async_copy(vb, vb_out, sems.at[2]),
    ]
    copies[0].start()
    copies[1].start()
    update(vb, vr, cb, index, 0, 32, 48, 1)
    update(vr, vb, cr, index, 2, 30, 48, 0)
    update(vb, vr, cb, index, 2, 30, 48, 1)
    copies[2].start()
    inner = [side_index(32, parity, 128) for parity in range(2)]
    swap = gx >= 2
    lane16, row16 = lanes(16), sublanes(16)
    spare = (lane16 % 64 >= 38) & (lane16 % 64 < 58)
    odd16 = [(row16 + parity) % 2 for parity in range(2)]
    own1 = {}
    for n in range(8):
        total = coarse = None
        for parity in range(2):
            p = 8 + 2 * n + parity
            er, eb = defect(vr, vb, cr, cb, p, parity, inner, 32, 8)
            b = br[p + 1, 16:48] + bb[p + 1, 16:48]
            total = er + eb if total is None else total + (er + eb)
            coarse = b if coarse is None else coarse + b
        f1 = pick(halve_rows(tmp, total, 32), by_colour(n, swap))
        b1 = halve_rows(tmp, coarse, 32)
        w1 = jnp.where(spare, pick(b1, spared(by_colour(n, swap))), f1)
        own1[n] = pick(b1, 2 * (lane16 % 32) + jnp.where(lane16 % 64 < 32, odd16[n % 2], 1 - odd16[n % 2]))
        for copy in range(16):
            g_ref[copy, 16 * n : 16 * n + 16] = w1
    for n in range(4):
        w1 = jnp.where(lane16 < 64, own1[n], own1[n + 4])
        for copy in range(16):
            g_ref[copy, 128 + 16 * n : 144 + 16 * n] = w1
    for c in copies:
        c.wait()


def across(g, a, start):
    r = slice(start, start + 16)
    return jnp.concatenate([g[4 * a + y, r] for y in range(4)], axis=0)


def joined_f(g, p):
    wa, wb = (across(g, p // 8 + up, 16 * (p % 8)) for up in (0, 2))
    half = lanes(64) < 64
    return jnp.where(half, wa, wb), turn(jnp.where(half, wb, wa), 64)


def joined_b(g, p):
    i = p % 8
    wa, wb = (across(g, p // 8 + up, 128 + 16 * (i % 4)) for up in (0, 2))
    half = lanes(64) < 64
    red = jnp.where(half, wa, turn(wb, 64)) if i < 4 else jnp.where(half, turn(wa, 64), wb)
    return red, turn(red, -32)


def seam(v, rows):
    r = slice(8, 8 + rows)
    half = lanes(rows) < 64
    v[0, r] = jnp.where(half, 0.0, turn(v[16, r], 64))
    v[17, r] = jnp.where(half, turn(v[1, r], 64), 0.0)


def mid_down(at, g, w2_ref, cr_out, cb_out, vb_out, br, bb, fr, fb, cr, cb, vr, vb, tmp, sems):
    gy, gz = at[1], at[2]
    lane = lanes(64)
    own = lane % 64 < 32
    keep = own | ((lane % 64 < 48) & (gz < 7)) | ((lane % 64 >= 48) & (gz > 0))
    kept = jnp.where(keep, 1.0, 0.0).astype(F32)
    halo = (lane + jnp.where(lane % 64 < 48, 6, -6)) % 128
    for v in (vr, vb):
        v[...] = jnp.zeros_like(v)
    for b in (br, bb):
        b[:, 0:8] = jnp.zeros((18, 8, 128), F32)
        b[:, 72:80] = jnp.zeros((18, 8, 128), F32)
    for p in range(16):
        fr[p], fb[p] = joined_f(g, p)
        red, black = joined_b(g, p)
        br[p + 1, 8:72] = kept * jnp.where(own, red, pick(fr[p], halo))
        bb[p + 1, 8:72] = kept * jnp.where(own, black, pick(fb[p], halo))
    seam(br, 64)
    seam(bb, 64)
    index = [side_index(64, parity, 64) for parity in range(2)]

    def coefs(p, parity):
        make_coefs(br, bb, fr[p], cr, p, index[parity], 0.25, 64)
        make_coefs(bb, br, fb[p], cb, p, index[1 - parity], 0.25, 64)
        vr[p + 1, 8:72] = cr[6, p]

    pairs(0, 16, coefs, 64)
    seam(vr, 64)
    window = pl.multiple_of(jnp.clip(gy * 16 - 8, 0, 32), 8)
    copies = [
        pltpu.make_async_copy(cr.at[:, :, pl.ds(window, 32)], cr_out, sems.at[0]),
        pltpu.make_async_copy(cb.at[:, :, pl.ds(window, 32)], cb_out, sems.at[1]),
        pltpu.make_async_copy(vb.at[:, pl.ds(window + 8, 32)], vb_out, sems.at[2]),
    ]
    copies[0].start()
    copies[1].start()
    update(vb, vr, cb, index, 0, 16, 64, 1)
    seam(vb, 64)
    update(vr, vb, cr, index, 0, 16, 64, 0)
    seam(vr, 64)
    update(vb, vr, cb, index, 0, 16, 64, 1)
    seam(vb, 64)
    copies[2].start()
    lane, row = lanes(32), sublanes(32)
    for n in range(8):
        total = coarse = None
        for parity in range(2):
            p = 2 * n + parity
            er, eb = defect(vr, vb, cr, cb, p, parity, index, 64)
            e = er + eb
            b = br[p + 1, 8:72] + bb[p + 1, 8:72]
            total = e if total is None else total + e
            coarse = b if coarse is None else coarse + b
        f2 = halve_rows(tmp, total, 64)
        b2 = halve_rows(tmp, coarse, 64)
        odd = (row + n) % 2
        idx = 64 * ((lane % 64) // 32) + 2 * (lane % 16) + jnp.where(lane % 32 < 16, odd, 1 - odd)
        w2 = jnp.where(lane < 64, pick(f2, idx), pick(b2, idx))
        w2_ref[n] = w2
    for c in copies:
        c.wait()


def transposed(blocks):
    slot = lanes(32) // 16
    for bit in (1, 2, 4):
        out = list(blocks)
        for i in range(8):
            if not i & bit:
                x, y = blocks[i], blocks[i + bit]
                out[i] = jnp.where(slot & bit == 0, x, turn(y, 16 * bit))
                out[i + bit] = jnp.where(slot & bit == 0, turn(x, -16 * bit), y)
        blocks = out
    return blocks


def level_scratch(planes, rows):
    return [pltpu.VMEM((planes + 2, rows + 16, 128), F32)] * 4 + [pltpu.VMEM((8, planes, rows, 128), F32)] * 2


def clear(refs):
    for v in refs:
        v[...] = jnp.zeros_like(v)


def smooth_down(br, bb, vr, vb, cr, cb, f_of, index, scale, planes, rows, inside):
    def coefs(p, parity):
        fr, fb = f_of(p)
        make_coefs(br, bb, fr, cr, p, index[parity], scale, rows, inside and inside[parity])
        make_coefs(bb, br, fb, cb, p, index[1 - parity], scale, rows, inside and inside[1 - parity])
        vr[p + 1, 8 : 8 + rows] = cr[6, p]

    pairs(0, planes, coefs, rows)
    update(vb, vr, cb, index, 0, planes, rows, 1)
    update(vr, vb, cr, index, 0, planes, rows, 0)
    update(vb, vr, cb, index, 0, planes, rows, 1)


def smooth_up(vr, vb, cr, cb, index, planes, rows):
    for _ in range(2):
        update(vr, vb, cr, index, 0, planes, rows, 0)
        update(vb, vr, cb, index, 0, planes, rows, 1)


def restrict(level, tmp, index, planes, rows, cells, put):
    br, bb, vr, vb, cr, cb = level
    lane, row = lanes(rows // 2), sublanes(rows // 2)
    for n in range(planes // 2):
        total = coarse = None
        for parity in range(2):
            p = 2 * n + parity
            er, eb = defect(vr, vb, cr, cb, p, parity, index, rows)
            b = br[p + 1, 8 : 8 + rows] + bb[p + 1, 8 : 8 + rows]
            total = er + eb if total is None else total + (er + eb)
            coarse = b if coarse is None else coarse + b
        f = halve_rows(tmp, total, rows)
        b = halve_rows(tmp, coarse, rows)
        odd = (row + n) % 2
        red = 2 * (lane % 64) + odd
        black = 2 * (lane % 64) + 1 - odd
        inside = lane < cells
        put(n, *[jnp.where(inside, pick(x, i), 0.0) for x in (f, b) for i in (red, black)])


def prolong(vr, vb, out, tmp, planes, rows):
    lane, row = lanes(rows), sublanes(rows)
    r = slice(8, 8 + rows)
    for n in range(planes):
        even = (row + lane + n) % 2 == 0
        c = jnp.where(even, pick(vr[n + 1, r], lane // 2), pick(vb[n + 1, r], lane // 2))
        double_rows(tmp, c, rows)
        for p in (2 * n, 2 * n + 1):
            out[p + 1, 8 : 8 + 2 * rows] += tmp[0 : 2 * rows]


def coarse_up(
    at, m0, m1, m2, m3, q0, q1, q2, q3, c1r_in, c1b_in, v1b_in, c0r_in, c0b_in, v0b_in, u_ref, res_ref,
    b2r, b2b, v2r, v2b, c2r, c2b, f2,
    b3r, b3b, v3r, v3b, c3r, c3b, f3,
    b4r, b4b, v4r, v4b, c4r, c4b, f4,
    v1r, v1b, c1r, c1b, v0r, v0b, c0r, c0b, tmp, sems,
):
    gx, gy, gz = at[0], at[1], at[2]
    copies = [
        pltpu.make_async_copy(c1r_in, c1r, sems.at[0]),
        pltpu.make_async_copy(c1b_in, c1b, sems.at[1]),
        pltpu.make_async_copy(v1b_in, v1b.at[:, pl.ds(8, 32)], sems.at[2]),
        pltpu.make_async_copy(c0r_in, c0r, sems.at[3]),
        pltpu.make_async_copy(c0b_in, c0b, sems.at[4]),
        pltpu.make_async_copy(v0b_in, v0b, sems.at[5]),
    ]
    for c in copies:
        c.start()
    clear((b2r, b2b, v2r, v2b, b3r, b3b, v3r, v3b, b4r, b4b, v4r, v4b, v1r, v0r))
    v1b[:, 0:8] = jnp.zeros((18, 8, 128), F32)
    v1b[:, 40:48] = jnp.zeros((18, 8, 128), F32)

    chip = gz // 2
    first = gz % 2 == 0
    for n in range(8):
        near = [(jnp.where(first, a[n], b[n]), jnp.where(first, b[n], a[n])) for a, b in ((m0, q0), (m1, q1), (m2, q2), (m3, q3))]
        blocks = []
        for c in range(4):
            for core in range(2):
                v = near[0][core]
                for back in range(1, 4):
                    v = jnp.where(chip == (c + back) % 4, near[back][core], v)
                blocks.append(v)
        out = transposed(blocks)
        for h in range(2):
            p = n + 8 * h
            f2[0, p] = out[2 * h]
            f2[1, p] = out[2 * h + 1]
            b2r[p + 1, 8:40] = out[4 + 2 * h]
            b2b[p + 1, 8:40] = out[5 + 2 * h]
    lane = lanes(32)
    index2 = [side_index(32, parity, 128) for parity in range(2)]
    inside2 = [jnp.abs(index2[parity] - lane) < 64 for parity in range(2)]
    smooth_down(b2r, b2b, v2r, v2b, c2r, c2b, lambda p: (f2[0, p], f2[1, p]), index2, 0.25**2, 16, 32, inside2)

    def put3(n, fr, fb, br, bb):
        f3[0, n], f3[1, n] = fr, fb
        b3r[n + 1, 8:24], b3b[n + 1, 8:24] = br, bb

    restrict((b2r, b2b, v2r, v2b, c2r, c2b), tmp, index2, 16, 32, 64, put3)

    index3 = [side_index(16, parity, 128) for parity in range(2)]
    smooth_down(b3r, b3b, v3r, v3b, c3r, c3b, lambda p: (f3[0, p], f3[1, p]), index3, 0.25**3, 8, 16, None)

    def put4(n, fr, fb, br, bb):
        f4[0, n], f4[1, n] = fr, fb
        b4r[n + 1, 8:16], b4b[n + 1, 8:16] = br, bb

    restrict((b3r, b3b, v3r, v3b, c3r, c3b), tmp, index3, 8, 16, 32, put4)

    index4 = [side_index(8, parity, 128) for parity in range(2)]

    for p in range(4):
        make_coefs(b4r, b4b, f4[0, p], c4r, p, index4[p % 2], 0.25**4, 8)
        make_coefs(b4b, b4r, f4[1, p], c4b, p, index4[1 - p % 2], 0.25**4, 8)
    row8 = sublanes(8)
    inner = (row8 > 0, row8 < 7)
    cr4 = [[c4r[w, p] for w in range(7)] for p in range(4)]
    cb4 = [[c4b[w, p] for w in range(7)] for p in range(4)]
    for c in cr4 + cb4:
        c[2] = jnp.where(inner[0], c[2], 0.0)
        c[3] = jnp.where(inner[1], c[3], 0.0)

    def half(other, coefs, flip):
        out = []
        for p in range(4):
            c, v = coefs[p], other[p]
            w = c[6] + c[4] * v
            if p > 0:
                w = w + c[0] * other[p - 1]
            if p < 3:
                w = w + c[1] * other[p + 1]
            w = w + c[2] * pltpu.roll(v, 1, 0) + c[3] * pltpu.roll(v, 7, 0)
            out.append(w + c[5] * pick(v, index4[(p + flip) % 2]))
        return out

    def coarse_step(count, state):
        black = list(state)
        red = half(black, cr4, 0)
        return tuple(half(red, cb4, 1))

    black = lax.fori_loop(0, COARSE_ITERS - 1, coarse_step, (jnp.zeros((8, 128), F32),) * 4)
    red = half(black, cr4, 0)
    black = half(red, cb4, 1)
    for p in range(4):
        v4r[p + 1, 8:16] = red[p]
        v4b[p + 1, 8:16] = black[p]

    prolong(v4r, v4b, v3b, tmp, 4, 8)
    smooth_up(v3r, v3b, c3r, c3b, index3, 8, 16)
    prolong(v3r, v3b, v2b, tmp, 8, 16)
    smooth_up(v2r, v2b, c2r, c2b, index2, 16, 32)

    for c in copies[:3]:
        c.wait()
    lane, row = lanes(32), sublanes(32)
    near = lane % 64 - jnp.where(lane % 64 < 48, 0, 64)
    cell = gz * 32 + near
    valid = (cell >= 0) & (cell < 256)
    idx = jnp.clip(cell, 0, 255) // 2
    window = pl.multiple_of(jnp.clip(gy * 16 - 8, 0, 32), 8)
    for n in range(8):
        even = (row + lane + n) % 2 == 0
        parts = []
        for p in (n, n + 8):
            parts.append(jnp.where(even, pick(v2r[p + 1, 8:40], idx), pick(v2b[p + 1, 8:40], idx)))
        c = jnp.where(valid, jnp.where(lane < 64, parts[0], parts[1]), 0.0)
        double_rows(tmp, c, 32)
        for p in (2 * n, 2 * n + 1):
            v1b[p + 1, 8:40] += tmp[pl.ds(window, 32)]
    seam(v1b, 32)
    index1 = [side_index(32, parity, 64) for parity in range(2)]
    for _ in range(2):
        update(v1r, v1b, c1r, index1, 0, 16, 32, 0)
        seam(v1r, 32)
        update(v1b, v1r, c1b, index1, 0, 16, 32, 1)
        seam(v1b, 32)

    for c in copies[3:]:
        c.wait()
    start = pl.multiple_of(gy * 16 - window, 8)
    cell = lane - jnp.where(lane < 96, 0, 128)
    idx = (cell // 2) % 64
    for n in range(-3, 11):
        plane = gx * 8 + n
        held = jnp.clip(plane, 0, 31)
        at_half = idx + 64 * (held // 16)
        even = (row + lane + n) % 2 == 0
        red = v1r[held % 16 + 1, pl.ds(start, 32)]
        black = v1b[held % 16 + 1, pl.ds(start, 32)]
        c = jnp.where(even, pick(red, at_half), pick(black, at_half))
        c = c * jnp.where((plane >= 0) & (plane < 32), 1.0, 0.0).astype(F32)
        tmp[64:96] = c
        double_rows(tmp, tmp[68:92], 24)
        for p in (2 * n + 8, 2 * n + 9):
            v0b[p + 1, 8:56] += tmp[0:48]
    index0 = [side_index(48, parity, 128) for parity in range(2)]
    update(v0r, v0b, c0r, index0, 4, 28, 48, 0, 4)
    update(v0b, v0r, c0b, index0, 4, 28, 48, 1, 4)
    update(v0r, v0b, c0r, index0, 6, 26, 48, 0, 4)
    update(v0b, v0r, c0b, index0, 6, 26, 48, 1, 4)

    def finish(p, parity):
        even = (row + lane + parity) % 2 == 0
        er, eb = defect(v0r, v0b, c0r, c0b, p, parity, index1_0, 32, 8, 4)
        res_ref[p - 8] = jnp.where(even, pick(er, lane // 2), pick(eb, lane // 2))
        red, black = v0r[p + 1, 16:48], v0b[p + 1, 16:48]
        u_ref[p - 8] = jnp.where(even, pick(red, lane // 2), pick(black, lane // 2))

    index1_0 = [side_index(32, parity, 128) for parity in range(2)]
    pairs(8, 24, finish, 32)


def around(lo, hi, axis):
    count = lax.axis_size(axis)
    from_above = lax.ppermute(lo, axis, [((i + 1) % count, i) for i in range(count)])
    from_below = lax.ppermute(hi, axis, [(i, (i + 1) % count) for i in range(count)])
    return from_below, from_above


def body(source, conductance):
    vmem, smem, hbm = (pl.BlockSpec(memory_space=m) for m in (pltpu.VMEM, pltpu.SMEM, pltpu.HBM))
    at = jnp.stack([lax.axis_index(a) for a in ("gx", "gy", "gz")]).astype(jnp.int32)
    dma = pltpu.SemaphoreType.DMA

    block, x_slab = arr(16, 32, 128), arr(17, 32, 128)
    buffer = pltpu.VMEM((16, 32, 128), F32)
    wf, wb, lo, hi = call(
        split_fine,
        [(block, block, x_slab, x_slab)],
        (source, conductance),
        [hbm] * 2,
        [buffer, buffer, dma((2,))],
        8,
    )
    xl, xu = around(lo, hi, "gx")
    lo, hi = call(pack_rows, [(arr(66, 8, 128),) * 2], (wf, wb, xl, xu), limit=8)
    yl, yu = around(lo, hi, "gy")
    lo, hi = call(pack_lanes, [(arr(96, 8, 128),) * 2], (wf, wb, xl, xu, yl, yu), limit=8)
    zl, zu = around(lo, hi, "gz")

    colour0 = pltpu.VMEM((34, 64, 128), F32)
    right0 = pltpu.VMEM((32, 48, 128), F32)
    coef0 = pltpu.VMEM((8, 32, 48, 128), F32)
    state0 = (arr(8, 24, 48, 128), arr(8, 24, 48, 128), arr(34, 64, 128))
    g, c0r, c0b, v0b = call(
        fine_down,
        [(arr(16, 192, 128),) + state0, (vmem, hbm, hbm, hbm)],
        (at, wf, wb, xl, xu, yl, yu, zl, zu),
        [smem] + [vmem] * 8,
        [colour0, colour0, right0, right0, coef0, coef0, colour0, colour0, pltpu.VMEM((32, 128), F32), dma((3,))],
        LIMIT,
    )
    g = lax.all_to_all(g, ("gx", "gy"), 0, 0, tiled=True)

    state1 = (arr(8, 16, 32, 128), arr(8, 16, 32, 128), arr(18, 32, 128))
    colour1 = pltpu.VMEM((18, 80, 128), F32)
    right1 = pltpu.VMEM((16, 64, 128), F32)
    coef1 = pltpu.VMEM((8, 16, 64, 128), F32)
    w2, c1r, c1b, v1b = call(
        mid_down,
        [(arr(8, 32, 128),) + state1, (vmem, hbm, hbm, hbm)],
        (at, g),
        [smem, vmem],
        [colour1, colour1, right1, right1, coef1, coef1, colour1, colour1, pltpu.VMEM((64, 128), F32), dma((3,))],
        LIMIT,
    )
    mine = [w2] + [lax.ppermute(w2, "gz", [(i, (i + d) % 8) for i in range(8)]) for d in (2, 4, 6)]
    pair = [lax.ppermute(w, "gz", [(i, i ^ 1) for i in range(8)]) for w in mine]

    scratch = []
    for planes, rows in ((16, 32), (8, 16), (4, 8)):
        scratch += level_scratch(planes, rows) + [pltpu.VMEM((2, planes, rows, 128), F32)]
    scratch += [pltpu.VMEM((18, 48, 128), F32)] * 2 + [pltpu.VMEM((8, 16, 32, 128), F32)] * 2
    scratch += [colour0] * 2 + [pltpu.VMEM((8, 24, 48, 128), F32)] * 2
    scratch += [pltpu.VMEM((96, 128), F32), dma((6,))]
    return call(
        coarse_up,
        [(block, block)],
        (at, *mine, *pair, c1r, c1b, v1b, c0r, c0b, v0b),
        [smem] + [vmem] * 8 + [hbm] * 6,
        scratch,
        LIMIT,
    )


def solution(mesh):
    placed = (P("gx", "gy", "gz"), P("gx", "gy", "gz"))
    return jax.shard_map(body, mesh=mesh, in_specs=placed, out_specs=placed, check_vma=False)
```

```python
import functools

import jax
import jax.numpy as jnp
from jax import lax
from jax.experimental import pallas as pl
from jax.experimental.pallas import tpu as pltpu
from jax.sharding import PartitionSpec as P

F32 = jnp.float32
COARSE_ITERS = 20
MIB = 1 << 20
GROUP = 64
LIMIT = 50
LIMIT_MID = 50
LIMIT_UP = 44


def lanes(rows):
    return lax.broadcasted_iota(jnp.int32, (rows, 128), 1)


def sublanes(rows):
    return lax.broadcasted_iota(jnp.int32, (rows, 128), 0)


def pick(x, idx):
    return jnp.take_along_axis(x, idx, axis=1, mode="promise_in_bounds")


def turn(x, shift):
    shift = shift % 128
    return pltpu.roll(x, shift, 1) if shift else x


def side_index(rows, parity, period):
    lane, row = lanes(rows), sublanes(rows)
    step = 2 * ((row + parity) % 2) - 1
    within = (lane % period + step + period) % period
    return lane - lane % period + within


def side_rule(rows, parity):
    return (sublanes(rows) + parity) % 2 == 0


def beside(x, rule):
    if rule.dtype == jnp.bool_:
        return jnp.where(rule, pltpu.roll(x, 1, 1), pltpu.roll(x, 127, 1))
    return pick(x, rule)


def call(kernel, out, args, specs=None, scratch=(), limit=40):
    vmem = pl.BlockSpec(memory_space=pltpu.VMEM)
    return pl.pallas_call(
        kernel,
        out_shape=out[0],
        in_specs=specs or [vmem] * len(args),
        out_specs=out[1] if len(out) > 1 else jax.tree.map(lambda _: vmem, out[0]),
        scratch_shapes=scratch,
        compiler_params=pltpu.CompilerParams(vmem_limit_bytes=limit * MIB),
        name=kernel.__name__,
    )(*args)


def arr(*shape):
    return jax.ShapeDtypeStruct(shape, F32)


def split_fine(f_in, b_in, wf_ref, wb_ref, lo_ref, hi_ref, f_ref, b_ref, sems):
    loads = [pltpu.make_async_copy(b_in, b_ref, sems.at[0]), pltpu.make_async_copy(f_in, f_ref, sems.at[1])]
    for c in loads:
        c.start()
    lane, row = lanes(32), sublanes(32)
    index = []
    for parity in range(2):
        odd = (row + parity) % 2
        index.append(2 * (lane % 64) + jnp.where(lane < 64, odd, 1 - odd))
    loads[0].wait()
    for i in range(16):
        wb = pick(b_ref[i], index[i % 2])
        wb_ref[i] = wb
        if i < 9:
            lo_ref[8 + i] = wb
        if i > 6:
            hi_ref[1 + i] = wb
    loads[1].wait()
    for i in range(16):
        wf = pick(f_ref[i], index[i % 2])
        wf_ref[i] = wf
        if i < 8:
            lo_ref[i] = wf
        else:
            hi_ref[i - 8] = wf


def by_colour(n, swap):
    lane, row = lanes(16), sublanes(16)
    odd = (row + n) % 2
    return (2 * (lane % 64) + jnp.where((lane < 64) != swap, odd, 1 - odd)) % 128


def spared(index):
    return (index + jnp.where(lanes(16) % 64 < 48, -12, 12)) % 128


def plane_f(wf, xl, xu, p):
    return xl.at[p] if p < 8 else wf.at[p - 8] if p < 24 else xu.at[p - 24]


def plane_b(wb, xl, xu, p):
    return xl.at[9 + p] if p < 8 else wb.at[p - 8] if p < 24 else xu.at[8 + p - 24]


def pack_rows(wf, wb, xl, xu, lo_ref, hi_ref):
    for p in range(32):
        f, b = plane_f(wf, xl, xu, p), plane_b(wb, xl, xu, p)
        lo_ref[p] = f[0:8]
        hi_ref[p] = f[24:32]
        lo_ref[32 + p] = b[0:8]
        hi_ref[32 + p] = b[24:32]
    for i in range(16):
        lo_ref[64 + i // 8, i % 8 : i % 8 + 1] = wb[i, 8:9]
        hi_ref[64 + i // 8, i % 8 : i % 8 + 1] = wb[i, 23:24]


def slab(plane, yl, yu, which, p):
    return jnp.concatenate([yl[32 * which + p], plane[...], yu[32 * which + p]], axis=0)


def pack_lanes(wf, wb, xl, xu, yl, yu, lo_ref, hi_ref):
    slot_of = lanes(48) % 64
    for which, width, base in ((0, 16, 0), (1, 16, 48)):
        count = 64 // width
        slot = slot_of // width
        for group in range(32 // count):
            for s in range(count):
                p = group * count + s
                plane = plane_b(wb, xl, xu, p) if which else plane_f(wf, xl, xu, p)
                v = turn(slab(plane, yl, yu, which, p), width * s)
                if s == 0:
                    low = high = v
                else:
                    low = jnp.where(slot == s, v, low)
                    high = jnp.where(slot == s - 1, v, high)
            start = base + 6 * group
            lo_ref[start : start + 6] = low.reshape(6, 8, 128)
            hi_ref[start : start + 6] = high.reshape(6, 8, 128)


def make_coefs(mine, other, f, coef, p, index, scale, rows, inside=None):
    r = slice(8, 8 + rows)
    centre = mine[p + 1, r]
    mid = other[p + 1, r]
    side = beside(mid, index)
    if inside is not None:
        side = jnp.where(inside, side, 0.0)
    others = (other[p, r], other[p + 2, r], other[p + 1, 7 : 7 + rows], other[p + 1, 9 : 9 + rows], mid, side)
    weights = [centre + b for b in others]
    total = weights[0]
    for w in weights[1:]:
        total = total + w
    inverse = jnp.where(centre > 0.0, 1.0 / jnp.where(centre > 0.0, total, 1.0), 0.0)
    for which in range(6):
        w = weights[which] * inverse
        if which == 5 and inside is not None:
            w = jnp.where(inside, w, 0.0)
        coef[which, p] = w
    coef[6, p] = f * (inverse * (2.0 / scale))
    coef[7, p] = total * (0.5 * scale)


def relaxed(other, coef, p, index, rows, first=0, shift=0):
    a = 8 + first
    r = slice(a, a + rows)
    c = slice(first, first + rows)
    q = p - shift
    mid = other[p + 1, r]
    out = coef[6, q, c] + coef[0, q, c] * other[p, r]
    out = out + coef[1, q, c] * other[p + 2, r]
    out = out + coef[2, q, c] * other[p + 1, a - 1 : a - 1 + rows]
    out = out + coef[3, q, c] * other[p + 1, a + 1 : a + 1 + rows]
    out = out + coef[4, q, c] * mid
    return out + coef[5, q, c] * beside(mid, index)


def pairs(start, stop, body, rows):
    count = stop - start
    most = 8 * GROUP if rows < 64 else 16 * GROUP
    width = max(w for w in (2, 4, 8, 16) if w == 2 or (count % w == 0 and w * rows <= most))

    def step(t, carry):
        for n in range(width):
            body(start + t * width + n, n % 2)
        return carry

    if count == width:
        step(0, 0)
    else:
        lax.fori_loop(0, count // width, step, 0)


def update(mine, other, coef, index, start, stop, rows, flip, shift=0):
    def body(p, parity):
        mine[p + 1, 8 : 8 + rows] = relaxed(other, coef, p, index[(parity + flip) % 2], rows, 0, shift)

    pairs(start, stop, body, rows)


def defect(red, black, cr, cb, p, parity, index, rows, first=0, shift=0):
    r = slice(8 + first, 8 + first + rows)
    c = slice(first, first + rows)
    er = cr[7, p - shift, c] * (relaxed(black, cr, p, index[parity], rows, first, shift) - red[p + 1, r])
    eb = cb[7, p - shift, c] * (relaxed(red, cb, p, index[1 - parity], rows, first, shift) - black[p + 1, r])
    return er, eb


def halve_rows(tmp, value, rows):
    tmp[0:rows] = value
    return 0.125 * (tmp[pl.ds(0, rows // 2, 2)] + tmp[pl.ds(1, rows // 2, 2)])


def double_rows(tmp, value, rows):
    tmp[pl.ds(0, rows, 2)] = value
    tmp[pl.ds(1, rows, 2)] = value


def fine_down(
    at, wf, wb, xl, xu, yl, yu, zl, zu, g_ref, cr_out, cb_out, vb_out, br, bb, fr, fb, cr, cb, vr, vb, tmp, sems
):
    gx, gy, gz = at[0], at[1], at[2]
    lane, row = lanes(48), sublanes(48)
    own = lane < 64
    keep = own | ((lane < 96) & (gz < 7)) | ((lane >= 96) & (gz > 0))
    keep = keep & ((row >= 8) | (gy > 0)) & ((row < 40) | (gy < 3))
    kept = jnp.where(keep, 1.0, 0.0).astype(F32)
    below = jnp.where(gx > 0, 1.0, 0.0).astype(F32)
    above = jnp.where(gx < 3, 1.0, 0.0).astype(F32)
    left = jnp.where(gy > 0, 1.0, 0.0).astype(F32)
    right = jnp.where(gy < 3, 1.0, 0.0).astype(F32)
    vr[...] = jnp.zeros_like(vr)
    vb[...] = jnp.zeros_like(vb)
    edge = jnp.zeros((8, 128), F32)
    for b in (br, bb):
        for q in range(34):
            b[q, 0:8] = edge
            b[q, 56:64] = edge
        for q in (0, 33):
            b[q, 8:56] = jnp.zeros((48, 128), F32)
    for which, width, base in ((0, 16, 0), (1, 16, 48)):
        count = 64 // width
        slot = (lane % 64) // width
        for p in range(32):
            plane = plane_b(wb, xl, xu, p) if which else plane_f(wf, xl, xu, p)
            w = slab(plane, yl, yu, which, p)
            s = p % count
            start = base + 6 * (p // count)
            up = zu[start : start + 6].reshape(48, 128)
            low = zl[start : start + 6].reshape(48, 128)
            both = jnp.where(slot == s, up, low)
            red = jnp.where(own, w, turn(both, 64 - width * s))
            black = jnp.where(own, turn(w, 64), turn(both, -width * s))
            if which:
                k = kept * below if p < 8 else kept * above if p >= 24 else kept
                br[p + 1, 8:56] = red * k
                bb[p + 1, 8:56] = black * k
            else:
                fr[p] = red
                fb[p] = black
    for a in range(2):
        for src, r, ok in ((yl, 7, left), (yu, 56, right)):
            v = src[64 + a] * ok
            t = turn(v, 64)
            for s in range(8):
                br[9 + 8 * a + s, r : r + 1] = v[s : s + 1]
                bb[9 + 8 * a + s, r : r + 1] = t[s : s + 1]
    for v, q in ((xl[8] * below, 0), (xu[16] * above, 33)):
        br[q, 16:48] = v
        bb[q, 16:48] = turn(v, 64)

    index = [side_rule(48, parity) for parity in range(2)]

    def coefs(p, parity):
        make_coefs(br, bb, fr[p], cr, p, index[parity], 1.0, 48)
        make_coefs(bb, br, fb[p], cb, p, index[1 - parity], 1.0, 48)
        vr[p + 1, 8:56] = cr[6, p]

    pairs(0, 32, coefs, 48)
    copies = [
        pltpu.make_async_copy(cr.at[:, pl.ds(4, 24)], cr_out, sems.at[0]),
        pltpu.make_async_copy(cb.at[:, pl.ds(4, 24)], cb_out, sems.at[1]),
        pltpu.make_async_copy(vb, vb_out, sems.at[2]),
    ]
    copies[0].start()
    copies[1].start()
    update(vb, vr, cb, index, 0, 32, 48, 1)
    update(vr, vb, cr, index, 2, 30, 48, 0)
    update(vb, vr, cb, index, 2, 30, 48, 1)
    copies[2].start()
    inner = [side_rule(32, parity) for parity in range(2)]
    swap = gx >= 2
    lane16, row16 = lanes(16), sublanes(16)
    spare = (lane16 % 64 >= 38) & (lane16 % 64 < 58)
    odd16 = [(row16 + parity) % 2 for parity in range(2)]
    own1 = {}
    for n in range(8):
        total = coarse = None
        for parity in range(2):
            p = 8 + 2 * n + parity
            er, eb = defect(vr, vb, cr, cb, p, parity, inner, 32, 8)
            b = br[p + 1, 16:48] + bb[p + 1, 16:48]
            total = er + eb if total is None else total + (er + eb)
            coarse = b if coarse is None else coarse + b
        f1 = pick(halve_rows(tmp, total, 32), by_colour(n, swap))
        b1 = halve_rows(tmp, coarse, 32)
        w1 = jnp.where(spare, pick(b1, spared(by_colour(n, swap))), f1)
        own1[n] = pick(b1, 2 * (lane16 % 32) + jnp.where(lane16 % 64 < 32, odd16[n % 2], 1 - odd16[n % 2]))
        for copy in range(16):
            g_ref[copy, 16 * n : 16 * n + 16] = w1
    for n in range(4):
        w1 = jnp.where(lane16 < 64, own1[n], own1[n + 4])
        for copy in range(16):
            g_ref[copy, 128 + 16 * n : 144 + 16 * n] = w1
    for c in copies:
        c.wait()


def across(g, a, start):
    r = slice(start, start + 16)
    return jnp.concatenate([g[4 * a + y, r] for y in range(4)], axis=0)


def joined_f(g, p):
    wa, wb = (across(g, p // 8 + up, 16 * (p % 8)) for up in (0, 2))
    half = lanes(64) < 64
    return jnp.where(half, wa, wb), turn(jnp.where(half, wb, wa), 64)


def joined_b(g, p):
    i = p % 8
    wa, wb = (across(g, p // 8 + up, 128 + 16 * (i % 4)) for up in (0, 2))
    half = lanes(64) < 64
    red = jnp.where(half, wa, turn(wb, 64)) if i < 4 else jnp.where(half, turn(wa, 64), wb)
    return red, turn(red, -32)


def seam(v, rows):
    r = slice(8, 8 + rows)
    half = lanes(rows) < 64
    v[0, r] = jnp.where(half, 0.0, turn(v[16, r], 64))
    v[17, r] = jnp.where(half, turn(v[1, r], 64), 0.0)


def mid_down(at, g, w2_ref, cr_out, cb_out, vb_out, br, bb, fr, fb, cr, cb, vr, vb, tmp, sems):
    gy, gz = at[1], at[2]
    lane = lanes(64)
    own = lane % 64 < 32
    keep = own | ((lane % 64 < 48) & (gz < 7)) | ((lane % 64 >= 48) & (gz > 0))
    kept = jnp.where(keep, 1.0, 0.0).astype(F32)
    halo = (lane + jnp.where(lane % 64 < 48, 6, -6)) % 128
    for v in (vr, vb):
        v[...] = jnp.zeros_like(v)
    for b in (br, bb):
        b[:, 0:8] = jnp.zeros((18, 8, 128), F32)
        b[:, 72:80] = jnp.zeros((18, 8, 128), F32)
    for p in range(16):
        fr[p], fb[p] = joined_f(g, p)
        red, black = joined_b(g, p)
        br[p + 1, 8:72] = kept * jnp.where(own, red, pick(fr[p], halo))
        bb[p + 1, 8:72] = kept * jnp.where(own, black, pick(fb[p], halo))
    seam(br, 64)
    seam(bb, 64)
    index = [side_index(64, parity, 64) for parity in range(2)]

    def coefs(p, parity):
        make_coefs(br, bb, fr[p], cr, p, index[parity], 0.25, 64)
        make_coefs(bb, br, fb[p], cb, p, index[1 - parity], 0.25, 64)
        vr[p + 1, 8:72] = cr[6, p]

    pairs(0, 16, coefs, 64)
    seam(vr, 64)
    window = pl.multiple_of(jnp.clip(gy * 16 - 8, 0, 32), 8)
    copies = [
        pltpu.make_async_copy(cr.at[:, :, pl.ds(window, 32)], cr_out, sems.at[0]),
        pltpu.make_async_copy(cb.at[:, :, pl.ds(window, 32)], cb_out, sems.at[1]),
        pltpu.make_async_copy(vb.at[:, pl.ds(window + 8, 32)], vb_out, sems.at[2]),
    ]
    copies[0].start()
    copies[1].start()
    update(vb, vr, cb, index, 0, 16, 64, 1)
    seam(vb, 64)
    update(vr, vb, cr, index, 0, 16, 64, 0)
    seam(vr, 64)
    update(vb, vr, cb, index, 0, 16, 64, 1)
    seam(vb, 64)
    copies[2].start()
    lane, row = lanes(32), sublanes(32)
    for n in range(8):
        total = coarse = None
        for parity in range(2):
            p = 2 * n + parity
            er, eb = defect(vr, vb, cr, cb, p, parity, index, 64)
            e = er + eb
            b = br[p + 1, 8:72] + bb[p + 1, 8:72]
            total = e if total is None else total + e
            coarse = b if coarse is None else coarse + b
        f2 = halve_rows(tmp, total, 64)
        b2 = halve_rows(tmp, coarse, 64)
        odd = (row + n) % 2
        idx = 64 * ((lane % 64) // 32) + 2 * (lane % 16) + jnp.where(lane % 32 < 16, odd, 1 - odd)
        w2 = jnp.where(lane < 64, pick(f2, idx), pick(b2, idx))
        w2_ref[n] = w2
    for c in copies:
        c.wait()


def transposed(blocks):
    slot = lanes(32) // 16
    for bit in (1, 2, 4):
        out = list(blocks)
        for i in range(8):
            if not i & bit:
                x, y = blocks[i], blocks[i + bit]
                out[i] = jnp.where(slot & bit == 0, x, turn(y, 16 * bit))
                out[i + bit] = jnp.where(slot & bit == 0, turn(x, -16 * bit), y)
        blocks = out
    return blocks


def level_scratch(planes, rows):
    return [pltpu.VMEM((planes + 2, rows + 16, 128), F32)] * 4 + [pltpu.VMEM((8, planes, rows, 128), F32)] * 2


def clear(refs):
    for v in refs:
        v[...] = jnp.zeros_like(v)


def smooth_down(br, bb, vr, vb, cr, cb, f_of, index, scale, planes, rows, inside):
    def coefs(p, parity):
        fr, fb = f_of(p)
        make_coefs(br, bb, fr, cr, p, index[parity], scale, rows, inside and inside[parity])
        make_coefs(bb, br, fb, cb, p, index[1 - parity], scale, rows, inside and inside[1 - parity])
        vr[p + 1, 8 : 8 + rows] = cr[6, p]

    pairs(0, planes, coefs, rows)
    update(vb, vr, cb, index, 0, planes, rows, 1)
    update(vr, vb, cr, index, 0, planes, rows, 0)
    update(vb, vr, cb, index, 0, planes, rows, 1)


def smooth_up(vr, vb, cr, cb, index, planes, rows):
    for _ in range(2):
        update(vr, vb, cr, index, 0, planes, rows, 0)
        update(vb, vr, cb, index, 0, planes, rows, 1)


def restrict(level, tmp, index, planes, rows, cells, put):
    br, bb, vr, vb, cr, cb = level
    lane, row = lanes(rows // 2), sublanes(rows // 2)
    for n in range(planes // 2):
        total = coarse = None
        for parity in range(2):
            p = 2 * n + parity
            er, eb = defect(vr, vb, cr, cb, p, parity, index, rows)
            b = br[p + 1, 8 : 8 + rows] + bb[p + 1, 8 : 8 + rows]
            total = er + eb if total is None else total + (er + eb)
            coarse = b if coarse is None else coarse + b
        f = halve_rows(tmp, total, rows)
        b = halve_rows(tmp, coarse, rows)
        odd = (row + n) % 2
        red = 2 * (lane % 64) + odd
        black = 2 * (lane % 64) + 1 - odd
        inside = lane < cells
        put(n, *[jnp.where(inside, pick(x, i), 0.0) for x in (f, b) for i in (red, black)])


def prolong(vr, vb, out, tmp, planes, rows):
    lane, row = lanes(rows), sublanes(rows)
    r = slice(8, 8 + rows)
    for n in range(planes):
        even = (row + lane + n) % 2 == 0
        c = jnp.where(even, pick(vr[n + 1, r], lane // 2), pick(vb[n + 1, r], lane // 2))
        double_rows(tmp, c, rows)
        for p in (2 * n, 2 * n + 1):
            out[p + 1, 8 : 8 + 2 * rows] += tmp[0 : 2 * rows]


def coarse_up(
    at, m0, m1, m2, m3, q0, q1, q2, q3, c1r_in, c1b_in, v1b_in, c0r_in, c0b_in, v0b_in, u_ref, res_ref,
    b2r, b2b, v2r, v2b, c2r, c2b, f2,
    b3r, b3b, v3r, v3b, c3r, c3b, f3,
    b4r, b4b, v4r, v4b, c4r, c4b, f4,
    v1r, v1b, c1r, c1b, v0r, v0b, c0r, c0b, tmp, sems,
):
    gx, gy, gz = at[0], at[1], at[2]
    copies = [
        pltpu.make_async_copy(c1r_in, c1r, sems.at[0]),
        pltpu.make_async_copy(c1b_in, c1b, sems.at[1]),
        pltpu.make_async_copy(v1b_in, v1b.at[:, pl.ds(8, 32)], sems.at[2]),
        pltpu.make_async_copy(c0r_in, c0r, sems.at[3]),
        pltpu.make_async_copy(c0b_in, c0b, sems.at[4]),
        pltpu.make_async_copy(v0b_in, v0b, sems.at[5]),
    ]
    for c in copies:
        c.start()
    clear((b2r, b2b, v2r, v2b, b3r, b3b, v3r, v3b, b4r, b4b, v4r, v4b, v1r, v0r))
    v1b[:, 0:8] = jnp.zeros((18, 8, 128), F32)
    v1b[:, 40:48] = jnp.zeros((18, 8, 128), F32)

    chip = gz // 2
    first = gz % 2 == 0
    for n in range(8):
        near = [(jnp.where(first, a[n], b[n]), jnp.where(first, b[n], a[n])) for a, b in ((m0, q0), (m1, q1), (m2, q2), (m3, q3))]
        blocks = []
        for c in range(4):
            for core in range(2):
                v = near[0][core]
                for back in range(1, 4):
                    v = jnp.where(chip == (c + back) % 4, near[back][core], v)
                blocks.append(v)
        out = transposed(blocks)
        for h in range(2):
            p = n + 8 * h
            f2[0, p] = out[2 * h]
            f2[1, p] = out[2 * h + 1]
            b2r[p + 1, 8:40] = out[4 + 2 * h]
            b2b[p + 1, 8:40] = out[5 + 2 * h]
    lane = lanes(32)
    index2 = [side_rule(32, parity) for parity in range(2)]
    inside2 = [lane != jnp.where(index2[parity], 0, 127) for parity in range(2)]
    smooth_down(b2r, b2b, v2r, v2b, c2r, c2b, lambda p: (f2[0, p], f2[1, p]), index2, 0.25**2, 16, 32, inside2)

    def put3(n, fr, fb, br, bb):
        f3[0, n], f3[1, n] = fr, fb
        b3r[n + 1, 8:24], b3b[n + 1, 8:24] = br, bb

    restrict((b2r, b2b, v2r, v2b, c2r, c2b), tmp, index2, 16, 32, 64, put3)

    index3 = [side_rule(16, parity) for parity in range(2)]
    smooth_down(b3r, b3b, v3r, v3b, c3r, c3b, lambda p: (f3[0, p], f3[1, p]), index3, 0.25**3, 8, 16, None)

    def put4(n, fr, fb, br, bb):
        f4[0, n], f4[1, n] = fr, fb
        b4r[n + 1, 8:16], b4b[n + 1, 8:16] = br, bb

    restrict((b3r, b3b, v3r, v3b, c3r, c3b), tmp, index3, 8, 16, 32, put4)

    index4 = [side_rule(8, parity) for parity in range(2)]

    for p in range(4):
        make_coefs(b4r, b4b, f4[0, p], c4r, p, index4[p % 2], 0.25**4, 8)
        make_coefs(b4b, b4r, f4[1, p], c4b, p, index4[1 - p % 2], 0.25**4, 8)
    row8 = sublanes(8)
    inner = (row8 > 0, row8 < 7)
    cr4 = [[c4r[w, p] for w in range(7)] for p in range(4)]
    cb4 = [[c4b[w, p] for w in range(7)] for p in range(4)]
    for c in cr4 + cb4:
        c[2] = jnp.where(inner[0], c[2], 0.0)
        c[3] = jnp.where(inner[1], c[3], 0.0)

    def half(other, coefs, flip):
        out = []
        for p in range(4):
            c, v = coefs[p], other[p]
            w = c[6] + c[4] * v
            if p > 0:
                w = w + c[0] * other[p - 1]
            if p < 3:
                w = w + c[1] * other[p + 1]
            w = w + c[2] * pltpu.roll(v, 1, 0) + c[3] * pltpu.roll(v, 7, 0)
            out.append(w + c[5] * beside(v, index4[(p + flip) % 2]))
        return out

    def coarse_step(count, state):
        black = list(state)
        red = half(black, cr4, 0)
        return tuple(half(red, cb4, 1))

    black = lax.fori_loop(0, COARSE_ITERS - 1, coarse_step, (jnp.zeros((8, 128), F32),) * 4)
    red = half(black, cr4, 0)
    black = half(red, cb4, 1)
    for p in range(4):
        v4r[p + 1, 8:16] = red[p]
        v4b[p + 1, 8:16] = black[p]

    prolong(v4r, v4b, v3b, tmp, 4, 8)
    smooth_up(v3r, v3b, c3r, c3b, index3, 8, 16)
    prolong(v3r, v3b, v2b, tmp, 8, 16)
    smooth_up(v2r, v2b, c2r, c2b, index2, 16, 32)

    for c in copies[:3]:
        c.wait()
    lane, row = lanes(32), sublanes(32)
    near = lane % 64 - jnp.where(lane % 64 < 48, 0, 64)
    cell = gz * 32 + near
    valid = (cell >= 0) & (cell < 256)
    idx = jnp.clip(cell, 0, 255) // 2
    window = pl.multiple_of(jnp.clip(gy * 16 - 8, 0, 32), 8)
    for n in range(8):
        even = (row + lane + n) % 2 == 0
        parts = []
        for p in (n, n + 8):
            parts.append(jnp.where(even, pick(v2r[p + 1, 8:40], idx), pick(v2b[p + 1, 8:40], idx)))
        c = jnp.where(valid, jnp.where(lane < 64, parts[0], parts[1]), 0.0)
        double_rows(tmp, c, 32)
        for p in (2 * n, 2 * n + 1):
            v1b[p + 1, 8:40] += tmp[pl.ds(window, 32)]
    seam(v1b, 32)
    index1 = [side_index(32, parity, 64) for parity in range(2)]
    for _ in range(2):
        update(v1r, v1b, c1r, index1, 0, 16, 32, 0)
        seam(v1r, 32)
        update(v1b, v1r, c1b, index1, 0, 16, 32, 1)
        seam(v1b, 32)

    for c in copies[3:]:
        c.wait()
    start = pl.multiple_of(gy * 16 - window, 8)
    cell = lane - jnp.where(lane < 96, 0, 128)
    idx = (cell // 2) % 64
    for n in range(-3, 11):
        plane = gx * 8 + n
        held = jnp.clip(plane, 0, 31)
        at_half = idx + 64 * (held // 16)
        even = (row + lane + n) % 2 == 0
        red = v1r[held % 16 + 1, pl.ds(start, 32)]
        black = v1b[held % 16 + 1, pl.ds(start, 32)]
        c = jnp.where(even, pick(red, at_half), pick(black, at_half))
        c = c * jnp.where((plane >= 0) & (plane < 32), 1.0, 0.0).astype(F32)
        tmp[64:96] = c
        double_rows(tmp, tmp[68:92], 24)
        for p in (2 * n + 8, 2 * n + 9):
            v0b[p + 1, 8:56] += tmp[0:48]
    index0 = [side_rule(48, parity) for parity in range(2)]
    update(v0r, v0b, c0r, index0, 4, 28, 48, 0, 4)
    update(v0b, v0r, c0b, index0, 4, 28, 48, 1, 4)
    update(v0r, v0b, c0r, index0, 6, 26, 48, 0, 4)
    update(v0b, v0r, c0b, index0, 6, 26, 48, 1, 4)

    def finish(p, parity):
        even = (row + lane + parity) % 2 == 0
        er, eb = defect(v0r, v0b, c0r, c0b, p, parity, index1_0, 32, 8, 4)
        res_ref[p - 8] = jnp.where(even, pick(er, lane // 2), pick(eb, lane // 2))
        red, black = v0r[p + 1, 16:48], v0b[p + 1, 16:48]
        u_ref[p - 8] = jnp.where(even, pick(red, lane // 2), pick(black, lane // 2))

    index1_0 = [side_rule(32, parity) for parity in range(2)]
    pairs(8, 24, finish, 32)


def around(lo, hi, axis):
    count = lax.axis_size(axis)
    from_above = lax.ppermute(lo, axis, [((i + 1) % count, i) for i in range(count)])
    from_below = lax.ppermute(hi, axis, [(i, (i + 1) % count) for i in range(count)])
    return from_below, from_above


def body(source, conductance):
    vmem, smem, hbm = (pl.BlockSpec(memory_space=m) for m in (pltpu.VMEM, pltpu.SMEM, pltpu.HBM))
    at = jnp.stack([lax.axis_index(a) for a in ("gx", "gy", "gz")]).astype(jnp.int32)
    dma = pltpu.SemaphoreType.DMA

    block, x_slab = arr(16, 32, 128), arr(17, 32, 128)
    buffer = pltpu.VMEM((16, 32, 128), F32)
    wf, wb, lo, hi = call(
        split_fine,
        [(block, block, x_slab, x_slab)],
        (source, conductance),
        [hbm] * 2,
        [buffer, buffer, dma((2,))],
        8,
    )
    xl, xu = around(lo, hi, "gx")
    lo, hi = call(pack_rows, [(arr(66, 8, 128),) * 2], (wf, wb, xl, xu), limit=8)
    yl, yu = around(lo, hi, "gy")
    lo, hi = call(pack_lanes, [(arr(96, 8, 128),) * 2], (wf, wb, xl, xu, yl, yu), limit=8)
    zl, zu = around(lo, hi, "gz")

    colour0 = pltpu.VMEM((34, 64, 128), F32)
    right0 = pltpu.VMEM((32, 48, 128), F32)
    coef0 = pltpu.VMEM((8, 32, 48, 128), F32)
    state0 = (arr(8, 24, 48, 128), arr(8, 24, 48, 128), arr(34, 64, 128))
    g, c0r, c0b, v0b = call(
        fine_down,
        [(arr(16, 192, 128),) + state0, (vmem, hbm, hbm, hbm)],
        (at, wf, wb, xl, xu, yl, yu, zl, zu),
        [smem] + [vmem] * 8,
        [colour0, colour0, right0, right0, coef0, coef0, colour0, colour0, pltpu.VMEM((32, 128), F32), dma((3,))],
        LIMIT,
    )
    g = lax.all_to_all(g, ("gx", "gy"), 0, 0, tiled=True)

    state1 = (arr(8, 16, 32, 128), arr(8, 16, 32, 128), arr(18, 32, 128))
    colour1 = pltpu.VMEM((18, 80, 128), F32)
    right1 = pltpu.VMEM((16, 64, 128), F32)
    coef1 = pltpu.VMEM((8, 16, 64, 128), F32)
    w2, c1r, c1b, v1b = call(
        mid_down,
        [(arr(8, 32, 128),) + state1, (vmem, hbm, hbm, hbm)],
        (at, g),
        [smem, vmem],
        [colour1, colour1, right1, right1, coef1, coef1, colour1, colour1, pltpu.VMEM((64, 128), F32), dma((3,))],
        LIMIT_MID,
    )
    mine = [w2] + [lax.ppermute(w2, "gz", [(i, (i + d) % 8) for i in range(8)]) for d in (2, 4, 6)]
    pair = [lax.ppermute(w, "gz", [(i, i ^ 1) for i in range(8)]) for w in mine]

    scratch = []
    for planes, rows in ((16, 32), (8, 16), (4, 8)):
        scratch += level_scratch(planes, rows) + [pltpu.VMEM((2, planes, rows, 128), F32)]
    scratch += [pltpu.VMEM((18, 48, 128), F32)] * 2 + [pltpu.VMEM((8, 16, 32, 128), F32)] * 2
    scratch += [colour0] * 2 + [pltpu.VMEM((8, 24, 48, 128), F32)] * 2
    scratch += [pltpu.VMEM((96, 128), F32), dma((6,))]
    return call(
        coarse_up,
        [(block, block)],
        (at, *mine, *pair, c1r, c1b, v1b, c0r, c0b, v0b),
        [smem] + [vmem] * 8 + [hbm] * 6,
        scratch,
        LIMIT_UP,
    )


def solution(mesh):
    placed = (P("gx", "gy", "gz"), P("gx", "gy", "gz"))
    return jax.shard_map(body, mesh=mesh, in_specs=placed, out_specs=placed, check_vma=False)
```

```python
import functools

import jax
import jax.numpy as jnp
from jax import lax
from jax.experimental import pallas as pl
from jax.experimental.pallas import tpu as pltpu
from jax.sharding import PartitionSpec as P

F32 = jnp.float32
COARSE_ITERS = 20
MIB = 1 << 20
GROUP = 64
LIMIT = 50
LIMIT_MID = 50
LIMIT_UP = 50


def lanes(rows):
    return lax.broadcasted_iota(jnp.int32, (rows, 128), 1)


def sublanes(rows):
    return lax.broadcasted_iota(jnp.int32, (rows, 128), 0)


def pick(x, idx):
    return jnp.take_along_axis(x, idx, axis=1, mode="promise_in_bounds")


def turn(x, shift):
    shift = shift % 128
    return pltpu.roll(x, shift, 1) if shift else x


def side_index(rows, parity, period):
    lane, row = lanes(rows), sublanes(rows)
    step = 2 * ((row + parity) % 2) - 1
    within = (lane % period + step + period) % period
    return lane - lane % period + within


def side_rule(rows, parity):
    return (sublanes(rows) + parity) % 2 == 0


def beside(x, rule):
    if rule.dtype == jnp.bool_:
        return jnp.where(rule, pltpu.roll(x, 1, 1), pltpu.roll(x, 127, 1))
    return pick(x, rule)


def call(kernel, out, args, specs=None, scratch=(), limit=40):
    vmem = pl.BlockSpec(memory_space=pltpu.VMEM)
    return pl.pallas_call(
        kernel,
        out_shape=out[0],
        in_specs=specs or [vmem] * len(args),
        out_specs=out[1] if len(out) > 1 else jax.tree.map(lambda _: vmem, out[0]),
        scratch_shapes=scratch,
        compiler_params=pltpu.CompilerParams(vmem_limit_bytes=limit * MIB),
        name=kernel.__name__,
    )(*args)


def arr(*shape):
    return jax.ShapeDtypeStruct(shape, F32)


def split_fine(f_in, b_in, wf_ref, wb_ref, lo_ref, hi_ref, b1_ref, f_ref, b_ref, tmp, sems):
    loads = [pltpu.make_async_copy(b_in, b_ref, sems.at[0]), pltpu.make_async_copy(f_in, f_ref, sems.at[1])]
    for c in loads:
        c.start()
    lane, row = lanes(32), sublanes(32)
    index = []
    for parity in range(2):
        odd = (row + parity) % 2
        index.append(2 * (lane % 64) + jnp.where(lane < 64, odd, 1 - odd))
    loads[0].wait()
    lane16, row16 = lanes(16), sublanes(16)
    own = []
    for n in range(8):
        w = [pick(b_ref[2 * n + parity], index[parity]) for parity in range(2)]
        for parity in range(2):
            i = 2 * n + parity
            wb_ref[i] = w[parity]
            if i < 9:
                lo_ref[8 + i] = w[parity]
            if i > 6:
                hi_ref[1 + i] = w[parity]
        both = w[0] + w[1]
        odd = (row16 + n) % 2
        cell = 2 * (lane16 % 32) + jnp.where(lane16 % 64 < 32, odd, 1 - odd)
        own.append(pick(halve_rows(tmp, both + turn(both, 64), 32), cell))
    for n in range(4):
        b1_ref[16 * n : 16 * n + 16] = jnp.where(lane16 < 64, own[n], own[n + 4])
    loads[1].wait()
    for i in range(16):
        wf = pick(f_ref[i], index[i % 2])
        wf_ref[i] = wf
        if i < 8:
            lo_ref[i] = wf
        else:
            hi_ref[i - 8] = wf


def by_colour(n, swap):
    lane, row = lanes(16), sublanes(16)
    odd = (row + n) % 2
    return (2 * (lane % 64) + jnp.where((lane < 64) != swap, odd, 1 - odd)) % 128


def spared(index):
    return (index + jnp.where(lanes(16) % 64 < 48, -12, 12)) % 128


def plane_f(wf, xl, xu, p):
    return xl.at[p] if p < 8 else wf.at[p - 8] if p < 24 else xu.at[p - 24]


def plane_b(wb, xl, xu, p):
    return xl.at[9 + p] if p < 8 else wb.at[p - 8] if p < 24 else xu.at[8 + p - 24]


def pack_rows(wf, wb, xl, xu, b0, b1, b2, b3, lo_ref, hi_ref, b1_ref):
    for back, b in enumerate((b0, b1, b2, b3)):
        b1_ref[back] = b[...]
    for p in range(32):
        f, b = plane_f(wf, xl, xu, p), plane_b(wb, xl, xu, p)
        lo_ref[p] = f[0:8]
        hi_ref[p] = f[24:32]
        lo_ref[32 + p] = b[0:8]
        hi_ref[32 + p] = b[24:32]
    for i in range(16):
        lo_ref[64 + i // 8, i % 8 : i % 8 + 1] = wb[i, 8:9]
        hi_ref[64 + i // 8, i % 8 : i % 8 + 1] = wb[i, 23:24]


def slab(plane, yl, yu, which, p):
    return jnp.concatenate([yl[32 * which + p], plane[...], yu[32 * which + p]], axis=0)


def pack_lanes(wf, wb, xl, xu, yl, yu, lo_ref, hi_ref):
    slot_of = lanes(48) % 64
    for which, width, base in ((0, 16, 0), (1, 16, 48)):
        count = 64 // width
        slot = slot_of // width
        for group in range(32 // count):
            for s in range(count):
                p = group * count + s
                plane = plane_b(wb, xl, xu, p) if which else plane_f(wf, xl, xu, p)
                v = turn(slab(plane, yl, yu, which, p), width * s)
                if s == 0:
                    low = high = v
                else:
                    low = jnp.where(slot == s, v, low)
                    high = jnp.where(slot == s - 1, v, high)
            start = base + 6 * group
            lo_ref[start : start + 6] = low.reshape(6, 8, 128)
            hi_ref[start : start + 6] = high.reshape(6, 8, 128)


def make_coefs(mine, other, f, coef, p, index, scale, rows, inside=None):
    r = slice(8, 8 + rows)
    centre = mine[p + 1, r]
    mid = other[p + 1, r]
    side = beside(mid, index)
    if inside is not None:
        side = jnp.where(inside, side, 0.0)
    others = (other[p, r], other[p + 2, r], other[p + 1, 7 : 7 + rows], other[p + 1, 9 : 9 + rows], mid, side)
    weights = [centre + b for b in others]
    total = weights[0]
    for w in weights[1:]:
        total = total + w
    inverse = jnp.where(centre > 0.0, 1.0 / jnp.where(centre > 0.0, total, 1.0), 0.0)
    for which in range(6):
        w = weights[which] * inverse
        if which == 5 and inside is not None:
            w = jnp.where(inside, w, 0.0)
        coef[which, p] = w
    coef[6, p] = f * (inverse * (2.0 / scale))
    coef[7, p] = total * (0.5 * scale)


def relaxed(other, coef, p, index, rows, first=0, shift=0):
    a = 8 + first
    r = slice(a, a + rows)
    c = slice(first, first + rows)
    q = p - shift
    mid = other[p + 1, r]
    out = coef[6, q, c] + coef[0, q, c] * other[p, r]
    out = out + coef[1, q, c] * other[p + 2, r]
    out = out + coef[2, q, c] * other[p + 1, a - 1 : a - 1 + rows]
    out = out + coef[3, q, c] * other[p + 1, a + 1 : a + 1 + rows]
    out = out + coef[4, q, c] * mid
    return out + coef[5, q, c] * beside(mid, index)


def pairs(start, stop, body, rows):
    count = stop - start
    most = 8 * GROUP if rows < 64 else 16 * GROUP
    width = max(w for w in (2, 4, 8, 16) if w == 2 or (count % w == 0 and w * rows <= most))

    def step(t, carry):
        for n in range(width):
            body(start + t * width + n, n % 2)
        return carry

    if count == width:
        step(0, 0)
    else:
        lax.fori_loop(0, count // width, step, 0)


def update(mine, other, coef, index, start, stop, rows, flip, shift=0):
    def body(p, parity):
        mine[p + 1, 8 : 8 + rows] = relaxed(other, coef, p, index[(parity + flip) % 2], rows, 0, shift)

    pairs(start, stop, body, rows)


def defect(red, black, cr, cb, p, parity, index, rows, first=0, shift=0):
    r = slice(8 + first, 8 + first + rows)
    c = slice(first, first + rows)
    er = cr[7, p - shift, c] * (relaxed(black, cr, p, index[parity], rows, first, shift) - red[p + 1, r])
    eb = cb[7, p - shift, c] * (relaxed(red, cb, p, index[1 - parity], rows, first, shift) - black[p + 1, r])
    return er, eb


def halve_rows(tmp, value, rows):
    tmp[0:rows] = value
    return 0.125 * (tmp[pl.ds(0, rows // 2, 2)] + tmp[pl.ds(1, rows // 2, 2)])


def double_rows(tmp, value, rows):
    tmp[pl.ds(0, rows, 2)] = value
    tmp[pl.ds(1, rows, 2)] = value


def fine_down(
    at, wf, wb, xl, xu, yl, yu, zl, zu, g_ref, cr_out, cb_out, vb_out, br, bb, fr, fb, cr, cb, vr, vb, tmp, sems
):
    gx, gy, gz = at[0], at[1], at[2]
    lane, row = lanes(48), sublanes(48)
    own = lane < 64
    keep = own | ((lane < 96) & (gz < 7)) | ((lane >= 96) & (gz > 0))
    keep = keep & ((row >= 8) | (gy > 0)) & ((row < 40) | (gy < 3))
    kept = jnp.where(keep, 1.0, 0.0).astype(F32)
    below = jnp.where(gx > 0, 1.0, 0.0).astype(F32)
    above = jnp.where(gx < 3, 1.0, 0.0).astype(F32)
    left = jnp.where(gy > 0, 1.0, 0.0).astype(F32)
    right = jnp.where(gy < 3, 1.0, 0.0).astype(F32)
    vr[...] = jnp.zeros_like(vr)
    vb[...] = jnp.zeros_like(vb)
    edge = jnp.zeros((8, 128), F32)
    for b in (br, bb):
        for q in range(34):
            b[q, 0:8] = edge
            b[q, 56:64] = edge
        for q in (0, 33):
            b[q, 8:56] = jnp.zeros((48, 128), F32)
    for which, width, base in ((0, 16, 0), (1, 16, 48)):
        count = 64 // width
        slot = (lane % 64) // width
        for p in range(32):
            plane = plane_b(wb, xl, xu, p) if which else plane_f(wf, xl, xu, p)
            w = slab(plane, yl, yu, which, p)
            s = p % count
            start = base + 6 * (p // count)
            up = zu[start : start + 6].reshape(48, 128)
            low = zl[start : start + 6].reshape(48, 128)
            both = jnp.where(slot == s, up, low)
            red = jnp.where(own, w, turn(both, 64 - width * s))
            black = jnp.where(own, turn(w, 64), turn(both, -width * s))
            if which:
                k = kept * below if p < 8 else kept * above if p >= 24 else kept
                br[p + 1, 8:56] = red * k
                bb[p + 1, 8:56] = black * k
            else:
                fr[p] = red
                fb[p] = black
    for a in range(2):
        for src, r, ok in ((yl, 7, left), (yu, 56, right)):
            v = src[64 + a] * ok
            t = turn(v, 64)
            for s in range(8):
                br[9 + 8 * a + s, r : r + 1] = v[s : s + 1]
                bb[9 + 8 * a + s, r : r + 1] = t[s : s + 1]
    for v, q in ((xl[8] * below, 0), (xu[16] * above, 33)):
        br[q, 16:48] = v
        bb[q, 16:48] = turn(v, 64)

    index = [side_rule(48, parity) for parity in range(2)]

    def coefs(p, parity):
        make_coefs(br, bb, fr[p], cr, p, index[parity], 1.0, 48)
        make_coefs(bb, br, fb[p], cb, p, index[1 - parity], 1.0, 48)
        vr[p + 1, 8:56] = cr[6, p]

    pairs(0, 32, coefs, 48)
    copies = [
        pltpu.make_async_copy(cr.at[:, pl.ds(4, 24)], cr_out, sems.at[0]),
        pltpu.make_async_copy(cb.at[:, pl.ds(4, 24)], cb_out, sems.at[1]),
        pltpu.make_async_copy(vb, vb_out, sems.at[2]),
    ]
    copies[0].start()
    copies[1].start()
    update(vb, vr, cb, index, 0, 32, 48, 1)
    update(vr, vb, cr, index, 2, 30, 48, 0)
    update(vb, vr, cb, index, 2, 30, 48, 1)
    copies[2].start()
    inner = [side_rule(32, parity) for parity in range(2)]
    swap = gx >= 2
    lane16 = lanes(16)
    spare = (lane16 % 64 >= 38) & (lane16 % 64 < 58)
    for n in range(8):
        total = coarse = None
        for parity in range(2):
            p = 8 + 2 * n + parity
            er, eb = defect(vr, vb, cr, cb, p, parity, inner, 32, 8)
            b = br[p + 1, 16:48] + bb[p + 1, 16:48]
            total = er + eb if total is None else total + (er + eb)
            coarse = b if coarse is None else coarse + b
        f1 = pick(halve_rows(tmp, total, 32), by_colour(n, swap))
        b1 = halve_rows(tmp, coarse, 32)
        w1 = jnp.where(spare, pick(b1, spared(by_colour(n, swap))), f1)
        for copy in range(16):
            g_ref[copy, 16 * n : 16 * n + 16] = w1
    for c in copies:
        c.wait()


def across(g, a, start):
    r = slice(start, start + 16)
    return jnp.concatenate([g[4 * a + y, r] for y in range(4)], axis=0)


def joined_f(g, p):
    wa, wb = (across(g, p // 8 + up, 16 * (p % 8)) for up in (0, 2))
    half = lanes(64) < 64
    return jnp.where(half, wa, wb), turn(jnp.where(half, wb, wa), 64)


def across_b(gx, gy, held, a, n):
    back = (gx - a + 4) % 4
    r = slice(16 * n, 16 * n + 16)
    out = []
    for y in range(4):
        e = (gy - y + 4) % 4
        v = held[0][e, r]
        for d in range(1, 4):
            v = jnp.where(back == d, held[d][e, r], v)
        out.append(v)
    return jnp.concatenate(out, axis=0)


def joined_b(gx, gy, held, a, n):
    wa, wb = (across_b(gx, gy, held, a + up, n) for up in (0, 2))
    half = lanes(64) < 64
    reds = jnp.where(half, wa, turn(wb, 64)), jnp.where(half, turn(wa, 64), wb)
    return [(red, turn(red, -32)) for red in reds]


def seam(v, rows):
    r = slice(8, 8 + rows)
    half = lanes(rows) < 64
    v[0, r] = jnp.where(half, 0.0, turn(v[16, r], 64))
    v[17, r] = jnp.where(half, turn(v[1, r], 64), 0.0)


def mid_down(at, g, h0, h1, h2, h3, w2_ref, c_out, vb_out, br, bb, fr, fb, cr, cb, vr, vb, tmp, sems):
    gx, gy, gz = at[0], at[1], at[2]
    lane = lanes(64)
    own = lane % 64 < 32
    keep = own | ((lane % 64 < 48) & (gz < 7)) | ((lane % 64 >= 48) & (gz > 0))
    kept = jnp.where(keep, 1.0, 0.0).astype(F32)
    halo = (lane + jnp.where(lane % 64 < 48, 6, -6)) % 128
    for v in (vr, vb):
        v[...] = jnp.zeros_like(v)
    for b in (br, bb):
        b[:, 0:8] = jnp.zeros((18, 8, 128), F32)
        b[:, 72:80] = jnp.zeros((18, 8, 128), F32)
    for p in range(16):
        fr[p], fb[p] = joined_f(g, p)
    for a in range(2):
        for n in range(4):
            for up, (red, black) in enumerate(joined_b(gx, gy, (h0, h1, h2, h3), a, n)):
                p = 8 * a + n + 4 * up
                br[p + 1, 8:72] = kept * jnp.where(own, red, pick(fr[p], halo))
                bb[p + 1, 8:72] = kept * jnp.where(own, black, pick(fb[p], halo))
    seam(br, 64)
    seam(bb, 64)
    index = [side_index(64, parity, 64) for parity in range(2)]

    def coefs(p, parity):
        make_coefs(br, bb, fr[p], cr, p, index[parity], 0.25, 64)
        make_coefs(bb, br, fb[p], cb, p, index[1 - parity], 0.25, 64)
        vr[p + 1, 8:72] = cr[6, p]

    pairs(0, 16, coefs, 64)
    seam(vr, 64)
    window = pl.multiple_of(jnp.clip(gy * 16 - 8, 0, 32), 8)
    copies = [
        pltpu.make_async_copy(cr.at[:, :, pl.ds(window, 32)], c_out.at[0], sems.at[0]),
        pltpu.make_async_copy(cb.at[:, :, pl.ds(window, 32)], c_out.at[1], sems.at[1]),
        pltpu.make_async_copy(vb.at[:, pl.ds(window + 8, 32)], vb_out, sems.at[2]),
    ]
    copies[0].start()
    copies[1].start()
    update(vb, vr, cb, index, 0, 16, 64, 1)
    seam(vb, 64)
    update(vr, vb, cr, index, 0, 16, 64, 0)
    seam(vr, 64)
    update(vb, vr, cb, index, 0, 16, 64, 1)
    seam(vb, 64)
    copies[2].start()
    lane, row = lanes(32), sublanes(32)
    for n in range(8):
        total = coarse = None
        for parity in range(2):
            p = 2 * n + parity
            er, eb = defect(vr, vb, cr, cb, p, parity, index, 64)
            e = er + eb
            b = br[p + 1, 8:72] + bb[p + 1, 8:72]
            total = e if total is None else total + e
            coarse = b if coarse is None else coarse + b
        f2 = halve_rows(tmp, total, 64)
        b2 = halve_rows(tmp, coarse, 64)
        odd = (row + n) % 2
        idx = 64 * ((lane % 64) // 32) + 2 * (lane % 16) + jnp.where(lane % 32 < 16, odd, 1 - odd)
        w2 = jnp.where(lane < 64, pick(f2, idx), pick(b2, idx))
        w2_ref[n] = w2
    for c in copies:
        c.wait()


def transposed(blocks):
    slot = lanes(32) // 16
    for bit in (1, 2, 4):
        out = list(blocks)
        for i in range(8):
            if not i & bit:
                x, y = blocks[i], blocks[i + bit]
                out[i] = jnp.where(slot & bit == 0, x, turn(y, 16 * bit))
                out[i + bit] = jnp.where(slot & bit == 0, turn(x, -16 * bit), y)
        blocks = out
    return blocks


def level_scratch(planes, rows):
    return [pltpu.VMEM((planes + 2, rows + 16, 128), F32)] * 4 + [pltpu.VMEM((8, planes, rows, 128), F32)] * 2


def clear(refs):
    for v in refs:
        v[...] = jnp.zeros_like(v)


def smooth_down(br, bb, vr, vb, cr, cb, f_of, index, scale, planes, rows, inside):
    def coefs(p, parity):
        fr, fb = f_of(p)
        make_coefs(br, bb, fr, cr, p, index[parity], scale, rows, inside and inside[parity])
        make_coefs(bb, br, fb, cb, p, index[1 - parity], scale, rows, inside and inside[1 - parity])
        vr[p + 1, 8 : 8 + rows] = cr[6, p]

    pairs(0, planes, coefs, rows)
    update(vb, vr, cb, index, 0, planes, rows, 1)
    update(vr, vb, cr, index, 0, planes, rows, 0)
    update(vb, vr, cb, index, 0, planes, rows, 1)


def smooth_up(vr, vb, cr, cb, index, planes, rows):
    for _ in range(2):
        update(vr, vb, cr, index, 0, planes, rows, 0)
        update(vb, vr, cb, index, 0, planes, rows, 1)


def restrict(level, tmp, index, planes, rows, cells, put):
    br, bb, vr, vb, cr, cb = level
    lane, row = lanes(rows // 2), sublanes(rows // 2)
    for n in range(planes // 2):
        total = coarse = None
        for parity in range(2):
            p = 2 * n + parity
            er, eb = defect(vr, vb, cr, cb, p, parity, index, rows)
            b = br[p + 1, 8 : 8 + rows] + bb[p + 1, 8 : 8 + rows]
            total = er + eb if total is None else total + (er + eb)
            coarse = b if coarse is None else coarse + b
        f = halve_rows(tmp, total, rows)
        b = halve_rows(tmp, coarse, rows)
        odd = (row + n) % 2
        red = 2 * (lane % 64) + odd
        black = 2 * (lane % 64) + 1 - odd
        inside = lane < cells
        put(n, *[jnp.where(inside, pick(x, i), 0.0) for x in (f, b) for i in (red, black)])


def prolong(vr, vb, out, tmp, planes, rows):
    lane, row = lanes(rows), sublanes(rows)
    r = slice(8, 8 + rows)
    for n in range(planes):
        even = (row + lane + n) % 2 == 0
        c = jnp.where(even, pick(vr[n + 1, r], lane // 2), pick(vb[n + 1, r], lane // 2))
        double_rows(tmp, c, rows)
        for p in (2 * n, 2 * n + 1):
            out[p + 1, 8 : 8 + 2 * rows] += tmp[0 : 2 * rows]


def coarse_up(
    at, m0, m1, m2, m3, q0, q1, q2, q3, c1_in, v1b_in, c0r_in, c0b_in, v0b_in, u_ref, res_ref,
    b2r, b2b, v2r, v2b, c2r, c2b, f2,
    b3r, b3b, v3r, v3b, c3r, c3b, f3,
    b4r, b4b, v4r, v4b, c4r, c4b, f4,
    v1r, v1b, c1r, c1b, v0r, v0b, c0r, c0b, tmp, sems,
):
    gx, gy, gz = at[0], at[1], at[2]
    copies = [
        pltpu.make_async_copy(c1_in.at[0], c1r, sems.at[0]),
        pltpu.make_async_copy(c1_in.at[1], c1b, sems.at[1]),
        pltpu.make_async_copy(v1b_in, v1b.at[:, pl.ds(8, 32)], sems.at[2]),
        pltpu.make_async_copy(c0r_in, c0r, sems.at[3]),
        pltpu.make_async_copy(c0b_in, c0b, sems.at[4]),
        pltpu.make_async_copy(v0b_in, v0b, sems.at[5]),
    ]
    for c in copies:
        c.start()
    clear((b2r, b2b, v2r, v2b, b3r, b3b, v3r, v3b, b4r, b4b, v4r, v4b, v1r, v0r))
    v1b[:, 0:8] = jnp.zeros((18, 8, 128), F32)
    v1b[:, 40:48] = jnp.zeros((18, 8, 128), F32)

    chip = gz // 2
    first = gz % 2 == 0
    for n in range(8):
        near = [(jnp.where(first, a[n], b[n]), jnp.where(first, b[n], a[n])) for a, b in ((m0, q0), (m1, q1), (m2, q2), (m3, q3))]
        blocks = []
        for c in range(4):
            for core in range(2):
                v = near[0][core]
                for back in range(1, 4):
                    v = jnp.where(chip == (c + back) % 4, near[back][core], v)
                blocks.append(v)
        out = transposed(blocks)
        for h in range(2):
            p = n + 8 * h
            f2[0, p] = out[2 * h]
            f2[1, p] = out[2 * h + 1]
            b2r[p + 1, 8:40] = out[4 + 2 * h]
            b2b[p + 1, 8:40] = out[5 + 2 * h]
    lane = lanes(32)
    index2 = [side_rule(32, parity) for parity in range(2)]
    inside2 = [lane != jnp.where(index2[parity], 0, 127) for parity in range(2)]
    smooth_down(b2r, b2b, v2r, v2b, c2r, c2b, lambda p: (f2[0, p], f2[1, p]), index2, 0.25**2, 16, 32, inside2)

    def put3(n, fr, fb, br, bb):
        f3[0, n], f3[1, n] = fr, fb
        b3r[n + 1, 8:24], b3b[n + 1, 8:24] = br, bb

    restrict((b2r, b2b, v2r, v2b, c2r, c2b), tmp, index2, 16, 32, 64, put3)

    index3 = [side_rule(16, parity) for parity in range(2)]
    smooth_down(b3r, b3b, v3r, v3b, c3r, c3b, lambda p: (f3[0, p], f3[1, p]), index3, 0.25**3, 8, 16, None)

    def put4(n, fr, fb, br, bb):
        f4[0, n], f4[1, n] = fr, fb
        b4r[n + 1, 8:16], b4b[n + 1, 8:16] = br, bb

    restrict((b3r, b3b, v3r, v3b, c3r, c3b), tmp, index3, 8, 16, 32, put4)

    index4 = [side_rule(8, parity) for parity in range(2)]

    for p in range(4):
        make_coefs(b4r, b4b, f4[0, p], c4r, p, index4[p % 2], 0.25**4, 8)
        make_coefs(b4b, b4r, f4[1, p], c4b, p, index4[1 - p % 2], 0.25**4, 8)
    row8 = sublanes(8)
    inner = (row8 > 0, row8 < 7)
    cr4 = [[c4r[w, p] for w in range(7)] for p in range(4)]
    cb4 = [[c4b[w, p] for w in range(7)] for p in range(4)]
    for c in cr4 + cb4:
        c[2] = jnp.where(inner[0], c[2], 0.0)
        c[3] = jnp.where(inner[1], c[3], 0.0)

    def half(other, coefs, flip):
        out = []
        for p in range(4):
            c, v = coefs[p], other[p]
            w = c[6] + c[4] * v
            if p > 0:
                w = w + c[0] * other[p - 1]
            if p < 3:
                w = w + c[1] * other[p + 1]
            w = w + c[2] * pltpu.roll(v, 1, 0) + c[3] * pltpu.roll(v, 7, 0)
            out.append(w + c[5] * beside(v, index4[(p + flip) % 2]))
        return out

    def coarse_step(count, state):
        black = list(state)
        red = half(black, cr4, 0)
        return tuple(half(red, cb4, 1))

    black = lax.fori_loop(0, COARSE_ITERS - 1, coarse_step, (jnp.zeros((8, 128), F32),) * 4)
    red = half(black, cr4, 0)
    black = half(red, cb4, 1)
    for p in range(4):
        v4r[p + 1, 8:16] = red[p]
        v4b[p + 1, 8:16] = black[p]

    prolong(v4r, v4b, v3b, tmp, 4, 8)
    smooth_up(v3r, v3b, c3r, c3b, index3, 8, 16)
    prolong(v3r, v3b, v2b, tmp, 8, 16)
    smooth_up(v2r, v2b, c2r, c2b, index2, 16, 32)

    for c in copies[:3]:
        c.wait()
    lane, row = lanes(32), sublanes(32)
    near = lane % 64 - jnp.where(lane % 64 < 48, 0, 64)
    cell = gz * 32 + near
    valid = (cell >= 0) & (cell < 256)
    idx = jnp.clip(cell, 0, 255) // 2
    window = pl.multiple_of(jnp.clip(gy * 16 - 8, 0, 32), 8)
    for n in range(8):
        even = (row + lane + n) % 2 == 0
        parts = []
        for p in (n, n + 8):
            parts.append(jnp.where(even, pick(v2r[p + 1, 8:40], idx), pick(v2b[p + 1, 8:40], idx)))
        c = jnp.where(valid, jnp.where(lane < 64, parts[0], parts[1]), 0.0)
        double_rows(tmp, c, 32)
        for p in (2 * n, 2 * n + 1):
            v1b[p + 1, 8:40] += tmp[pl.ds(window, 32)]
    seam(v1b, 32)
    index1 = [side_index(32, parity, 64) for parity in range(2)]
    for _ in range(2):
        update(v1r, v1b, c1r, index1, 0, 16, 32, 0)
        seam(v1r, 32)
        update(v1b, v1r, c1b, index1, 0, 16, 32, 1)
        seam(v1b, 32)

    for c in copies[3:]:
        c.wait()
    start = pl.multiple_of(gy * 16 - window, 8)
    cell = lane - jnp.where(lane < 96, 0, 128)
    idx = (cell // 2) % 64
    for n in range(-3, 11):
        plane = gx * 8 + n
        held = jnp.clip(plane, 0, 31)
        at_half = idx + 64 * (held // 16)
        even = (row + lane + n) % 2 == 0
        red = v1r[held % 16 + 1, pl.ds(start, 32)]
        black = v1b[held % 16 + 1, pl.ds(start, 32)]
        c = jnp.where(even, pick(red, at_half), pick(black, at_half))
        c = c * jnp.where((plane >= 0) & (plane < 32), 1.0, 0.0).astype(F32)
        tmp[64:96] = c
        double_rows(tmp, tmp[68:92], 24)
        for p in (2 * n + 8, 2 * n + 9):
            v0b[p + 1, 8:56] += tmp[0:48]
    index0 = [side_rule(48, parity) for parity in range(2)]
    update(v0r, v0b, c0r, index0, 4, 28, 48, 0, 4)
    update(v0b, v0r, c0b, index0, 4, 28, 48, 1, 4)
    update(v0r, v0b, c0r, index0, 6, 26, 48, 0, 4)
    update(v0b, v0r, c0b, index0, 6, 26, 48, 1, 4)

    def finish(p, parity):
        even = (row + lane + parity) % 2 == 0
        er, eb = defect(v0r, v0b, c0r, c0b, p, parity, index1_0, 32, 8, 4)
        res_ref[p - 8] = jnp.where(even, pick(er, lane // 2), pick(eb, lane // 2))
        red, black = v0r[p + 1, 16:48], v0b[p + 1, 16:48]
        u_ref[p - 8] = jnp.where(even, pick(red, lane // 2), pick(black, lane // 2))

    index1_0 = [side_rule(32, parity) for parity in range(2)]
    pairs(8, 24, finish, 32)


def around(lo, hi, axis):
    count = lax.axis_size(axis)
    from_above = lax.ppermute(lo, axis, [((i + 1) % count, i) for i in range(count)])
    from_below = lax.ppermute(hi, axis, [(i, (i + 1) % count) for i in range(count)])
    return from_below, from_above


def beyond(x, axis):
    count = lax.axis_size(axis)
    return [lax.ppermute(x, axis, [(i, (i + d) % count) for i in range(count)]) for d in range(1, count)]


def body(source, conductance):
    vmem, smem, hbm = (pl.BlockSpec(memory_space=m) for m in (pltpu.VMEM, pltpu.SMEM, pltpu.HBM))
    at = jnp.stack([lax.axis_index(a) for a in ("gx", "gy", "gz")]).astype(jnp.int32)
    dma = pltpu.SemaphoreType.DMA

    block, x_slab = arr(16, 32, 128), arr(17, 32, 128)
    buffer = pltpu.VMEM((16, 32, 128), F32)
    wf, wb, lo, hi, b1 = call(
        split_fine,
        [(block, block, x_slab, x_slab, arr(64, 128))],
        (source, conductance),
        [hbm] * 2,
        [buffer, buffer, pltpu.VMEM((32, 128), F32), dma((2,))],
        8,
    )
    xl, xu = around(lo, hi, "gx")
    b1 = [b1] + beyond(b1, "gy")
    y_slab = arr(66, 8, 128)
    lo, hi, b1 = call(pack_rows, [(y_slab, y_slab, arr(4, 64, 128))], (wf, wb, xl, xu, *b1), limit=8)
    yl, yu = around(lo, hi, "gy")
    b1 = [b1] + beyond(b1, "gx")
    lo, hi = call(pack_lanes, [(arr(96, 8, 128),) * 2], (wf, wb, xl, xu, yl, yu), limit=8)
    zl, zu = around(lo, hi, "gz")

    colour0 = pltpu.VMEM((34, 64, 128), F32)
    right0 = pltpu.VMEM((32, 48, 128), F32)
    coef0 = pltpu.VMEM((8, 32, 48, 128), F32)
    state0 = (arr(8, 24, 48, 128), arr(8, 24, 48, 128), arr(34, 64, 128))
    g, c0r, c0b, v0b = call(
        fine_down,
        [(arr(16, 128, 128),) + state0, (vmem, hbm, hbm, hbm)],
        (at, wf, wb, xl, xu, yl, yu, zl, zu),
        [smem] + [vmem] * 8,
        [colour0, colour0, right0, right0, coef0, coef0, colour0, colour0, pltpu.VMEM((32, 128), F32), dma((3,))],
        LIMIT,
    )
    g = lax.all_to_all(g, ("gx", "gy"), 0, 0, tiled=True)

    state1 = (arr(2, 8, 16, 32, 128), arr(18, 32, 128))
    colour1 = pltpu.VMEM((18, 80, 128), F32)
    right1 = pltpu.VMEM((16, 64, 128), F32)
    coef1 = pltpu.VMEM((8, 16, 64, 128), F32)
    w2, c1, v1b = call(
        mid_down,
        [(arr(8, 32, 128),) + state1, (vmem, hbm, hbm)],
        (at, g, *b1),
        [smem] + [vmem] * 5,
        [colour1, colour1, right1, right1, coef1, coef1, colour1, colour1, pltpu.VMEM((64, 128), F32), dma((3,))],
        LIMIT_MID,
    )
    mine = [w2] + [lax.ppermute(w2, "gz", [(i, (i + d) % 8) for i in range(8)]) for d in (2, 4, 6)]
    pair = [lax.ppermute(w, "gz", [(i, i ^ 1) for i in range(8)]) for w in mine]

    scratch = []
    for planes, rows in ((16, 32), (8, 16), (4, 8)):
        scratch += level_scratch(planes, rows) + [pltpu.VMEM((2, planes, rows, 128), F32)]
    scratch += [pltpu.VMEM((18, 48, 128), F32)] * 2 + [pltpu.VMEM((8, 16, 32, 128), F32)] * 2
    scratch += [colour0] * 2 + [pltpu.VMEM((8, 24, 48, 128), F32)] * 2
    scratch += [pltpu.VMEM((96, 128), F32), dma((6,))]
    return call(
        coarse_up,
        [(block, block)],
        (at, *mine, *pair, c1, v1b, c0r, c0b, v0b),
        [smem] + [vmem] * 8 + [hbm] * 5,
        scratch,
        LIMIT_UP,
    )


def solution(mesh):
    placed = (P("gx", "gy", "gz"), P("gx", "gy", "gz"))
    return jax.shard_map(body, mesh=mesh, in_specs=placed, out_specs=placed, check_vma=False)
```

```python
import functools

import jax
import jax.numpy as jnp
from jax import lax
from jax.experimental import pallas as pl
from jax.experimental.pallas import tpu as pltpu
from jax.sharding import PartitionSpec as P

F32 = jnp.float32
COARSE_ITERS = 20
MIB = 1 << 20
GROUP = 64
LIMIT = 50
LIMIT_MID = 50
LIMIT_UP = 50


def lanes(rows):
    return lax.broadcasted_iota(jnp.int32, (rows, 128), 1)


def sublanes(rows):
    return lax.broadcasted_iota(jnp.int32, (rows, 128), 0)


def pick(x, idx):
    return jnp.take_along_axis(x, idx, axis=1, mode="promise_in_bounds")


def turn(x, shift):
    shift = shift % 128
    return pltpu.roll(x, shift, 1) if shift else x


def side_index(rows, parity, period):
    lane, row = lanes(rows), sublanes(rows)
    step = 2 * ((row + parity) % 2) - 1
    within = (lane % period + step + period) % period
    return lane - lane % period + within


def side_rule(rows, parity):
    return (sublanes(rows) + parity) % 2 == 0


def beside(x, rule):
    if rule.dtype == jnp.bool_:
        return jnp.where(rule, pltpu.roll(x, 1, 1), pltpu.roll(x, 127, 1))
    return pick(x, rule)


def call(kernel, out, args, specs=None, scratch=(), limit=40):
    vmem = pl.BlockSpec(memory_space=pltpu.VMEM)
    return pl.pallas_call(
        kernel,
        out_shape=out[0],
        in_specs=specs or [vmem] * len(args),
        out_specs=out[1] if len(out) > 1 else jax.tree.map(lambda _: vmem, out[0]),
        scratch_shapes=scratch,
        compiler_params=pltpu.CompilerParams(vmem_limit_bytes=limit * MIB),
        name=kernel.__name__,
    )(*args)


def arr(*shape):
    return jax.ShapeDtypeStruct(shape, F32)


def split_fine(f_in, b_in, wf_ref, wb_ref, lo_ref, hi_ref, b1_ref, f_ref, b_ref, tmp, sems):
    loads = [pltpu.make_async_copy(b_in, b_ref, sems.at[0]), pltpu.make_async_copy(f_in, f_ref, sems.at[1])]
    for c in loads:
        c.start()
    lane, row = lanes(32), sublanes(32)
    index = []
    for parity in range(2):
        odd = (row + parity) % 2
        index.append(2 * (lane % 64) + jnp.where(lane < 64, odd, 1 - odd))
    loads[0].wait()
    lane16, row16 = lanes(16), sublanes(16)
    own = []
    for n in range(8):
        w = [pick(b_ref[2 * n + parity], index[parity]) for parity in range(2)]
        for parity in range(2):
            i = 2 * n + parity
            wb_ref[i] = w[parity]
            if i < 9:
                lo_ref[8 + i] = w[parity]
            if i > 6:
                hi_ref[1 + i] = w[parity]
        both = w[0] + w[1]
        odd = (row16 + n) % 2
        cell = 2 * (lane16 % 32) + jnp.where(lane16 % 64 < 32, odd, 1 - odd)
        own.append(pick(halve_rows(tmp, both + turn(both, 64), 32), cell))
    for n in range(4):
        b1_ref[16 * n : 16 * n + 16] = jnp.where(lane16 < 64, own[n], own[n + 4])
    loads[1].wait()
    for i in range(16):
        wf = pick(f_ref[i], index[i % 2])
        wf_ref[i] = wf
        if i < 8:
            lo_ref[i] = wf
        else:
            hi_ref[i - 8] = wf


def by_colour(n, swap):
    lane, row = lanes(16), sublanes(16)
    odd = (row + n) % 2
    return (2 * (lane % 64) + jnp.where((lane < 64) != swap, odd, 1 - odd)) % 128


def spared(index):
    return (index + jnp.where(lanes(16) % 64 < 48, -12, 12)) % 128


def plane_f(wf, xl, xu, p):
    return xl.at[p] if p < 8 else wf.at[p - 8] if p < 24 else xu.at[p - 24]


def plane_b(wb, xl, xu, p):
    return xl.at[9 + p] if p < 8 else wb.at[p - 8] if p < 24 else xu.at[8 + p - 24]


def pack_rows(wf, wb, xl, xu, b0, b1, b2, b3, lo_ref, hi_ref, b1_ref):
    for back, b in enumerate((b0, b1, b2, b3)):
        b1_ref[back] = b[...]
    for p in range(32):
        f, b = plane_f(wf, xl, xu, p), plane_b(wb, xl, xu, p)
        lo_ref[p] = f[0:8]
        hi_ref[p] = f[24:32]
        lo_ref[32 + p] = b[0:8]
        hi_ref[32 + p] = b[24:32]
    for i in range(16):
        lo_ref[64 + i // 8, i % 8 : i % 8 + 1] = wb[i, 8:9]
        hi_ref[64 + i // 8, i % 8 : i % 8 + 1] = wb[i, 23:24]


def slab(plane, yl, yu, which, p):
    return jnp.concatenate([yl[32 * which + p], plane[...], yu[32 * which + p]], axis=0)


def pack_lanes(wf, wb, xl, xu, yl, yu, lo_ref, hi_ref):
    slot_of = lanes(48) % 64
    for which, width, base in ((0, 16, 0), (1, 16, 48)):
        count = 64 // width
        slot = slot_of // width
        for group in range(32 // count):
            for s in range(count):
                p = group * count + s
                plane = plane_b(wb, xl, xu, p) if which else plane_f(wf, xl, xu, p)
                v = turn(slab(plane, yl, yu, which, p), width * s)
                if s == 0:
                    low = high = v
                else:
                    low = jnp.where(slot == s, v, low)
                    high = jnp.where(slot == s - 1, v, high)
            start = base + 6 * group
            lo_ref[start : start + 6] = low.reshape(6, 8, 128)
            hi_ref[start : start + 6] = high.reshape(6, 8, 128)


def make_coefs(mine, other, f, coef, p, index, scale, rows, inside=None):
    r = slice(8, 8 + rows)
    centre = mine[p + 1, r]
    mid = other[p + 1, r]
    side = beside(mid, index)
    if inside is not None:
        side = jnp.where(inside, side, 0.0)
    others = (other[p, r], other[p + 2, r], other[p + 1, 7 : 7 + rows], other[p + 1, 9 : 9 + rows], mid, side)
    weights = [centre + b for b in others]
    total = weights[0]
    for w in weights[1:]:
        total = total + w
    inverse = jnp.where(centre > 0.0, 1.0 / jnp.where(centre > 0.0, total, 1.0), 0.0)
    for which in range(6):
        w = weights[which] * inverse
        if which == 5 and inside is not None:
            w = jnp.where(inside, w, 0.0)
        coef[which, p] = w
    coef[6, p] = f * (inverse * (2.0 / scale))
    coef[7, p] = total * (0.5 * scale)


def relaxed(other, coef, p, index, rows, first=0, shift=0):
    a = 8 + first
    r = slice(a, a + rows)
    c = slice(first, first + rows)
    q = p - shift
    mid = other[p + 1, r]
    out = coef[6, q, c] + coef[0, q, c] * other[p, r]
    out = out + coef[1, q, c] * other[p + 2, r]
    out = out + coef[2, q, c] * other[p + 1, a - 1 : a - 1 + rows]
    out = out + coef[3, q, c] * other[p + 1, a + 1 : a + 1 + rows]
    out = out + coef[4, q, c] * mid
    return out + coef[5, q, c] * beside(mid, index)


def pairs(start, stop, body, rows):
    count = stop - start
    most = 8 * GROUP if rows < 64 else 16 * GROUP
    width = max(w for w in (2, 4, 8, 16) if w == 2 or (count % w == 0 and w * rows <= most))

    def step(t, carry):
        for n in range(width):
            body(start + t * width + n, n % 2)
        return carry

    if count == width:
        step(0, 0)
    else:
        lax.fori_loop(0, count // width, step, 0)


def update(mine, other, coef, index, start, stop, rows, flip, shift=0):
    def body(p, parity):
        mine[p + 1, 8 : 8 + rows] = relaxed(other, coef, p, index[(parity + flip) % 2], rows, 0, shift)

    pairs(start, stop, body, rows)


def defect(red, black, cr, cb, p, parity, index, rows, first=0, shift=0):
    r = slice(8 + first, 8 + first + rows)
    c = slice(first, first + rows)
    er = cr[7, p - shift, c] * (relaxed(black, cr, p, index[parity], rows, first, shift) - red[p + 1, r])
    eb = cb[7, p - shift, c] * (relaxed(red, cb, p, index[1 - parity], rows, first, shift) - black[p + 1, r])
    return er, eb


def halve_rows(tmp, value, rows):
    tmp[0:rows] = value
    return 0.125 * (tmp[pl.ds(0, rows // 2, 2)] + tmp[pl.ds(1, rows // 2, 2)])


def double_rows(tmp, value, rows):
    tmp[pl.ds(0, rows, 2)] = value
    tmp[pl.ds(1, rows, 2)] = value


def fine_down(
    at, wf, wb, xl, xu, yl, yu, zl, zu, g_ref, cr_out, cb_out, br, bb, fr, fb, cr, cb, vr, vb, tmp, sems
):
    gx, gy, gz = at[0], at[1], at[2]
    lane, row = lanes(48), sublanes(48)
    own = lane < 64
    keep = own | ((lane < 96) & (gz < 7)) | ((lane >= 96) & (gz > 0))
    keep = keep & ((row >= 8) | (gy > 0)) & ((row < 40) | (gy < 3))
    kept = jnp.where(keep, 1.0, 0.0).astype(F32)
    below = jnp.where(gx > 0, 1.0, 0.0).astype(F32)
    above = jnp.where(gx < 3, 1.0, 0.0).astype(F32)
    left = jnp.where(gy > 0, 1.0, 0.0).astype(F32)
    right = jnp.where(gy < 3, 1.0, 0.0).astype(F32)
    vr[...] = jnp.zeros_like(vr)
    vb[...] = jnp.zeros_like(vb)
    edge = jnp.zeros((8, 128), F32)
    for b in (br, bb):
        for q in range(34):
            b[q, 0:8] = edge
            b[q, 56:64] = edge
        for q in (0, 33):
            b[q, 8:56] = jnp.zeros((48, 128), F32)
    for which, width, base in ((0, 16, 0), (1, 16, 48)):
        count = 64 // width
        slot = (lane % 64) // width
        for p in range(32):
            plane = plane_b(wb, xl, xu, p) if which else plane_f(wf, xl, xu, p)
            w = slab(plane, yl, yu, which, p)
            s = p % count
            start = base + 6 * (p // count)
            up = zu[start : start + 6].reshape(48, 128)
            low = zl[start : start + 6].reshape(48, 128)
            both = jnp.where(slot == s, up, low)
            red = jnp.where(own, w, turn(both, 64 - width * s))
            black = jnp.where(own, turn(w, 64), turn(both, -width * s))
            if which:
                k = kept * below if p < 8 else kept * above if p >= 24 else kept
                br[p + 1, 8:56] = red * k
                bb[p + 1, 8:56] = black * k
            else:
                fr[p] = red
                fb[p] = black
    for a in range(2):
        for src, r, ok in ((yl, 7, left), (yu, 56, right)):
            v = src[64 + a] * ok
            t = turn(v, 64)
            for s in range(8):
                br[9 + 8 * a + s, r : r + 1] = v[s : s + 1]
                bb[9 + 8 * a + s, r : r + 1] = t[s : s + 1]
    for v, q in ((xl[8] * below, 0), (xu[16] * above, 33)):
        br[q, 16:48] = v
        bb[q, 16:48] = turn(v, 64)

    index = [side_rule(48, parity) for parity in range(2)]

    def coefs(p, parity):
        make_coefs(br, bb, fr[p], cr, p, index[parity], 1.0, 48)
        make_coefs(bb, br, fb[p], cb, p, index[1 - parity], 1.0, 48)
        vr[p + 1, 8:56] = cr[6, p]

    pairs(0, 32, coefs, 48)
    copies = [
        pltpu.make_async_copy(cr.at[:, pl.ds(4, 24)], cr_out, sems.at[0]),
        pltpu.make_async_copy(cb.at[:, pl.ds(3, 26)], cb_out.at[pl.ds(0, 8)], sems.at[1]),
        pltpu.make_async_copy(vb.at[pl.ds(4, 26), pl.ds(8, 48)], cb_out.at[8], sems.at[2]),
    ]
    copies[0].start()
    copies[1].start()
    update(vb, vr, cb, index, 0, 32, 48, 1)
    update(vr, vb, cr, index, 2, 30, 48, 0)
    update(vb, vr, cb, index, 2, 30, 48, 1)
    copies[2].start()
    inner = [side_rule(32, parity) for parity in range(2)]
    swap = gx >= 2
    lane16 = lanes(16)
    spare = (lane16 % 64 >= 38) & (lane16 % 64 < 58)
    for n in range(8):
        total = coarse = None
        for parity in range(2):
            p = 8 + 2 * n + parity
            er, eb = defect(vr, vb, cr, cb, p, parity, inner, 32, 8)
            b = br[p + 1, 16:48] + bb[p + 1, 16:48]
            total = er + eb if total is None else total + (er + eb)
            coarse = b if coarse is None else coarse + b
        f1 = pick(halve_rows(tmp, total, 32), by_colour(n, swap))
        b1 = halve_rows(tmp, coarse, 32)
        w1 = jnp.where(spare, pick(b1, spared(by_colour(n, swap))), f1)
        for copy in range(16):
            g_ref[copy, 16 * n : 16 * n + 16] = w1
    for c in copies:
        c.wait()


def across(g, a, start):
    r = slice(start, start + 16)
    return jnp.concatenate([g[4 * a + y, r] for y in range(4)], axis=0)


def joined_f(g, p):
    wa, wb = (across(g, p // 8 + up, 16 * (p % 8)) for up in (0, 2))
    half = lanes(64) < 64
    return jnp.where(half, wa, wb), turn(jnp.where(half, wb, wa), 64)


def across_b(gx, gy, held, a, n):
    back = (gx - a + 4) % 4
    r = slice(16 * n, 16 * n + 16)
    out = []
    for y in range(4):
        e = (gy - y + 4) % 4
        v = held[0][e, r]
        for d in range(1, 4):
            v = jnp.where(back == d, held[d][e, r], v)
        out.append(v)
    return jnp.concatenate(out, axis=0)


def joined_b(gx, gy, held, a, n):
    wa, wb = (across_b(gx, gy, held, a + up, n) for up in (0, 2))
    half = lanes(64) < 64
    reds = jnp.where(half, wa, turn(wb, 64)), jnp.where(half, turn(wa, 64), wb)
    return [(red, turn(red, -32)) for red in reds]


def seam(v, rows):
    r = slice(8, 8 + rows)
    half = lanes(rows) < 64
    v[0, r] = jnp.where(half, 0.0, turn(v[16, r], 64))
    v[17, r] = jnp.where(half, turn(v[1, r], 64), 0.0)


def mid_down(at, g, h0, h1, h2, h3, w2_ref, c_out, vb_out, br, bb, fr, fb, cr, cb, vr, vb, tmp, sems):
    gx, gy, gz = at[0], at[1], at[2]
    lane = lanes(64)
    own = lane % 64 < 32
    keep = own | ((lane % 64 < 48) & (gz < 7)) | ((lane % 64 >= 48) & (gz > 0))
    kept = jnp.where(keep, 1.0, 0.0).astype(F32)
    halo = (lane + jnp.where(lane % 64 < 48, 6, -6)) % 128
    for v in (vr, vb):
        v[...] = jnp.zeros_like(v)
    for b in (br, bb):
        b[:, 0:8] = jnp.zeros((18, 8, 128), F32)
        b[:, 72:80] = jnp.zeros((18, 8, 128), F32)
    for p in range(16):
        fr[p], fb[p] = joined_f(g, p)
    for a in range(2):
        for n in range(4):
            for up, (red, black) in enumerate(joined_b(gx, gy, (h0, h1, h2, h3), a, n)):
                p = 8 * a + n + 4 * up
                br[p + 1, 8:72] = kept * jnp.where(own, red, pick(fr[p], halo))
                bb[p + 1, 8:72] = kept * jnp.where(own, black, pick(fb[p], halo))
    seam(br, 64)
    seam(bb, 64)
    index = [side_index(64, parity, 64) for parity in range(2)]

    def coefs(p, parity):
        make_coefs(br, bb, fr[p], cr, p, index[parity], 0.25, 64)
        make_coefs(bb, br, fb[p], cb, p, index[1 - parity], 0.25, 64)
        vr[p + 1, 8:72] = cr[6, p]

    pairs(0, 16, coefs, 64)
    seam(vr, 64)
    window = pl.multiple_of(jnp.clip(gy * 16 - 8, 0, 32), 8)
    copies = [
        pltpu.make_async_copy(cr.at[:, :, pl.ds(window, 32)], c_out.at[0], sems.at[0]),
        pltpu.make_async_copy(cb.at[:, :, pl.ds(window, 32)], c_out.at[1], sems.at[1]),
        pltpu.make_async_copy(vb.at[:, pl.ds(window + 8, 32)], vb_out, sems.at[2]),
    ]
    copies[0].start()
    copies[1].start()
    update(vb, vr, cb, index, 0, 16, 64, 1)
    seam(vb, 64)
    update(vr, vb, cr, index, 0, 16, 64, 0)
    seam(vr, 64)
    update(vb, vr, cb, index, 0, 16, 64, 1)
    seam(vb, 64)
    copies[2].start()
    lane, row = lanes(32), sublanes(32)
    for n in range(8):
        total = coarse = None
        for parity in range(2):
            p = 2 * n + parity
            er, eb = defect(vr, vb, cr, cb, p, parity, index, 64)
            e = er + eb
            b = br[p + 1, 8:72] + bb[p + 1, 8:72]
            total = e if total is None else total + e
            coarse = b if coarse is None else coarse + b
        f2 = halve_rows(tmp, total, 64)
        b2 = halve_rows(tmp, coarse, 64)
        odd = (row + n) % 2
        idx = 64 * ((lane % 64) // 32) + 2 * (lane % 16) + jnp.where(lane % 32 < 16, odd, 1 - odd)
        w2 = jnp.where(lane < 64, pick(f2, idx), pick(b2, idx))
        w2_ref[n] = w2
    for c in copies:
        c.wait()


def transposed(blocks):
    slot = lanes(32) // 16
    for bit in (1, 2, 4):
        out = list(blocks)
        for i in range(8):
            if not i & bit:
                x, y = blocks[i], blocks[i + bit]
                out[i] = jnp.where(slot & bit == 0, x, turn(y, 16 * bit))
                out[i + bit] = jnp.where(slot & bit == 0, turn(x, -16 * bit), y)
        blocks = out
    return blocks


def level_scratch(planes, rows):
    return [pltpu.VMEM((planes + 2, rows + 16, 128), F32)] * 4 + [pltpu.VMEM((8, planes, rows, 128), F32)] * 2


def clear(refs):
    for v in refs:
        v[...] = jnp.zeros_like(v)


def smooth_down(br, bb, vr, vb, cr, cb, f_of, index, scale, planes, rows, inside):
    def coefs(p, parity):
        fr, fb = f_of(p)
        make_coefs(br, bb, fr, cr, p, index[parity], scale, rows, inside and inside[parity])
        make_coefs(bb, br, fb, cb, p, index[1 - parity], scale, rows, inside and inside[1 - parity])
        vr[p + 1, 8 : 8 + rows] = cr[6, p]

    pairs(0, planes, coefs, rows)
    update(vb, vr, cb, index, 0, planes, rows, 1)
    update(vr, vb, cr, index, 0, planes, rows, 0)
    update(vb, vr, cb, index, 0, planes, rows, 1)


def smooth_up(vr, vb, cr, cb, index, planes, rows):
    for _ in range(2):
        update(vr, vb, cr, index, 0, planes, rows, 0)
        update(vb, vr, cb, index, 0, planes, rows, 1)


def restrict(level, tmp, index, planes, rows, cells, put):
    br, bb, vr, vb, cr, cb = level
    lane, row = lanes(rows // 2), sublanes(rows // 2)
    for n in range(planes // 2):
        total = coarse = None
        for parity in range(2):
            p = 2 * n + parity
            er, eb = defect(vr, vb, cr, cb, p, parity, index, rows)
            b = br[p + 1, 8 : 8 + rows] + bb[p + 1, 8 : 8 + rows]
            total = er + eb if total is None else total + (er + eb)
            coarse = b if coarse is None else coarse + b
        f = halve_rows(tmp, total, rows)
        b = halve_rows(tmp, coarse, rows)
        odd = (row + n) % 2
        red = 2 * (lane % 64) + odd
        black = 2 * (lane % 64) + 1 - odd
        inside = lane < cells
        put(n, *[jnp.where(inside, pick(x, i), 0.0) for x in (f, b) for i in (red, black)])


def prolong(vr, vb, out, tmp, planes, rows):
    lane, row = lanes(rows), sublanes(rows)
    r = slice(8, 8 + rows)
    for n in range(planes):
        even = (row + lane + n) % 2 == 0
        c = jnp.where(even, pick(vr[n + 1, r], lane // 2), pick(vb[n + 1, r], lane // 2))
        double_rows(tmp, c, rows)
        for p in (2 * n, 2 * n + 1):
            out[p + 1, 8 : 8 + 2 * rows] += tmp[0 : 2 * rows]


def coarse_up(
    at, m0, m1, m2, m3, q0, q1, q2, q3, c1_in, v1b_in, c0r_in, c0b_in, u_ref, res_ref,
    b2r, b2b, v2r, v2b, c2r, c2b, f2,
    b3r, b3b, v3r, v3b, c3r, c3b, f3,
    b4r, b4b, v4r, v4b, c4r, c4b, f4,
    v1r, v1b, c1r, c1b, v0r, v0b, c0r, c0b, tmp, sems,
):
    gx, gy, gz = at[0], at[1], at[2]
    copies = [
        pltpu.make_async_copy(c1_in.at[0], c1r, sems.at[0]),
        pltpu.make_async_copy(c1_in.at[1], c1b, sems.at[1]),
        pltpu.make_async_copy(v1b_in, v1b.at[:, pl.ds(8, 32)], sems.at[2]),
        pltpu.make_async_copy(c0r_in, c0r, sems.at[3]),
        pltpu.make_async_copy(c0b_in.at[pl.ds(0, 8), pl.ds(1, 24)], c0b, sems.at[4]),
        pltpu.make_async_copy(c0b_in.at[8], v0b.at[pl.ds(4, 26), pl.ds(8, 48)], sems.at[5]),
    ]
    for c in copies:
        c.start()
    clear((b2r, b2b, v2r, v2b, b3r, b3b, v3r, v3b, b4r, b4b, v4r, v4b, v1r, v0r))
    v0b[:, 0:8] = jnp.zeros((34, 8, 128), F32)
    v0b[:, 56:64] = jnp.zeros((34, 8, 128), F32)
    v1b[:, 0:8] = jnp.zeros((18, 8, 128), F32)
    v1b[:, 40:48] = jnp.zeros((18, 8, 128), F32)

    chip = gz // 2
    first = gz % 2 == 0
    for n in range(8):
        near = [(jnp.where(first, a[n], b[n]), jnp.where(first, b[n], a[n])) for a, b in ((m0, q0), (m1, q1), (m2, q2), (m3, q3))]
        blocks = []
        for c in range(4):
            for core in range(2):
                v = near[0][core]
                for back in range(1, 4):
                    v = jnp.where(chip == (c + back) % 4, near[back][core], v)
                blocks.append(v)
        out = transposed(blocks)
        for h in range(2):
            p = n + 8 * h
            f2[0, p] = out[2 * h]
            f2[1, p] = out[2 * h + 1]
            b2r[p + 1, 8:40] = out[4 + 2 * h]
            b2b[p + 1, 8:40] = out[5 + 2 * h]
    lane = lanes(32)
    index2 = [side_rule(32, parity) for parity in range(2)]
    inside2 = [lane != jnp.where(index2[parity], 0, 127) for parity in range(2)]
    smooth_down(b2r, b2b, v2r, v2b, c2r, c2b, lambda p: (f2[0, p], f2[1, p]), index2, 0.25**2, 16, 32, inside2)

    def put3(n, fr, fb, br, bb):
        f3[0, n], f3[1, n] = fr, fb
        b3r[n + 1, 8:24], b3b[n + 1, 8:24] = br, bb

    restrict((b2r, b2b, v2r, v2b, c2r, c2b), tmp, index2, 16, 32, 64, put3)

    index3 = [side_rule(16, parity) for parity in range(2)]
    smooth_down(b3r, b3b, v3r, v3b, c3r, c3b, lambda p: (f3[0, p], f3[1, p]), index3, 0.25**3, 8, 16, None)

    def put4(n, fr, fb, br, bb):
        f4[0, n], f4[1, n] = fr, fb
        b4r[n + 1, 8:16], b4b[n + 1, 8:16] = br, bb

    restrict((b3r, b3b, v3r, v3b, c3r, c3b), tmp, index3, 8, 16, 32, put4)

    index4 = [side_rule(8, parity) for parity in range(2)]

    for p in range(4):
        make_coefs(b4r, b4b, f4[0, p], c4r, p, index4[p % 2], 0.25**4, 8)
        make_coefs(b4b, b4r, f4[1, p], c4b, p, index4[1 - p % 2], 0.25**4, 8)
    row8 = sublanes(8)
    inner = (row8 > 0, row8 < 7)
    cr4 = [[c4r[w, p] for w in range(7)] for p in range(4)]
    cb4 = [[c4b[w, p] for w in range(7)] for p in range(4)]
    for c in cr4 + cb4:
        c[2] = jnp.where(inner[0], c[2], 0.0)
        c[3] = jnp.where(inner[1], c[3], 0.0)

    def half(other, coefs, flip):
        out = []
        for p in range(4):
            c, v = coefs[p], other[p]
            w = c[6] + c[4] * v
            if p > 0:
                w = w + c[0] * other[p - 1]
            if p < 3:
                w = w + c[1] * other[p + 1]
            w = w + c[2] * pltpu.roll(v, 1, 0) + c[3] * pltpu.roll(v, 7, 0)
            out.append(w + c[5] * beside(v, index4[(p + flip) % 2]))
        return out

    def coarse_step(count, state):
        black = list(state)
        red = half(black, cr4, 0)
        return tuple(half(red, cb4, 1))

    black = lax.fori_loop(0, COARSE_ITERS - 1, coarse_step, (jnp.zeros((8, 128), F32),) * 4)
    red = half(black, cr4, 0)
    black = half(red, cb4, 1)
    for p in range(4):
        v4r[p + 1, 8:16] = red[p]
        v4b[p + 1, 8:16] = black[p]

    prolong(v4r, v4b, v3b, tmp, 4, 8)
    smooth_up(v3r, v3b, c3r, c3b, index3, 8, 16)
    prolong(v3r, v3b, v2b, tmp, 8, 16)
    smooth_up(v2r, v2b, c2r, c2b, index2, 16, 32)

    for c in copies[:3]:
        c.wait()
    lane, row = lanes(32), sublanes(32)
    near = lane % 64 - jnp.where(lane % 64 < 48, 0, 64)
    cell = gz * 32 + near
    valid = (cell >= 0) & (cell < 256)
    idx = jnp.clip(cell, 0, 255) // 2
    window = pl.multiple_of(jnp.clip(gy * 16 - 8, 0, 32), 8)
    for n in range(8):
        even = (row + lane + n) % 2 == 0
        parts = []
        for p in (n, n + 8):
            parts.append(jnp.where(even, pick(v2r[p + 1, 8:40], idx), pick(v2b[p + 1, 8:40], idx)))
        c = jnp.where(valid, jnp.where(lane < 64, parts[0], parts[1]), 0.0)
        double_rows(tmp, c, 32)
        for p in (2 * n, 2 * n + 1):
            v1b[p + 1, 8:40] += tmp[pl.ds(window, 32)]
    seam(v1b, 32)
    index1 = [side_index(32, parity, 64) for parity in range(2)]
    for _ in range(2):
        update(v1r, v1b, c1r, index1, 0, 16, 32, 0)
        seam(v1r, 32)
        update(v1b, v1r, c1b, index1, 0, 16, 32, 1)
        seam(v1b, 32)

    for c in copies[3:]:
        c.wait()
    start = pl.multiple_of(gy * 16 - window, 8)
    cell = lane - jnp.where(lane < 96, 0, 128)
    idx = (cell // 2) % 64
    for n in range(-3, 11):
        plane = gx * 8 + n
        held = jnp.clip(plane, 0, 31)
        at_half = idx + 64 * (held // 16)
        even = (row + lane + n) % 2 == 0
        red = v1r[held % 16 + 1, pl.ds(start, 32)]
        black = v1b[held % 16 + 1, pl.ds(start, 32)]
        c = jnp.where(even, pick(red, at_half), pick(black, at_half))
        c = c * jnp.where((plane >= 0) & (plane < 32), 1.0, 0.0).astype(F32)
        tmp[64:96] = c
        double_rows(tmp, tmp[68:92], 24)
        for p in (2 * n + 8, 2 * n + 9):
            v0b[p + 1, 8:56] += tmp[0:48]
    index0 = [side_rule(48, parity) for parity in range(2)]
    update(v0r, v0b, c0r, index0, 4, 28, 48, 0, 4)
    update(v0b, v0r, c0b, index0, 4, 28, 48, 1, 4)
    update(v0r, v0b, c0r, index0, 6, 26, 48, 0, 4)
    update(v0b, v0r, c0b, index0, 6, 26, 48, 1, 4)

    def finish(p, parity):
        even = (row + lane + parity) % 2 == 0
        er, eb = defect(v0r, v0b, c0r, c0b, p, parity, index1_0, 32, 8, 4)
        res_ref[p - 8] = jnp.where(even, pick(er, lane // 2), pick(eb, lane // 2))
        red, black = v0r[p + 1, 16:48], v0b[p + 1, 16:48]
        u_ref[p - 8] = jnp.where(even, pick(red, lane // 2), pick(black, lane // 2))

    index1_0 = [side_rule(32, parity) for parity in range(2)]
    pairs(8, 24, finish, 32)


def around(lo, hi, axis):
    count = lax.axis_size(axis)
    from_above = lax.ppermute(lo, axis, [((i + 1) % count, i) for i in range(count)])
    from_below = lax.ppermute(hi, axis, [(i, (i + 1) % count) for i in range(count)])
    return from_below, from_above


def beyond(x, axis):
    count = lax.axis_size(axis)
    return [lax.ppermute(x, axis, [(i, (i + d) % count) for i in range(count)]) for d in range(1, count)]


def body(source, conductance):
    vmem, smem, hbm = (pl.BlockSpec(memory_space=m) for m in (pltpu.VMEM, pltpu.SMEM, pltpu.HBM))
    at = jnp.stack([lax.axis_index(a) for a in ("gx", "gy", "gz")]).astype(jnp.int32)
    dma = pltpu.SemaphoreType.DMA

    block, x_slab = arr(16, 32, 128), arr(17, 32, 128)
    buffer = pltpu.VMEM((16, 32, 128), F32)
    wf, wb, lo, hi, b1 = call(
        split_fine,
        [(block, block, x_slab, x_slab, arr(64, 128))],
        (source, conductance),
        [hbm] * 2,
        [buffer, buffer, pltpu.VMEM((32, 128), F32), dma((2,))],
        8,
    )
    xl, xu = around(lo, hi, "gx")
    b1 = [b1] + beyond(b1, "gy")
    y_slab = arr(66, 8, 128)
    lo, hi, b1 = call(pack_rows, [(y_slab, y_slab, arr(4, 64, 128))], (wf, wb, xl, xu, *b1), limit=8)
    yl, yu = around(lo, hi, "gy")
    b1 = [b1] + beyond(b1, "gx")
    lo, hi = call(pack_lanes, [(arr(96, 8, 128),) * 2], (wf, wb, xl, xu, yl, yu), limit=8)
    zl, zu = around(lo, hi, "gz")

    zl, zu, *b1 = lax.optimization_barrier((zl, zu, *b1))

    colour0 = pltpu.VMEM((34, 64, 128), F32)
    right0 = pltpu.VMEM((32, 48, 128), F32)
    coef0 = pltpu.VMEM((8, 32, 48, 128), F32)
    state0 = (arr(8, 24, 48, 128), arr(9, 26, 48, 128))
    g, c0r, c0b = call(
        fine_down,
        [(arr(16, 128, 128),) + state0, (vmem, hbm, hbm)],
        (at, wf, wb, xl, xu, yl, yu, zl, zu),
        [smem] + [vmem] * 8,
        [colour0, colour0, right0, right0, coef0, coef0, colour0, colour0, pltpu.VMEM((32, 128), F32), dma((3,))],
        LIMIT,
    )
    g = lax.all_to_all(g, ("gx", "gy"), 0, 0, tiled=True)

    state1 = (arr(2, 8, 16, 32, 128), arr(18, 32, 128))
    colour1 = pltpu.VMEM((18, 80, 128), F32)
    right1 = pltpu.VMEM((16, 64, 128), F32)
    coef1 = pltpu.VMEM((8, 16, 64, 128), F32)
    w2, c1, v1b = call(
        mid_down,
        [(arr(8, 32, 128),) + state1, (vmem, hbm, hbm)],
        (at, g, *b1),
        [smem] + [vmem] * 5,
        [colour1, colour1, right1, right1, coef1, coef1, colour1, colour1, pltpu.VMEM((64, 128), F32), dma((3,))],
        LIMIT_MID,
    )
    mine = [w2] + [lax.ppermute(w2, "gz", [(i, (i + d) % 8) for i in range(8)]) for d in (2, 4, 6)]
    pair = [lax.ppermute(w, "gz", [(i, i ^ 1) for i in range(8)]) for w in mine]

    scratch = []
    for planes, rows in ((16, 32), (8, 16), (4, 8)):
        scratch += level_scratch(planes, rows) + [pltpu.VMEM((2, planes, rows, 128), F32)]
    scratch += [pltpu.VMEM((18, 48, 128), F32)] * 2 + [pltpu.VMEM((8, 16, 32, 128), F32)] * 2
    scratch += [colour0] * 2 + [pltpu.VMEM((8, 24, 48, 128), F32)] * 2
    scratch += [pltpu.VMEM((96, 128), F32), dma((6,))]
    return call(
        coarse_up,
        [(block, block)],
        (at, *mine, *pair, c1, v1b, c0r, c0b),
        [smem] + [vmem] * 8 + [hbm] * 4,
        scratch,
        LIMIT_UP,
    )


def solution(mesh):
    placed = (P("gx", "gy", "gz"), P("gx", "gy", "gz"))
    return jax.shard_map(body, mesh=mesh, in_specs=placed, out_specs=placed, check_vma=False)
```

```python
import functools

import jax
import jax.numpy as jnp
from jax import lax
from jax.experimental import pallas as pl
from jax.experimental.pallas import tpu as pltpu
from jax.sharding import PartitionSpec as P

F32 = jnp.float32
COARSE_ITERS = 20
MIB = 1 << 20
GROUP = 64
LIMIT_FINE = 50
LIMIT_MID = 50
LIMIT_UP = 50


def lanes(rows):
    return lax.broadcasted_iota(jnp.int32, (rows, 128), 1)


def sublanes(rows):
    return lax.broadcasted_iota(jnp.int32, (rows, 128), 0)


def pick(x, idx):
    return jnp.take_along_axis(x, idx, axis=1, mode="promise_in_bounds")


def turn(x, shift):
    shift = shift % 128
    return pltpu.roll(x, shift, 1) if shift else x


def side_index(rows, parity, period):
    lane, row = lanes(rows), sublanes(rows)
    step = 2 * ((row + parity) % 2) - 1
    within = (lane % period + step + period) % period
    return lane - lane % period + within


def side_rule(rows, parity):
    return (sublanes(rows) + parity) % 2 == 0


def beside(x, rule):
    if rule.dtype == jnp.bool_:
        return jnp.where(rule, pltpu.roll(x, 1, 1), pltpu.roll(x, 127, 1))
    return pick(x, rule)


def call(kernel, out, args, specs=None, scratch=(), limit=40):
    vmem = pl.BlockSpec(memory_space=pltpu.VMEM)
    return pl.pallas_call(
        kernel,
        out_shape=out[0],
        in_specs=specs or [vmem] * len(args),
        out_specs=out[1] if len(out) > 1 else jax.tree.map(lambda _: vmem, out[0]),
        scratch_shapes=scratch,
        compiler_params=pltpu.CompilerParams(vmem_limit_bytes=limit * MIB),
        name=kernel.__name__,
    )(*args)


def arr(*shape):
    return jax.ShapeDtypeStruct(shape, F32)


def split_fine(both_ref, wf_ref, wb_ref, lo_ref, hi_ref, b1_ref, tmp):
    lane, row = lanes(32), sublanes(32)
    index = []
    for parity in range(2):
        odd = (row + parity) % 2
        index.append(2 * (lane % 64) + jnp.where(lane < 64, odd, 1 - odd))
    lane16, row16 = lanes(16), sublanes(16)
    own = []
    for n in range(8):
        w = [pick(both_ref[16 + 2 * n + parity], index[parity]) for parity in range(2)]
        for parity in range(2):
            i = 2 * n + parity
            wb_ref[i] = w[parity]
            if i < 9:
                lo_ref[8 + i] = w[parity]
            if i > 6:
                hi_ref[1 + i] = w[parity]
        both = w[0] + w[1]
        odd = (row16 + n) % 2
        cell = 2 * (lane16 % 32) + jnp.where(lane16 % 64 < 32, odd, 1 - odd)
        own.append(pick(halve_rows(tmp, both + turn(both, 64), 32), cell))
    for n in range(4):
        b1_ref[16 * n : 16 * n + 16] = jnp.where(lane16 < 64, own[n], own[n + 4])
    for i in range(16):
        wf = pick(both_ref[i], index[i % 2])
        wf_ref[i] = wf
        if i < 8:
            lo_ref[i] = wf
        else:
            hi_ref[i - 8] = wf


def by_colour(n, swap):
    lane, row = lanes(16), sublanes(16)
    odd = (row + n) % 2
    return (2 * (lane % 64) + jnp.where((lane < 64) != swap, odd, 1 - odd)) % 128


def spared(index):
    return (index + jnp.where(lanes(16) % 64 < 48, -12, 12)) % 128


def plane_f(wf, xl, xu, p):
    return xl.at[p] if p < 8 else wf.at[p - 8] if p < 24 else xu.at[p - 24]


def plane_b(wb, xl, xu, p):
    return xl.at[9 + p] if p < 8 else wb.at[p - 8] if p < 24 else xu.at[8 + p - 24]


def pack_rows(wf, wb, xl, xu, b0, b1, b2, b3, lo_ref, hi_ref, b1_ref):
    for back, b in enumerate((b0, b1, b2, b3)):
        b1_ref[back] = b[...]
    for p in range(32):
        f, b = plane_f(wf, xl, xu, p), plane_b(wb, xl, xu, p)
        lo_ref[p] = f[0:8]
        hi_ref[p] = f[24:32]
        lo_ref[32 + p] = b[0:8]
        hi_ref[32 + p] = b[24:32]
    for i in range(16):
        lo_ref[64 + i // 8, i % 8 : i % 8 + 1] = wb[i, 8:9]
        hi_ref[64 + i // 8, i % 8 : i % 8 + 1] = wb[i, 23:24]


def slab(plane, yl, yu, which, p):
    return jnp.concatenate([yl[32 * which + p], plane[...], yu[32 * which + p]], axis=0)


def pack_lanes(wf, wb, xl, xu, yl, yu, lo_ref, hi_ref):
    slot_of = lanes(48) % 64
    for which, width, base in ((0, 16, 0), (1, 16, 48)):
        count = 64 // width
        slot = slot_of // width
        for group in range(32 // count):
            for s in range(count):
                p = group * count + s
                plane = plane_b(wb, xl, xu, p) if which else plane_f(wf, xl, xu, p)
                v = turn(slab(plane, yl, yu, which, p), width * s)
                if s == 0:
                    low = high = v
                else:
                    low = jnp.where(slot == s, v, low)
                    high = jnp.where(slot == s - 1, v, high)
            start = base + 6 * group
            lo_ref[start : start + 6] = low.reshape(6, 8, 128)
            hi_ref[start : start + 6] = high.reshape(6, 8, 128)


def make_coefs(mine, other, f, coef, p, index, scale, rows, inside=None):
    r = slice(8, 8 + rows)
    centre = mine[p + 1, r]
    mid = other[p + 1, r]
    side = beside(mid, index)
    if inside is not None:
        side = jnp.where(inside, side, 0.0)
    others = (other[p, r], other[p + 2, r], other[p + 1, 7 : 7 + rows], other[p + 1, 9 : 9 + rows], mid, side)
    weights = [centre + b for b in others]
    total = weights[0]
    for w in weights[1:]:
        total = total + w
    inverse = jnp.where(centre > 0.0, 1.0 / jnp.where(centre > 0.0, total, 1.0), 0.0)
    for which in range(6):
        w = weights[which] * inverse
        if which == 5 and inside is not None:
            w = jnp.where(inside, w, 0.0)
        coef[which, p] = w
    coef[6, p] = f * (inverse * (2.0 / scale))
    coef[7, p] = total * (0.5 * scale)


def relaxed(other, coef, p, index, rows, first=0, shift=0):
    a = 8 + first
    r = slice(a, a + rows)
    c = slice(first, first + rows)
    q = p - shift
    mid = other[p + 1, r]
    out = coef[6, q, c] + coef[0, q, c] * other[p, r]
    out = out + coef[1, q, c] * other[p + 2, r]
    out = out + coef[2, q, c] * other[p + 1, a - 1 : a - 1 + rows]
    out = out + coef[3, q, c] * other[p + 1, a + 1 : a + 1 + rows]
    out = out + coef[4, q, c] * mid
    return out + coef[5, q, c] * beside(mid, index)


def pairs(start, stop, body, rows):
    count = stop - start
    most = 8 * GROUP if rows < 64 else 16 * GROUP
    width = max(w for w in (2, 4, 8, 16) if w == 2 or (count % w == 0 and w * rows <= most))

    def step(t, carry):
        for n in range(width):
            body(start + t * width + n, n % 2)
        return carry

    if count == width:
        step(0, 0)
    else:
        lax.fori_loop(0, count // width, step, 0)


def update(mine, other, coef, index, start, stop, rows, flip, shift=0):
    def body(p, parity):
        mine[p + 1, 8 : 8 + rows] = relaxed(other, coef, p, index[(parity + flip) % 2], rows, 0, shift)

    pairs(start, stop, body, rows)


def defect(red, black, cr, cb, p, parity, index, rows, first=0, shift=0):
    r = slice(8 + first, 8 + first + rows)
    c = slice(first, first + rows)
    er = cr[7, p - shift, c] * (relaxed(black, cr, p, index[parity], rows, first, shift) - red[p + 1, r])
    eb = cb[7, p - shift, c] * (relaxed(red, cb, p, index[1 - parity], rows, first, shift) - black[p + 1, r])
    return er, eb


def halve_rows(tmp, value, rows):
    tmp[0:rows] = value
    return 0.125 * (tmp[pl.ds(0, rows // 2, 2)] + tmp[pl.ds(1, rows // 2, 2)])


def double_rows(tmp, value, rows):
    tmp[pl.ds(0, rows, 2)] = value
    tmp[pl.ds(1, rows, 2)] = value


def fine_down(
    at, wf, wb, xl, xu, yl, yu, zl, zu, g_ref, cr_out, cb_out, br, bb, fr, fb, cr, cb, vr, vb, tmp, sems
):
    gx, gy, gz = at[0], at[1], at[2]
    lane, row = lanes(48), sublanes(48)
    own = lane < 64
    keep = own | ((lane < 96) & (gz < 7)) | ((lane >= 96) & (gz > 0))
    keep = keep & ((row >= 8) | (gy > 0)) & ((row < 40) | (gy < 3))
    kept = jnp.where(keep, 1.0, 0.0).astype(F32)
    below = jnp.where(gx > 0, 1.0, 0.0).astype(F32)
    above = jnp.where(gx < 3, 1.0, 0.0).astype(F32)
    left = jnp.where(gy > 0, 1.0, 0.0).astype(F32)
    right = jnp.where(gy < 3, 1.0, 0.0).astype(F32)
    vr[...] = jnp.zeros_like(vr)
    vb[...] = jnp.zeros_like(vb)
    edge = jnp.zeros((8, 128), F32)
    for b in (br, bb):
        for q in range(34):
            b[q, 0:8] = edge
            b[q, 56:64] = edge
        for q in (0, 33):
            b[q, 8:56] = jnp.zeros((48, 128), F32)
    for which, width, base in ((0, 16, 0), (1, 16, 48)):
        count = 64 // width
        slot = (lane % 64) // width
        for p in range(32):
            plane = plane_b(wb, xl, xu, p) if which else plane_f(wf, xl, xu, p)
            w = slab(plane, yl, yu, which, p)
            s = p % count
            start = base + 6 * (p // count)
            up = zu[start : start + 6].reshape(48, 128)
            low = zl[start : start + 6].reshape(48, 128)
            both = jnp.where(slot == s, up, low)
            red = jnp.where(own, w, turn(both, 64 - width * s))
            black = jnp.where(own, turn(w, 64), turn(both, -width * s))
            if which:
                k = kept * below if p < 8 else kept * above if p >= 24 else kept
                br[p + 1, 8:56] = red * k
                bb[p + 1, 8:56] = black * k
            else:
                fr[p] = red
                fb[p] = black
    for a in range(2):
        for src, r, ok in ((yl, 7, left), (yu, 56, right)):
            v = src[64 + a] * ok
            t = turn(v, 64)
            for s in range(8):
                br[9 + 8 * a + s, r : r + 1] = v[s : s + 1]
                bb[9 + 8 * a + s, r : r + 1] = t[s : s + 1]
    for v, q in ((xl[8] * below, 0), (xu[16] * above, 33)):
        br[q, 16:48] = v
        bb[q, 16:48] = turn(v, 64)

    index = [side_rule(48, parity) for parity in range(2)]

    def coefs(p, parity):
        make_coefs(br, bb, fr[p], cr, p, index[parity], 1.0, 48)
        make_coefs(bb, br, fb[p], cb, p, index[1 - parity], 1.0, 48)
        vr[p + 1, 8:56] = cr[6, p]

    pairs(0, 32, coefs, 48)
    copies = [
        pltpu.make_async_copy(cr.at[:, pl.ds(4, 24)], cr_out, sems.at[0]),
        pltpu.make_async_copy(cb.at[:, pl.ds(3, 26)], cb_out.at[pl.ds(0, 8)], sems.at[1]),
        pltpu.make_async_copy(vb.at[pl.ds(4, 26), pl.ds(8, 48)], cb_out.at[8], sems.at[2]),
    ]
    copies[0].start()
    copies[1].start()
    update(vb, vr, cb, index, 0, 32, 48, 1)
    update(vr, vb, cr, index, 2, 30, 48, 0)
    update(vb, vr, cb, index, 2, 30, 48, 1)
    copies[2].start()
    inner = [side_rule(32, parity) for parity in range(2)]
    swap = gx >= 2
    lane16 = lanes(16)
    spare = (lane16 % 64 >= 38) & (lane16 % 64 < 58)
    for n in range(8):
        total = coarse = None
        for parity in range(2):
            p = 8 + 2 * n + parity
            er, eb = defect(vr, vb, cr, cb, p, parity, inner, 32, 8)
            b = br[p + 1, 16:48] + bb[p + 1, 16:48]
            total = er + eb if total is None else total + (er + eb)
            coarse = b if coarse is None else coarse + b
        f1 = pick(halve_rows(tmp, total, 32), by_colour(n, swap))
        b1 = halve_rows(tmp, coarse, 32)
        w1 = jnp.where(spare, pick(b1, spared(by_colour(n, swap))), f1)
        for copy in range(16):
            g_ref[copy, 16 * n : 16 * n + 16] = w1
    for c in copies:
        c.wait()


def across(g, a, start):
    r = slice(start, start + 16)
    return jnp.concatenate([g[4 * a + y, r] for y in range(4)], axis=0)


def joined_f(g, p):
    wa, wb = (across(g, p // 8 + up, 16 * (p % 8)) for up in (0, 2))
    half = lanes(64) < 64
    return jnp.where(half, wa, wb), turn(jnp.where(half, wb, wa), 64)


def across_b(gx, gy, held, a, n):
    back = (gx - a + 4) % 4
    r = slice(16 * n, 16 * n + 16)
    out = []
    for y in range(4):
        e = (gy - y + 4) % 4
        v = held[0][e, r]
        for d in range(1, 4):
            v = jnp.where(back == d, held[d][e, r], v)
        out.append(v)
    return jnp.concatenate(out, axis=0)


def joined_b(gx, gy, held, a, n):
    wa, wb = (across_b(gx, gy, held, a + up, n) for up in (0, 2))
    half = lanes(64) < 64
    reds = jnp.where(half, wa, turn(wb, 64)), jnp.where(half, turn(wa, 64), wb)
    return [(red, turn(red, -32)) for red in reds]


def seam(v, rows):
    r = slice(8, 8 + rows)
    half = lanes(rows) < 64
    v[0, r] = jnp.where(half, 0.0, turn(v[16, r], 64))
    v[17, r] = jnp.where(half, turn(v[1, r], 64), 0.0)


def mid_down(at, g, h0, h1, h2, h3, w2_ref, c_out, vb_out, br, bb, fr, fb, cr, cb, vr, vb, tmp, sems):
    gx, gy, gz = at[0], at[1], at[2]
    lane = lanes(64)
    own = lane % 64 < 32
    keep = own | ((lane % 64 < 48) & (gz < 7)) | ((lane % 64 >= 48) & (gz > 0))
    kept = jnp.where(keep, 1.0, 0.0).astype(F32)
    halo = (lane + jnp.where(lane % 64 < 48, 6, -6)) % 128
    for v in (vr, vb):
        v[...] = jnp.zeros_like(v)
    for b in (br, bb):
        b[:, 0:8] = jnp.zeros((18, 8, 128), F32)
        b[:, 72:80] = jnp.zeros((18, 8, 128), F32)
    for p in range(16):
        fr[p], fb[p] = joined_f(g, p)
    for a in range(2):
        for n in range(4):
            for up, (red, black) in enumerate(joined_b(gx, gy, (h0, h1, h2, h3), a, n)):
                p = 8 * a + n + 4 * up
                br[p + 1, 8:72] = kept * jnp.where(own, red, pick(fr[p], halo))
                bb[p + 1, 8:72] = kept * jnp.where(own, black, pick(fb[p], halo))
    seam(br, 64)
    seam(bb, 64)
    index = [side_index(64, parity, 64) for parity in range(2)]

    def coefs(p, parity):
        make_coefs(br, bb, fr[p], cr, p, index[parity], 0.25, 64)
        make_coefs(bb, br, fb[p], cb, p, index[1 - parity], 0.25, 64)
        vr[p + 1, 8:72] = cr[6, p]

    pairs(0, 16, coefs, 64)
    seam(vr, 64)
    window = pl.multiple_of(jnp.clip(gy * 16 - 8, 0, 32), 8)
    copies = [
        pltpu.make_async_copy(cr.at[:, :, pl.ds(window, 32)], c_out.at[0], sems.at[0]),
        pltpu.make_async_copy(cb.at[:, :, pl.ds(window, 32)], c_out.at[1], sems.at[1]),
        pltpu.make_async_copy(vb.at[:, pl.ds(window + 8, 32)], vb_out, sems.at[2]),
    ]
    copies[0].start()
    copies[1].start()
    update(vb, vr, cb, index, 0, 16, 64, 1)
    seam(vb, 64)
    update(vr, vb, cr, index, 0, 16, 64, 0)
    seam(vr, 64)
    update(vb, vr, cb, index, 0, 16, 64, 1)
    seam(vb, 64)
    copies[2].start()
    lane, row = lanes(32), sublanes(32)
    for n in range(8):
        total = coarse = None
        for parity in range(2):
            p = 2 * n + parity
            er, eb = defect(vr, vb, cr, cb, p, parity, index, 64)
            e = er + eb
            b = br[p + 1, 8:72] + bb[p + 1, 8:72]
            total = e if total is None else total + e
            coarse = b if coarse is None else coarse + b
        f2 = halve_rows(tmp, total, 64)
        b2 = halve_rows(tmp, coarse, 64)
        odd = (row + n) % 2
        idx = 64 * ((lane % 64) // 32) + 2 * (lane % 16) + jnp.where(lane % 32 < 16, odd, 1 - odd)
        w2 = jnp.where(lane < 64, pick(f2, idx), pick(b2, idx))
        w2_ref[n] = w2
    for c in copies:
        c.wait()


def transposed(blocks):
    slot = lanes(32) // 16
    for bit in (1, 2, 4):
        out = list(blocks)
        for i in range(8):
            if not i & bit:
                x, y = blocks[i], blocks[i + bit]
                out[i] = jnp.where(slot & bit == 0, x, turn(y, 16 * bit))
                out[i + bit] = jnp.where(slot & bit == 0, turn(x, -16 * bit), y)
        blocks = out
    return blocks


def level_scratch(planes, rows):
    return [pltpu.VMEM((planes + 2, rows + 16, 128), F32)] * 4 + [pltpu.VMEM((8, planes, rows, 128), F32)] * 2


def clear(refs):
    for v in refs:
        v[...] = jnp.zeros_like(v)


def smooth_down(br, bb, vr, vb, cr, cb, f_of, index, scale, planes, rows, inside):
    def coefs(p, parity):
        fr, fb = f_of(p)
        make_coefs(br, bb, fr, cr, p, index[parity], scale, rows, inside and inside[parity])
        make_coefs(bb, br, fb, cb, p, index[1 - parity], scale, rows, inside and inside[1 - parity])
        vr[p + 1, 8 : 8 + rows] = cr[6, p]

    pairs(0, planes, coefs, rows)
    update(vb, vr, cb, index, 0, planes, rows, 1)
    update(vr, vb, cr, index, 0, planes, rows, 0)
    update(vb, vr, cb, index, 0, planes, rows, 1)


def smooth_up(vr, vb, cr, cb, index, planes, rows):
    for _ in range(2):
        update(vr, vb, cr, index, 0, planes, rows, 0)
        update(vb, vr, cb, index, 0, planes, rows, 1)


def restrict(level, tmp, index, planes, rows, cells, put):
    br, bb, vr, vb, cr, cb = level
    lane, row = lanes(rows // 2), sublanes(rows // 2)
    for n in range(planes // 2):
        total = coarse = None
        for parity in range(2):
            p = 2 * n + parity
            er, eb = defect(vr, vb, cr, cb, p, parity, index, rows)
            b = br[p + 1, 8 : 8 + rows] + bb[p + 1, 8 : 8 + rows]
            total = er + eb if total is None else total + (er + eb)
            coarse = b if coarse is None else coarse + b
        f = halve_rows(tmp, total, rows)
        b = halve_rows(tmp, coarse, rows)
        odd = (row + n) % 2
        red = 2 * (lane % 64) + odd
        black = 2 * (lane % 64) + 1 - odd
        inside = lane < cells
        put(n, *[jnp.where(inside, pick(x, i), 0.0) for x in (f, b) for i in (red, black)])


def prolong(vr, vb, out, tmp, planes, rows):
    lane, row = lanes(rows), sublanes(rows)
    r = slice(8, 8 + rows)
    for n in range(planes):
        even = (row + lane + n) % 2 == 0
        c = jnp.where(even, pick(vr[n + 1, r], lane // 2), pick(vb[n + 1, r], lane // 2))
        double_rows(tmp, c, rows)
        for p in (2 * n, 2 * n + 1):
            out[p + 1, 8 : 8 + 2 * rows] += tmp[0 : 2 * rows]


def coarse_up(
    at, m0, m1, m2, m3, q0, q1, q2, q3, c1_in, v1b_in, c0r_in, c0b_in, u_ref, res_ref,
    b2r, b2b, v2r, v2b, c2r, c2b, f2,
    b3r, b3b, v3r, v3b, c3r, c3b, f3,
    b4r, b4b, v4r, v4b, c4r, c4b, f4,
    v1r, v1b, c1r, c1b, v0r, v0b, c0r, c0b, tmp, sems,
):
    gx, gy, gz = at[0], at[1], at[2]
    copies = [
        pltpu.make_async_copy(c1_in.at[0], c1r, sems.at[0]),
        pltpu.make_async_copy(c1_in.at[1], c1b, sems.at[1]),
        pltpu.make_async_copy(v1b_in, v1b.at[:, pl.ds(8, 32)], sems.at[2]),
        pltpu.make_async_copy(c0r_in, c0r, sems.at[3]),
        pltpu.make_async_copy(c0b_in.at[pl.ds(0, 8), pl.ds(1, 24)], c0b, sems.at[4]),
        pltpu.make_async_copy(c0b_in.at[8], v0b.at[pl.ds(4, 26), pl.ds(8, 48)], sems.at[5]),
    ]
    for c in copies:
        c.start()
    clear((b2r, b2b, v2r, v2b, b3r, b3b, v3r, v3b, b4r, b4b, v4r, v4b, v1r, v0r))
    v0b[:, 0:8] = jnp.zeros((34, 8, 128), F32)
    v0b[:, 56:64] = jnp.zeros((34, 8, 128), F32)
    v1b[:, 0:8] = jnp.zeros((18, 8, 128), F32)
    v1b[:, 40:48] = jnp.zeros((18, 8, 128), F32)

    chip = gz // 2
    first = gz % 2 == 0
    for n in range(8):
        near = [(jnp.where(first, a[n], b[n]), jnp.where(first, b[n], a[n])) for a, b in ((m0, q0), (m1, q1), (m2, q2), (m3, q3))]
        blocks = []
        for c in range(4):
            for core in range(2):
                v = near[0][core]
                for back in range(1, 4):
                    v = jnp.where(chip == (c + back) % 4, near[back][core], v)
                blocks.append(v)
        out = transposed(blocks)
        for h in range(2):
            p = n + 8 * h
            f2[0, p] = out[2 * h]
            f2[1, p] = out[2 * h + 1]
            b2r[p + 1, 8:40] = out[4 + 2 * h]
            b2b[p + 1, 8:40] = out[5 + 2 * h]
    lane = lanes(32)
    index2 = [side_rule(32, parity) for parity in range(2)]
    inside2 = [lane != jnp.where(index2[parity], 0, 127) for parity in range(2)]
    smooth_down(b2r, b2b, v2r, v2b, c2r, c2b, lambda p: (f2[0, p], f2[1, p]), index2, 0.25**2, 16, 32, inside2)

    def put3(n, fr, fb, br, bb):
        f3[0, n], f3[1, n] = fr, fb
        b3r[n + 1, 8:24], b3b[n + 1, 8:24] = br, bb

    restrict((b2r, b2b, v2r, v2b, c2r, c2b), tmp, index2, 16, 32, 64, put3)

    index3 = [side_rule(16, parity) for parity in range(2)]
    smooth_down(b3r, b3b, v3r, v3b, c3r, c3b, lambda p: (f3[0, p], f3[1, p]), index3, 0.25**3, 8, 16, None)

    def put4(n, fr, fb, br, bb):
        f4[0, n], f4[1, n] = fr, fb
        b4r[n + 1, 8:16], b4b[n + 1, 8:16] = br, bb

    restrict((b3r, b3b, v3r, v3b, c3r, c3b), tmp, index3, 8, 16, 32, put4)

    index4 = [side_rule(8, parity) for parity in range(2)]

    for p in range(4):
        make_coefs(b4r, b4b, f4[0, p], c4r, p, index4[p % 2], 0.25**4, 8)
        make_coefs(b4b, b4r, f4[1, p], c4b, p, index4[1 - p % 2], 0.25**4, 8)
    row8 = sublanes(8)
    inner = (row8 > 0, row8 < 7)
    cr4 = [[c4r[w, p] for w in range(7)] for p in range(4)]
    cb4 = [[c4b[w, p] for w in range(7)] for p in range(4)]
    for c in cr4 + cb4:
        c[2] = jnp.where(inner[0], c[2], 0.0)
        c[3] = jnp.where(inner[1], c[3], 0.0)

    def half(other, coefs, flip):
        out = []
        for p in range(4):
            c, v = coefs[p], other[p]
            w = c[6] + c[4] * v
            if p > 0:
                w = w + c[0] * other[p - 1]
            if p < 3:
                w = w + c[1] * other[p + 1]
            w = w + c[2] * pltpu.roll(v, 1, 0) + c[3] * pltpu.roll(v, 7, 0)
            out.append(w + c[5] * beside(v, index4[(p + flip) % 2]))
        return out

    def coarse_step(count, state):
        black = list(state)
        red = half(black, cr4, 0)
        return tuple(half(red, cb4, 1))

    black = lax.fori_loop(0, COARSE_ITERS - 1, coarse_step, (jnp.zeros((8, 128), F32),) * 4)
    red = half(black, cr4, 0)
    black = half(red, cb4, 1)
    for p in range(4):
        v4r[p + 1, 8:16] = red[p]
        v4b[p + 1, 8:16] = black[p]

    prolong(v4r, v4b, v3b, tmp, 4, 8)
    smooth_up(v3r, v3b, c3r, c3b, index3, 8, 16)
    prolong(v3r, v3b, v2b, tmp, 8, 16)
    smooth_up(v2r, v2b, c2r, c2b, index2, 16, 32)

    for c in copies[:3]:
        c.wait()
    lane, row = lanes(32), sublanes(32)
    near = lane % 64 - jnp.where(lane % 64 < 48, 0, 64)
    cell = gz * 32 + near
    valid = (cell >= 0) & (cell < 256)
    idx = jnp.clip(cell, 0, 255) // 2
    window = pl.multiple_of(jnp.clip(gy * 16 - 8, 0, 32), 8)
    for n in range(8):
        even = (row + lane + n) % 2 == 0
        parts = []
        for p in (n, n + 8):
            parts.append(jnp.where(even, pick(v2r[p + 1, 8:40], idx), pick(v2b[p + 1, 8:40], idx)))
        c = jnp.where(valid, jnp.where(lane < 64, parts[0], parts[1]), 0.0)
        double_rows(tmp, c, 32)
        for p in (2 * n, 2 * n + 1):
            v1b[p + 1, 8:40] += tmp[pl.ds(window, 32)]
    seam(v1b, 32)
    index1 = [side_index(32, parity, 64) for parity in range(2)]
    for _ in range(2):
        update(v1r, v1b, c1r, index1, 0, 16, 32, 0)
        seam(v1r, 32)
        update(v1b, v1r, c1b, index1, 0, 16, 32, 1)
        seam(v1b, 32)

    for c in copies[3:]:
        c.wait()
    start = pl.multiple_of(gy * 16 - window, 8)
    cell = lane - jnp.where(lane < 96, 0, 128)
    idx = (cell // 2) % 64
    for n in range(-3, 11):
        plane = gx * 8 + n
        held = jnp.clip(plane, 0, 31)
        at_half = idx + 64 * (held // 16)
        even = (row + lane + n) % 2 == 0
        red = v1r[held % 16 + 1, pl.ds(start, 32)]
        black = v1b[held % 16 + 1, pl.ds(start, 32)]
        c = jnp.where(even, pick(red, at_half), pick(black, at_half))
        c = c * jnp.where((plane >= 0) & (plane < 32), 1.0, 0.0).astype(F32)
        tmp[64:96] = c
        double_rows(tmp, tmp[68:92], 24)
        for p in (2 * n + 8, 2 * n + 9):
            v0b[p + 1, 8:56] += tmp[0:48]
    index0 = [side_rule(48, parity) for parity in range(2)]
    update(v0r, v0b, c0r, index0, 4, 28, 48, 0, 4)
    update(v0b, v0r, c0b, index0, 4, 28, 48, 1, 4)
    update(v0r, v0b, c0r, index0, 6, 26, 48, 0, 4)
    update(v0b, v0r, c0b, index0, 6, 26, 48, 1, 4)

    def finish(p, parity):
        even = (row + lane + parity) % 2 == 0
        er, eb = defect(v0r, v0b, c0r, c0b, p, parity, index1_0, 32, 8, 4)
        res_ref[p - 8] = jnp.where(even, pick(er, lane // 2), pick(eb, lane // 2))
        red, black = v0r[p + 1, 16:48], v0b[p + 1, 16:48]
        u_ref[p - 8] = jnp.where(even, pick(red, lane // 2), pick(black, lane // 2))

    index1_0 = [side_rule(32, parity) for parity in range(2)]
    pairs(8, 24, finish, 32)


def around(lo, hi, axis):
    count = lax.axis_size(axis)
    from_above = lax.ppermute(lo, axis, [((i + 1) % count, i) for i in range(count)])
    from_below = lax.ppermute(hi, axis, [(i, (i + 1) % count) for i in range(count)])
    return from_below, from_above


def beyond(x, axis):
    count = lax.axis_size(axis)
    return [lax.ppermute(x, axis, [(i, (i + d) % count) for i in range(count)]) for d in range(1, count)]


def body(source, conductance):
    vmem, smem, hbm = (pl.BlockSpec(memory_space=m) for m in (pltpu.VMEM, pltpu.SMEM, pltpu.HBM))
    at = jnp.stack([lax.axis_index(a) for a in ("gx", "gy", "gz")]).astype(jnp.int32)
    dma = pltpu.SemaphoreType.DMA

    block, x_slab = arr(16, 32, 128), arr(17, 32, 128)
    wf, wb, lo, hi, b1 = call(
        split_fine,
        [(block, block, x_slab, x_slab, arr(64, 128))],
        (jnp.concatenate([source, conductance]),),
        None,
        [pltpu.VMEM((32, 128), F32)],
        8,
    )
    xl, xu = around(lo, hi, "gx")
    b1 = [b1] + beyond(b1, "gy")
    y_slab = arr(66, 8, 128)
    lo, hi, b1 = call(pack_rows, [(y_slab, y_slab, arr(4, 64, 128))], (wf, wb, xl, xu, *b1), limit=8)
    yl, yu = around(lo, hi, "gy")
    yl, yu, *b1 = lax.optimization_barrier((yl, yu, b1, *beyond(b1, "gx")))
    lo, hi = call(pack_lanes, [(arr(96, 8, 128),) * 2], (wf, wb, xl, xu, yl, yu), limit=8)
    zl, zu = around(lo, hi, "gz")

    colour0 = pltpu.VMEM((34, 64, 128), F32)
    right0 = pltpu.VMEM((32, 48, 128), F32)
    coef0 = pltpu.VMEM((8, 32, 48, 128), F32)
    state0 = (arr(8, 24, 48, 128), arr(9, 26, 48, 128))
    g, c0r, c0b = call(
        fine_down,
        [(arr(16, 128, 128),) + state0, (vmem, hbm, hbm)],
        (at, wf, wb, xl, xu, yl, yu, zl, zu),
        [smem] + [vmem] * 8,
        [colour0, colour0, right0, right0, coef0, coef0, colour0, colour0, pltpu.VMEM((32, 128), F32), dma((3,))],
        LIMIT_FINE,
    )
    g = lax.all_to_all(g, ("gx", "gy"), 0, 0, tiled=True)

    state1 = (arr(2, 8, 16, 32, 128), arr(18, 32, 128))
    colour1 = pltpu.VMEM((18, 80, 128), F32)
    right1 = pltpu.VMEM((16, 64, 128), F32)
    coef1 = pltpu.VMEM((8, 16, 64, 128), F32)
    w2, c1, v1b = call(
        mid_down,
        [(arr(8, 32, 128),) + state1, (vmem, hbm, hbm)],
        (at, g, *b1),
        [smem] + [vmem] * 5,
        [colour1, colour1, right1, right1, coef1, coef1, colour1, colour1, pltpu.VMEM((64, 128), F32), dma((3,))],
        LIMIT_MID,
    )
    mine = [w2] + [lax.ppermute(w2, "gz", [(i, (i + d) % 8) for i in range(8)]) for d in (2, 4, 6)]
    pair = [lax.ppermute(w, "gz", [(i, i ^ 1) for i in range(8)]) for w in mine]

    scratch = []
    for planes, rows in ((16, 32), (8, 16), (4, 8)):
        scratch += level_scratch(planes, rows) + [pltpu.VMEM((2, planes, rows, 128), F32)]
    scratch += [pltpu.VMEM((18, 48, 128), F32)] * 2 + [pltpu.VMEM((8, 16, 32, 128), F32)] * 2
    scratch += [colour0] * 2 + [pltpu.VMEM((8, 24, 48, 128), F32)] * 2
    scratch += [pltpu.VMEM((96, 128), F32), dma((6,))]
    return call(
        coarse_up,
        [(block, block)],
        (at, *mine, *pair, c1, v1b, c0r, c0b),
        [smem] + [vmem] * 8 + [hbm] * 4,
        scratch,
        LIMIT_UP,
    )


def solution(mesh):
    placed = (P("gx", "gy", "gz"), P("gx", "gy", "gz"))
    return jax.shard_map(body, mesh=mesh, in_specs=placed, out_specs=placed, check_vma=False)
```

```python
import functools

import jax
import jax.numpy as jnp
from jax import lax
from jax.experimental import pallas as pl
from jax.experimental.pallas import tpu as pltpu
from jax.sharding import PartitionSpec as P

F32 = jnp.float32
COARSE_ITERS = 20
MIB = 1 << 20
GROUP = 64
LIMIT_FINE = 50
LIMIT_MID = 50
LIMIT_UP = 50


def lanes(rows):
    return lax.broadcasted_iota(jnp.int32, (rows, 128), 1)


def sublanes(rows):
    return lax.broadcasted_iota(jnp.int32, (rows, 128), 0)


def pick(x, idx):
    return jnp.take_along_axis(x, idx, axis=1, mode="promise_in_bounds")


def turn(x, shift):
    shift = shift % 128
    return pltpu.roll(x, shift, 1) if shift else x


def side_index(rows, parity, period):
    lane, row = lanes(rows), sublanes(rows)
    step = 2 * ((row + parity) % 2) - 1
    within = (lane % period + step + period) % period
    return lane - lane % period + within


def side_rule(rows, parity):
    return (sublanes(rows) + parity) % 2 == 0


def beside(x, rule):
    if rule.dtype == jnp.bool_:
        return jnp.where(rule, pltpu.roll(x, 1, 1), pltpu.roll(x, 127, 1))
    return pick(x, rule)


def call(kernel, out, args, specs=None, scratch=(), limit=40):
    vmem = pl.BlockSpec(memory_space=pltpu.VMEM)
    return pl.pallas_call(
        kernel,
        out_shape=out[0],
        in_specs=specs or [vmem] * len(args),
        out_specs=out[1] if len(out) > 1 else jax.tree.map(lambda _: vmem, out[0]),
        scratch_shapes=scratch,
        compiler_params=pltpu.CompilerParams(vmem_limit_bytes=limit * MIB),
        name=kernel.__name__,
    )(*args)


def arr(*shape):
    return jax.ShapeDtypeStruct(shape, F32)


def split_fine(both_ref, wf_ref, wb_ref, lo_ref, hi_ref, b1_ref, tmp):
    lane, row = lanes(32), sublanes(32)
    index = []
    for parity in range(2):
        odd = (row + parity) % 2
        index.append(2 * (lane % 64) + jnp.where(lane < 64, odd, 1 - odd))
    lane16, row16 = lanes(16), sublanes(16)
    own = []
    for n in range(8):
        w = [pick(both_ref[16 + 2 * n + parity], index[parity]) for parity in range(2)]
        for parity in range(2):
            i = 2 * n + parity
            wb_ref[i] = w[parity]
            if i < 9:
                lo_ref[8 + i] = w[parity]
            if i > 6:
                hi_ref[1 + i] = w[parity]
        both = w[0] + w[1]
        odd = (row16 + n) % 2
        cell = 2 * (lane16 % 32) + jnp.where(lane16 % 64 < 32, odd, 1 - odd)
        own.append(pick(halve_rows(tmp, both + turn(both, 64), 32), cell))
    for n in range(4):
        b1_ref[16 * n : 16 * n + 16] = jnp.where(lane16 < 64, own[n], own[n + 4])
    for i in range(16):
        wf = pick(both_ref[i], index[i % 2])
        wf_ref[i] = wf
        if i < 8:
            lo_ref[i] = wf
        else:
            hi_ref[i - 8] = wf


def by_colour(n, swap):
    lane, row = lanes(16), sublanes(16)
    odd = (row + n) % 2
    return (2 * (lane % 64) + jnp.where((lane < 64) != swap, odd, 1 - odd)) % 128


def spared(index):
    return (index + jnp.where(lanes(16) % 64 < 48, -12, 12)) % 128


def plane_f(wf, xl, xu, p):
    return xl.at[p] if p < 8 else wf.at[p - 8] if p < 24 else xu.at[p - 24]


def plane_b(wb, xl, xu, p):
    return xl.at[9 + p] if p < 8 else wb.at[p - 8] if p < 24 else xu.at[8 + p - 24]


def pack_rows(wf, wb, xl, xu, b0, b1, b2, b3, lo_ref, hi_ref, b1_ref):
    for back, b in enumerate((b0, b1, b2, b3)):
        b1_ref[back] = b[...]
    for p in range(32):
        f, b = plane_f(wf, xl, xu, p), plane_b(wb, xl, xu, p)
        lo_ref[p] = f[0:8]
        hi_ref[p] = f[24:32]
        lo_ref[32 + p] = b[0:8]
        hi_ref[32 + p] = b[24:32]
    for i in range(16):
        lo_ref[64 + i // 8, i % 8 : i % 8 + 1] = wb[i, 8:9]
        hi_ref[64 + i // 8, i % 8 : i % 8 + 1] = wb[i, 23:24]


def slab(plane, yl, yu, which, p):
    return jnp.concatenate([yl[32 * which + p], plane[...], yu[32 * which + p]], axis=0)


def pack_lanes(wf, wb, xl, xu, yl, yu, lo_ref, hi_ref):
    slot_of = lanes(48) % 64
    for which, width, base in ((0, 16, 0), (1, 16, 48)):
        count = 64 // width
        slot = slot_of // width
        for group in range(32 // count):
            for s in range(count):
                p = group * count + s
                plane = plane_b(wb, xl, xu, p) if which else plane_f(wf, xl, xu, p)
                v = turn(slab(plane, yl, yu, which, p), width * s)
                if s == 0:
                    low = high = v
                else:
                    low = jnp.where(slot == s, v, low)
                    high = jnp.where(slot == s - 1, v, high)
            start = base + 6 * group
            lo_ref[start : start + 6] = low.reshape(6, 8, 128)
            hi_ref[start : start + 6] = high.reshape(6, 8, 128)


def make_coefs(mine, other, f, coef, p, index, scale, rows, inside=None):
    r = slice(8, 8 + rows)
    centre = mine[p + 1, r]
    mid = other[p + 1, r]
    side = beside(mid, index)
    if inside is not None:
        side = jnp.where(inside, side, 0.0)
    others = (other[p, r], other[p + 2, r], other[p + 1, 7 : 7 + rows], other[p + 1, 9 : 9 + rows], mid, side)
    weights = [centre + b for b in others]
    total = weights[0]
    for w in weights[1:]:
        total = total + w
    inverse = jnp.where(centre > 0.0, 1.0 / jnp.where(centre > 0.0, total, 1.0), 0.0)
    for which in range(6):
        w = weights[which] * inverse
        if which == 5 and inside is not None:
            w = jnp.where(inside, w, 0.0)
        coef[which, p] = w
    coef[6, p] = f * (inverse * (2.0 / scale))
    coef[7, p] = total * (0.5 * scale)


def relaxed(other, coef, p, index, rows, first=0, shift=0):
    a = 8 + first
    r = slice(a, a + rows)
    c = slice(first, first + rows)
    q = p - shift
    mid = other[p + 1, r]
    out = coef[6, q, c] + coef[0, q, c] * other[p, r]
    out = out + coef[1, q, c] * other[p + 2, r]
    out = out + coef[2, q, c] * other[p + 1, a - 1 : a - 1 + rows]
    out = out + coef[3, q, c] * other[p + 1, a + 1 : a + 1 + rows]
    out = out + coef[4, q, c] * mid
    return out + coef[5, q, c] * beside(mid, index)


def pairs(start, stop, body, rows):
    count = stop - start
    most = 8 * GROUP if rows < 64 else 16 * GROUP
    width = max(w for w in (2, 4, 8, 16) if w == 2 or (count % w == 0 and w * rows <= most))

    def step(t, carry):
        for n in range(width):
            body(start + t * width + n, n % 2)
        return carry

    if count == width:
        step(0, 0)
    else:
        lax.fori_loop(0, count // width, step, 0)


def update(mine, other, coef, index, start, stop, rows, flip, shift=0):
    def body(p, parity):
        mine[p + 1, 8 : 8 + rows] = relaxed(other, coef, p, index[(parity + flip) % 2], rows, 0, shift)

    pairs(start, stop, body, rows)


def defect(red, black, cr, cb, p, parity, index, rows, first=0, shift=0):
    r = slice(8 + first, 8 + first + rows)
    c = slice(first, first + rows)
    er = cr[7, p - shift, c] * (relaxed(black, cr, p, index[parity], rows, first, shift) - red[p + 1, r])
    eb = cb[7, p - shift, c] * (relaxed(red, cb, p, index[1 - parity], rows, first, shift) - black[p + 1, r])
    return er, eb


def halve_rows(tmp, value, rows):
    tmp[0:rows] = value
    return 0.125 * (tmp[pl.ds(0, rows // 2, 2)] + tmp[pl.ds(1, rows // 2, 2)])


def double_rows(tmp, value, rows):
    tmp[pl.ds(0, rows, 2)] = value
    tmp[pl.ds(1, rows, 2)] = value


def fine_down(
    at, wf, wb, xl, xu, yl, yu, zl, zu, g_ref, cr_out, cb_out, br, bb, fr, fb, cr, cb, vr, vb, tmp, sems
):
    gx, gy, gz = at[0], at[1], at[2]
    lane, row = lanes(48), sublanes(48)
    own = lane < 64
    keep = own | ((lane < 96) & (gz < 7)) | ((lane >= 96) & (gz > 0))
    keep = keep & ((row >= 8) | (gy > 0)) & ((row < 40) | (gy < 3))
    kept = jnp.where(keep, 1.0, 0.0).astype(F32)
    below = jnp.where(gx > 0, 1.0, 0.0).astype(F32)
    above = jnp.where(gx < 3, 1.0, 0.0).astype(F32)
    left = jnp.where(gy > 0, 1.0, 0.0).astype(F32)
    right = jnp.where(gy < 3, 1.0, 0.0).astype(F32)
    vr[...] = jnp.zeros_like(vr)
    vb[...] = jnp.zeros_like(vb)
    edge = jnp.zeros((8, 128), F32)
    for b in (br, bb):
        for q in range(34):
            b[q, 0:8] = edge
            b[q, 56:64] = edge
        for q in (0, 33):
            b[q, 8:56] = jnp.zeros((48, 128), F32)
    for which, width, base in ((0, 16, 0), (1, 16, 48)):
        count = 64 // width
        slot = (lane % 64) // width
        for p in range(32):
            plane = plane_b(wb, xl, xu, p) if which else plane_f(wf, xl, xu, p)
            w = slab(plane, yl, yu, which, p)
            s = p % count
            start = base + 6 * (p // count)
            up = zu[start : start + 6].reshape(48, 128)
            low = zl[start : start + 6].reshape(48, 128)
            both = jnp.where(slot == s, up, low)
            red = jnp.where(own, w, turn(both, 64 - width * s))
            black = jnp.where(own, turn(w, 64), turn(both, -width * s))
            if which:
                k = kept * below if p < 8 else kept * above if p >= 24 else kept
                br[p + 1, 8:56] = red * k
                bb[p + 1, 8:56] = black * k
            else:
                fr[p] = red
                fb[p] = black
    for a in range(2):
        for src, r, ok in ((yl, 7, left), (yu, 56, right)):
            v = src[64 + a] * ok
            t = turn(v, 64)
            for s in range(8):
                br[9 + 8 * a + s, r : r + 1] = v[s : s + 1]
                bb[9 + 8 * a + s, r : r + 1] = t[s : s + 1]
    for v, q in ((xl[8] * below, 0), (xu[16] * above, 33)):
        br[q, 16:48] = v
        bb[q, 16:48] = turn(v, 64)

    index = [side_rule(48, parity) for parity in range(2)]

    def coefs(p, parity):
        make_coefs(br, bb, fr[p], cr, p, index[parity], 1.0, 48)
        make_coefs(bb, br, fb[p], cb, p, index[1 - parity], 1.0, 48)
        vr[p + 1, 8:56] = cr[6, p]

    pairs(0, 32, coefs, 48)
    copies = [
        pltpu.make_async_copy(cr.at[:, pl.ds(4, 24)], cr_out, sems.at[0]),
        pltpu.make_async_copy(cb.at[:, pl.ds(3, 26)], cb_out.at[pl.ds(0, 8)], sems.at[1]),
        pltpu.make_async_copy(vb.at[pl.ds(4, 26), pl.ds(8, 48)], cb_out.at[8], sems.at[2]),
    ]
    copies[0].start()
    copies[1].start()
    update(vb, vr, cb, index, 0, 32, 48, 1)
    update(vr, vb, cr, index, 2, 30, 48, 0)
    update(vb, vr, cb, index, 2, 30, 48, 1)
    copies[2].start()
    inner = [side_rule(32, parity) for parity in range(2)]
    swap = gx >= 2
    lane16 = lanes(16)
    spare = (lane16 % 64 >= 38) & (lane16 % 64 < 58)
    for n in range(8):
        total = coarse = None
        for parity in range(2):
            p = 8 + 2 * n + parity
            er, eb = defect(vr, vb, cr, cb, p, parity, inner, 32, 8)
            b = br[p + 1, 16:48] + bb[p + 1, 16:48]
            total = er + eb if total is None else total + (er + eb)
            coarse = b if coarse is None else coarse + b
        f1 = pick(halve_rows(tmp, total, 32), by_colour(n, swap))
        b1 = halve_rows(tmp, coarse, 32)
        w1 = jnp.where(spare, pick(b1, spared(by_colour(n, swap))), f1)
        for copy in range(16):
            g_ref[copy, 16 * n : 16 * n + 16] = w1
    for c in copies:
        c.wait()


def across(g, a, start):
    r = slice(start, start + 16)
    return jnp.concatenate([g[4 * a + y, r] for y in range(4)], axis=0)


def joined_f(g, p):
    wa, wb = (across(g, p // 8 + up, 16 * (p % 8)) for up in (0, 2))
    half = lanes(64) < 64
    return jnp.where(half, wa, wb), turn(jnp.where(half, wb, wa), 64)


def across_b(gx, gy, held, a, n):
    back = (gx - a + 4) % 4
    r = slice(16 * n, 16 * n + 16)
    out = []
    for y in range(4):
        e = (gy - y + 4) % 4
        v = held[0][e, r]
        for d in range(1, 4):
            v = jnp.where(back == d, held[d][e, r], v)
        out.append(v)
    return jnp.concatenate(out, axis=0)


def joined_b(gx, gy, held, a, n):
    wa, wb = (across_b(gx, gy, held, a + up, n) for up in (0, 2))
    half = lanes(64) < 64
    reds = jnp.where(half, wa, turn(wb, 64)), jnp.where(half, turn(wa, 64), wb)
    return [(red, turn(red, -32)) for red in reds]


def seam(v, rows):
    r = slice(8, 8 + rows)
    half = lanes(rows) < 64
    v[0, r] = jnp.where(half, 0.0, turn(v[16, r], 64))
    v[17, r] = jnp.where(half, turn(v[1, r], 64), 0.0)


def mid_down(at, g, h0, h1, h2, h3, w2_ref, c_out, vb_out, br, bb, fr, fb, cr, cb, vr, vb, tmp, sems):
    gx, gy, gz = at[0], at[1], at[2]
    lane = lanes(64)
    own = lane % 64 < 32
    keep = own | ((lane % 64 < 48) & (gz < 7)) | ((lane % 64 >= 48) & (gz > 0))
    kept = jnp.where(keep, 1.0, 0.0).astype(F32)
    halo = (lane + jnp.where(lane % 64 < 48, 6, -6)) % 128
    for v in (vr, vb):
        v[...] = jnp.zeros_like(v)
    for b in (br, bb):
        b[:, 0:8] = jnp.zeros((18, 8, 128), F32)
        b[:, 72:80] = jnp.zeros((18, 8, 128), F32)
    for p in range(16):
        fr[p], fb[p] = joined_f(g, p)
    for a in range(2):
        for n in range(4):
            for up, (red, black) in enumerate(joined_b(gx, gy, (h0, h1, h2, h3), a, n)):
                p = 8 * a + n + 4 * up
                br[p + 1, 8:72] = kept * jnp.where(own, red, pick(fr[p], halo))
                bb[p + 1, 8:72] = kept * jnp.where(own, black, pick(fb[p], halo))
    seam(br, 64)
    seam(bb, 64)
    index = [side_index(64, parity, 64) for parity in range(2)]

    def coefs(p, parity):
        make_coefs(br, bb, fr[p], cr, p, index[parity], 0.25, 64)
        make_coefs(bb, br, fb[p], cb, p, index[1 - parity], 0.25, 64)
        vr[p + 1, 8:72] = cr[6, p]

    pairs(0, 16, coefs, 64)
    seam(vr, 64)
    window = pl.multiple_of(jnp.clip(gy * 16 - 8, 0, 32), 8)
    copies = [
        pltpu.make_async_copy(cr.at[:, :, pl.ds(window, 32)], c_out.at[0], sems.at[0]),
        pltpu.make_async_copy(cb.at[:, :, pl.ds(window, 32)], c_out.at[1], sems.at[1]),
        pltpu.make_async_copy(vb.at[:, pl.ds(window + 8, 32)], vb_out, sems.at[2]),
    ]
    copies[0].start()
    copies[1].start()
    update(vb, vr, cb, index, 0, 16, 64, 1)
    seam(vb, 64)
    update(vr, vb, cr, index, 0, 16, 64, 0)
    seam(vr, 64)
    update(vb, vr, cb, index, 0, 16, 64, 1)
    seam(vb, 64)
    copies[2].start()
    lane, row = lanes(32), sublanes(32)
    for n in range(8):
        total = coarse = None
        for parity in range(2):
            p = 2 * n + parity
            er, eb = defect(vr, vb, cr, cb, p, parity, index, 64)
            e = er + eb
            b = br[p + 1, 8:72] + bb[p + 1, 8:72]
            total = e if total is None else total + e
            coarse = b if coarse is None else coarse + b
        f2 = halve_rows(tmp, total, 64)
        b2 = halve_rows(tmp, coarse, 64)
        odd = (row + n) % 2
        idx = 64 * ((lane % 64) // 32) + 2 * (lane % 16) + jnp.where(lane % 32 < 16, odd, 1 - odd)
        w2 = jnp.where(lane < 64, pick(f2, idx), pick(b2, idx))
        w2_ref[n] = w2
    for c in copies:
        c.wait()


def transposed(blocks):
    slot = lanes(32) // 16
    for bit in (1, 2, 4):
        out = list(blocks)
        for i in range(8):
            if not i & bit:
                x, y = blocks[i], blocks[i + bit]
                out[i] = jnp.where(slot & bit == 0, x, turn(y, 16 * bit))
                out[i + bit] = jnp.where(slot & bit == 0, turn(x, -16 * bit), y)
        blocks = out
    return blocks


def level_scratch(planes, rows):
    return [pltpu.VMEM((planes + 2, rows + 16, 128), F32)] * 4 + [pltpu.VMEM((8, planes, rows, 128), F32)] * 2


def clear(refs):
    for v in refs:
        v[...] = jnp.zeros_like(v)


def smooth_down(br, bb, vr, vb, cr, cb, f_of, index, scale, planes, rows, inside):
    def coefs(p, parity):
        fr, fb = f_of(p)
        make_coefs(br, bb, fr, cr, p, index[parity], scale, rows, inside and inside[parity])
        make_coefs(bb, br, fb, cb, p, index[1 - parity], scale, rows, inside and inside[1 - parity])
        vr[p + 1, 8 : 8 + rows] = cr[6, p]

    pairs(0, planes, coefs, rows)
    update(vb, vr, cb, index, 0, planes, rows, 1)
    update(vr, vb, cr, index, 0, planes, rows, 0)
    update(vb, vr, cb, index, 0, planes, rows, 1)


def smooth_up(vr, vb, cr, cb, index, planes, rows):
    for _ in range(2):
        update(vr, vb, cr, index, 0, planes, rows, 0)
        update(vb, vr, cb, index, 0, planes, rows, 1)


def restrict(level, tmp, index, planes, rows, cells, put):
    br, bb, vr, vb, cr, cb = level
    lane, row = lanes(rows // 2), sublanes(rows // 2)
    for n in range(planes // 2):
        total = coarse = None
        for parity in range(2):
            p = 2 * n + parity
            er, eb = defect(vr, vb, cr, cb, p, parity, index, rows)
            b = br[p + 1, 8 : 8 + rows] + bb[p + 1, 8 : 8 + rows]
            total = er + eb if total is None else total + (er + eb)
            coarse = b if coarse is None else coarse + b
        f = halve_rows(tmp, total, rows)
        b = halve_rows(tmp, coarse, rows)
        odd = (row + n) % 2
        red = 2 * (lane % 64) + odd
        black = 2 * (lane % 64) + 1 - odd
        inside = lane < cells
        put(n, *[jnp.where(inside, pick(x, i), 0.0) for x in (f, b) for i in (red, black)])


def prolong(vr, vb, out, tmp, planes, rows):
    lane, row = lanes(rows), sublanes(rows)
    r = slice(8, 8 + rows)
    for n in range(planes):
        even = (row + lane + n) % 2 == 0
        c = jnp.where(even, pick(vr[n + 1, r], lane // 2), pick(vb[n + 1, r], lane // 2))
        double_rows(tmp, c, rows)
        for p in (2 * n, 2 * n + 1):
            out[p + 1, 8 : 8 + 2 * rows] += tmp[0 : 2 * rows]


def coarse_up(
    at, m0, m1, m2, m3, q0, q123, c1_in, v1b_in, c0r_in, c0b_in, u_ref, res_ref,
    b2r, b2b, v2r, v2b, c2r, c2b, f2,
    b3r, b3b, v3r, v3b, c3r, c3b, f3,
    b4r, b4b, v4r, v4b, c4r, c4b, f4,
    v1r, v1b, c1r, c1b, v0r, v0b, c0r, c0b, tmp, sems,
):
    gx, gy, gz = at[0], at[1], at[2]
    copies = [
        pltpu.make_async_copy(c1_in.at[0], c1r, sems.at[0]),
        pltpu.make_async_copy(c1_in.at[1], c1b, sems.at[1]),
        pltpu.make_async_copy(v1b_in, v1b.at[:, pl.ds(8, 32)], sems.at[2]),
        pltpu.make_async_copy(c0r_in, c0r, sems.at[3]),
        pltpu.make_async_copy(c0b_in.at[pl.ds(0, 8), pl.ds(1, 24)], c0b, sems.at[4]),
        pltpu.make_async_copy(c0b_in.at[8], v0b.at[pl.ds(4, 26), pl.ds(8, 48)], sems.at[5]),
    ]
    for c in copies:
        c.start()
    clear((b2r, b2b, v2r, v2b, b3r, b3b, v3r, v3b, b4r, b4b, v4r, v4b, v1r, v0r))
    v0b[:, 0:8] = jnp.zeros((34, 8, 128), F32)
    v0b[:, 56:64] = jnp.zeros((34, 8, 128), F32)
    v1b[:, 0:8] = jnp.zeros((18, 8, 128), F32)
    v1b[:, 40:48] = jnp.zeros((18, 8, 128), F32)

    chip = gz // 2
    first = gz % 2 == 0
    q1, q2, q3 = (q123.at[pl.ds(8 * n, 8)] for n in range(3))
    for n in range(8):
        near = [(jnp.where(first, a[n], b[n]), jnp.where(first, b[n], a[n])) for a, b in ((m0, q0), (m1, q1), (m2, q2), (m3, q3))]
        blocks = []
        for c in range(4):
            for core in range(2):
                v = near[0][core]
                for back in range(1, 4):
                    v = jnp.where(chip == (c + back) % 4, near[back][core], v)
                blocks.append(v)
        out = transposed(blocks)
        for h in range(2):
            p = n + 8 * h
            f2[0, p] = out[2 * h]
            f2[1, p] = out[2 * h + 1]
            b2r[p + 1, 8:40] = out[4 + 2 * h]
            b2b[p + 1, 8:40] = out[5 + 2 * h]
    lane = lanes(32)
    index2 = [side_rule(32, parity) for parity in range(2)]
    inside2 = [lane != jnp.where(index2[parity], 0, 127) for parity in range(2)]
    smooth_down(b2r, b2b, v2r, v2b, c2r, c2b, lambda p: (f2[0, p], f2[1, p]), index2, 0.25**2, 16, 32, inside2)

    def put3(n, fr, fb, br, bb):
        f3[0, n], f3[1, n] = fr, fb
        b3r[n + 1, 8:24], b3b[n + 1, 8:24] = br, bb

    restrict((b2r, b2b, v2r, v2b, c2r, c2b), tmp, index2, 16, 32, 64, put3)

    index3 = [side_rule(16, parity) for parity in range(2)]
    smooth_down(b3r, b3b, v3r, v3b, c3r, c3b, lambda p: (f3[0, p], f3[1, p]), index3, 0.25**3, 8, 16, None)

    def put4(n, fr, fb, br, bb):
        f4[0, n], f4[1, n] = fr, fb
        b4r[n + 1, 8:16], b4b[n + 1, 8:16] = br, bb

    restrict((b3r, b3b, v3r, v3b, c3r, c3b), tmp, index3, 8, 16, 32, put4)

    index4 = [side_rule(8, parity) for parity in range(2)]

    for p in range(4):
        make_coefs(b4r, b4b, f4[0, p], c4r, p, index4[p % 2], 0.25**4, 8)
        make_coefs(b4b, b4r, f4[1, p], c4b, p, index4[1 - p % 2], 0.25**4, 8)
    row8 = sublanes(8)
    inner = (row8 > 0, row8 < 7)
    cr4 = [[c4r[w, p] for w in range(7)] for p in range(4)]
    cb4 = [[c4b[w, p] for w in range(7)] for p in range(4)]
    for c in cr4 + cb4:
        c[2] = jnp.where(inner[0], c[2], 0.0)
        c[3] = jnp.where(inner[1], c[3], 0.0)

    def half(other, coefs, flip):
        out = []
        for p in range(4):
            c, v = coefs[p], other[p]
            w = c[6] + c[4] * v
            if p > 0:
                w = w + c[0] * other[p - 1]
            if p < 3:
                w = w + c[1] * other[p + 1]
            w = w + c[2] * pltpu.roll(v, 1, 0) + c[3] * pltpu.roll(v, 7, 0)
            out.append(w + c[5] * beside(v, index4[(p + flip) % 2]))
        return out

    def coarse_step(count, state):
        black = list(state)
        red = half(black, cr4, 0)
        return tuple(half(red, cb4, 1))

    black = lax.fori_loop(0, COARSE_ITERS - 1, coarse_step, (jnp.zeros((8, 128), F32),) * 4)
    red = half(black, cr4, 0)
    black = half(red, cb4, 1)
    for p in range(4):
        v4r[p + 1, 8:16] = red[p]
        v4b[p + 1, 8:16] = black[p]

    prolong(v4r, v4b, v3b, tmp, 4, 8)
    smooth_up(v3r, v3b, c3r, c3b, index3, 8, 16)
    prolong(v3r, v3b, v2b, tmp, 8, 16)
    smooth_up(v2r, v2b, c2r, c2b, index2, 16, 32)

    for c in copies[:3]:
        c.wait()
    lane, row = lanes(32), sublanes(32)
    near = lane % 64 - jnp.where(lane % 64 < 48, 0, 64)
    cell = gz * 32 + near
    valid = (cell >= 0) & (cell < 256)
    idx = jnp.clip(cell, 0, 255) // 2
    window = pl.multiple_of(jnp.clip(gy * 16 - 8, 0, 32), 8)
    for n in range(8):
        even = (row + lane + n) % 2 == 0
        parts = []
        for p in (n, n + 8):
            parts.append(jnp.where(even, pick(v2r[p + 1, 8:40], idx), pick(v2b[p + 1, 8:40], idx)))
        c = jnp.where(valid, jnp.where(lane < 64, parts[0], parts[1]), 0.0)
        double_rows(tmp, c, 32)
        for p in (2 * n, 2 * n + 1):
            v1b[p + 1, 8:40] += tmp[pl.ds(window, 32)]
    seam(v1b, 32)
    index1 = [side_index(32, parity, 64) for parity in range(2)]
    for _ in range(2):
        update(v1r, v1b, c1r, index1, 0, 16, 32, 0)
        seam(v1r, 32)
        update(v1b, v1r, c1b, index1, 0, 16, 32, 1)
        seam(v1b, 32)

    for c in copies[3:]:
        c.wait()
    start = pl.multiple_of(gy * 16 - window, 8)
    cell = lane - jnp.where(lane < 96, 0, 128)
    idx = (cell // 2) % 64
    for n in range(-3, 11):
        plane = gx * 8 + n
        held = jnp.clip(plane, 0, 31)
        at_half = idx + 64 * (held // 16)
        even = (row + lane + n) % 2 == 0
        red = v1r[held % 16 + 1, pl.ds(start, 32)]
        black = v1b[held % 16 + 1, pl.ds(start, 32)]
        c = jnp.where(even, pick(red, at_half), pick(black, at_half))
        c = c * jnp.where((plane >= 0) & (plane < 32), 1.0, 0.0).astype(F32)
        tmp[64:96] = c
        double_rows(tmp, tmp[68:92], 24)
        for p in (2 * n + 8, 2 * n + 9):
            v0b[p + 1, 8:56] += tmp[0:48]
    index0 = [side_rule(48, parity) for parity in range(2)]
    update(v0r, v0b, c0r, index0, 4, 28, 48, 0, 4)
    update(v0b, v0r, c0b, index0, 4, 28, 48, 1, 4)
    update(v0r, v0b, c0r, index0, 6, 26, 48, 0, 4)
    update(v0b, v0r, c0b, index0, 6, 26, 48, 1, 4)

    def finish(p, parity):
        even = (row + lane + parity) % 2 == 0
        er, eb = defect(v0r, v0b, c0r, c0b, p, parity, index1_0, 32, 8, 4)
        res_ref[p - 8] = jnp.where(even, pick(er, lane // 2), pick(eb, lane // 2))
        red, black = v0r[p + 1, 16:48], v0b[p + 1, 16:48]
        u_ref[p - 8] = jnp.where(even, pick(red, lane // 2), pick(black, lane // 2))

    index1_0 = [side_rule(32, parity) for parity in range(2)]
    pairs(8, 24, finish, 32)


def around(lo, hi, axis):
    count = lax.axis_size(axis)
    from_above = lax.ppermute(lo, axis, [((i + 1) % count, i) for i in range(count)])
    from_below = lax.ppermute(hi, axis, [(i, (i + 1) % count) for i in range(count)])
    return from_below, from_above


def beyond(x, axis):
    count = lax.axis_size(axis)
    return [lax.ppermute(x, axis, [(i, (i + d) % count) for i in range(count)]) for d in range(1, count)]


def body(source, conductance):
    vmem, smem, hbm = (pl.BlockSpec(memory_space=m) for m in (pltpu.VMEM, pltpu.SMEM, pltpu.HBM))
    at = jnp.stack([lax.axis_index(a) for a in ("gx", "gy", "gz")]).astype(jnp.int32)
    dma = pltpu.SemaphoreType.DMA

    block, x_slab = arr(16, 32, 128), arr(17, 32, 128)
    wf, wb, lo, hi, b1 = call(
        split_fine,
        [(block, block, x_slab, x_slab, arr(64, 128))],
        (jnp.concatenate([source, conductance]),),
        None,
        [pltpu.VMEM((32, 128), F32)],
        8,
    )
    xl, xu = around(lo, hi, "gx")
    b1 = [b1] + beyond(b1, "gy")
    y_slab = arr(66, 8, 128)
    lo, hi, b1 = call(pack_rows, [(y_slab, y_slab, arr(4, 64, 128))], (wf, wb, xl, xu, *b1), limit=8)
    yl, yu = around(lo, hi, "gy")
    yl, yu, *b1 = lax.optimization_barrier((yl, yu, b1, *beyond(b1, "gx")))
    lo, hi = call(pack_lanes, [(arr(96, 8, 128),) * 2], (wf, wb, xl, xu, yl, yu), limit=8)
    zl, zu = around(lo, hi, "gz")

    colour0 = pltpu.VMEM((34, 64, 128), F32)
    right0 = pltpu.VMEM((32, 48, 128), F32)
    coef0 = pltpu.VMEM((8, 32, 48, 128), F32)
    state0 = (arr(8, 24, 48, 128), arr(9, 26, 48, 128))
    g, c0r, c0b = call(
        fine_down,
        [(arr(16, 128, 128),) + state0, (vmem, hbm, hbm)],
        (at, wf, wb, xl, xu, yl, yu, zl, zu),
        [smem] + [vmem] * 8,
        [colour0, colour0, right0, right0, coef0, coef0, colour0, colour0, pltpu.VMEM((32, 128), F32), dma((3,))],
        LIMIT_FINE,
    )
    g = lax.all_to_all(g, ("gx", "gy"), 0, 0, tiled=True)

    state1 = (arr(2, 8, 16, 32, 128), arr(18, 32, 128))
    colour1 = pltpu.VMEM((18, 80, 128), F32)
    right1 = pltpu.VMEM((16, 64, 128), F32)
    coef1 = pltpu.VMEM((8, 16, 64, 128), F32)
    w2, c1, v1b = call(
        mid_down,
        [(arr(8, 32, 128),) + state1, (vmem, hbm, hbm)],
        (at, g, *b1),
        [smem] + [vmem] * 5,
        [colour1, colour1, right1, right1, coef1, coef1, colour1, colour1, pltpu.VMEM((64, 128), F32), dma((3,))],
        LIMIT_MID,
    )
    mine = [w2] + [lax.ppermute(w2, "gz", [(i, (i + d) % 8) for i in range(8)]) for d in (2, 4, 6)]
    swap = [(i, i ^ 1) for i in range(8)]
    near, *mine = lax.optimization_barrier((lax.ppermute(w2, "gz", swap), *mine))
    pair = [near, lax.ppermute(jnp.concatenate(mine[1:]), "gz", swap)]

    scratch = []
    for planes, rows in ((16, 32), (8, 16), (4, 8)):
        scratch += level_scratch(planes, rows) + [pltpu.VMEM((2, planes, rows, 128), F32)]
    scratch += [pltpu.VMEM((18, 48, 128), F32)] * 2 + [pltpu.VMEM((8, 16, 32, 128), F32)] * 2
    scratch += [colour0] * 2 + [pltpu.VMEM((8, 24, 48, 128), F32)] * 2
    scratch += [pltpu.VMEM((96, 128), F32), dma((6,))]
    return call(
        coarse_up,
        [(block, block)],
        (at, *mine, *pair, c1, v1b, c0r, c0b),
        [smem] + [vmem] * 6 + [hbm] * 4,
        scratch,
        LIMIT_UP,
    )


def solution(mesh):
    placed = (P("gx", "gy", "gz"), P("gx", "gy", "gz"))
    return jax.shard_map(body, mesh=mesh, in_specs=placed, out_specs=placed, check_vma=False)
```

```python
import functools

import jax
import jax.numpy as jnp
from jax import lax
from jax.experimental import pallas as pl
from jax.experimental.pallas import tpu as pltpu
from jax.sharding import PartitionSpec as P

F32 = jnp.float32
COARSE_ITERS = 20
MIB = 1 << 20
GROUP = 64
LIMIT_FINE = 50
LIMIT_MID = 50
LIMIT_UP = 50


def lanes(rows):
    return lax.broadcasted_iota(jnp.int32, (rows, 128), 1)


def sublanes(rows):
    return lax.broadcasted_iota(jnp.int32, (rows, 128), 0)


def pick(x, idx):
    return jnp.take_along_axis(x, idx, axis=1, mode="promise_in_bounds")


def turn(x, shift):
    shift = shift % 128
    return pltpu.roll(x, shift, 1) if shift else x


def side_index(rows, parity, period):
    lane, row = lanes(rows), sublanes(rows)
    step = 2 * ((row + parity) % 2) - 1
    within = (lane % period + step + period) % period
    return lane - lane % period + within


def side_rule(rows, parity):
    return (sublanes(rows) + parity) % 2 == 0


def beside(x, rule):
    if rule.dtype == jnp.bool_:
        return jnp.where(rule, pltpu.roll(x, 1, 1), pltpu.roll(x, 127, 1))
    return pick(x, rule)


def call(kernel, out, args, specs=None, scratch=(), limit=40):
    vmem = pl.BlockSpec(memory_space=pltpu.VMEM)
    return pl.pallas_call(
        kernel,
        out_shape=out[0],
        in_specs=specs or [vmem] * len(args),
        out_specs=out[1] if len(out) > 1 else jax.tree.map(lambda _: vmem, out[0]),
        scratch_shapes=scratch,
        compiler_params=pltpu.CompilerParams(vmem_limit_bytes=limit * MIB),
        name=kernel.__name__,
    )(*args)


def arr(*shape):
    return jax.ShapeDtypeStruct(shape, F32)


def split_fine(both_ref, wf_ref, wb_ref, lo_ref, hi_ref, b1_ref, tmp):
    lane, row = lanes(32), sublanes(32)
    index = []
    for parity in range(2):
        odd = (row + parity) % 2
        index.append(2 * (lane % 64) + jnp.where(lane < 64, odd, 1 - odd))
    lane16, row16 = lanes(16), sublanes(16)
    own = []
    for n in range(8):
        w = [pick(both_ref[16 + 2 * n + parity], index[parity]) for parity in range(2)]
        for parity in range(2):
            i = 2 * n + parity
            wb_ref[i] = w[parity]
            if i < 9:
                lo_ref[8 + i] = w[parity]
            if i > 6:
                hi_ref[1 + i] = w[parity]
        both = w[0] + w[1]
        odd = (row16 + n) % 2
        cell = 2 * (lane16 % 32) + jnp.where(lane16 % 64 < 32, odd, 1 - odd)
        own.append(pick(halve_rows(tmp, both + turn(both, 64), 32), cell))
    for n in range(4):
        b1_ref[16 * n : 16 * n + 16] = jnp.where(lane16 < 64, own[n], own[n + 4])
    for i in range(16):
        wf = pick(both_ref[i], index[i % 2])
        wf_ref[i] = wf
        if i < 8:
            lo_ref[i] = wf
        else:
            hi_ref[i - 8] = wf


def by_colour(n, swap):
    lane, row = lanes(16), sublanes(16)
    odd = (row + n) % 2
    return (2 * (lane % 64) + jnp.where((lane < 64) != swap, odd, 1 - odd)) % 128


def spared(index):
    return (index + jnp.where(lanes(16) % 64 < 48, -12, 12)) % 128


def plane_f(wf, xl, xu, p):
    return xl.at[p] if p < 8 else wf.at[p - 8] if p < 24 else xu.at[p - 24]


def plane_b(wb, xl, xu, p):
    return xl.at[9 + p] if p < 8 else wb.at[p - 8] if p < 24 else xu.at[8 + p - 24]


def pack_rows(wf, wb, xl, xu, b0, b1, b2, b3, lo_ref, hi_ref, b1_ref):
    for back, b in enumerate((b0, b1, b2, b3)):
        b1_ref[back] = b[...]
    for p in range(32):
        f, b = plane_f(wf, xl, xu, p), plane_b(wb, xl, xu, p)
        lo_ref[p] = f[0:8]
        hi_ref[p] = f[24:32]
        lo_ref[32 + p] = b[0:8]
        hi_ref[32 + p] = b[24:32]
    for i in range(16):
        lo_ref[64 + i // 8, i % 8 : i % 8 + 1] = wb[i, 8:9]
        hi_ref[64 + i // 8, i % 8 : i % 8 + 1] = wb[i, 23:24]


def slab(plane, yl, yu, which, p):
    return jnp.concatenate([yl[32 * which + p], plane[...], yu[32 * which + p]], axis=0)


def pack_lanes(wf, wb, xl, xu, yl, yu, lo_ref, hi_ref):
    slot_of = lanes(48) % 64
    for which, width, base in ((0, 16, 0), (1, 16, 48)):
        count = 64 // width
        slot = slot_of // width
        for group in range(32 // count):
            for s in range(count):
                p = group * count + s
                plane = plane_b(wb, xl, xu, p) if which else plane_f(wf, xl, xu, p)
                v = turn(slab(plane, yl, yu, which, p), width * s)
                if s == 0:
                    low = high = v
                else:
                    low = jnp.where(slot == s, v, low)
                    high = jnp.where(slot == s - 1, v, high)
            start = base + 6 * group
            lo_ref[start : start + 6] = low.reshape(6, 8, 128)
            hi_ref[start : start + 6] = high.reshape(6, 8, 128)


def make_coefs(mine, other, f, coef, p, index, scale, rows, inside=None):
    r = slice(8, 8 + rows)
    centre = mine[p + 1, r]
    mid = other[p + 1, r]
    side = beside(mid, index)
    if inside is not None:
        side = jnp.where(inside, side, 0.0)
    others = (other[p, r], other[p + 2, r], other[p + 1, 7 : 7 + rows], other[p + 1, 9 : 9 + rows], mid, side)
    weights = [centre + b for b in others]
    total = weights[0]
    for w in weights[1:]:
        total = total + w
    inverse = jnp.where(centre > 0.0, 1.0 / jnp.where(centre > 0.0, total, 1.0), 0.0)
    for which in range(6):
        w = weights[which] * inverse
        if which == 5 and inside is not None:
            w = jnp.where(inside, w, 0.0)
        coef[which, p] = w
    coef[6, p] = f * (inverse * (2.0 / scale))
    coef[7, p] = total * (0.5 * scale)


def relaxed(other, coef, p, index, rows, first=0, shift=0):
    a = 8 + first
    r = slice(a, a + rows)
    c = slice(first, first + rows)
    q = p - shift
    mid = other[p + 1, r]
    out = coef[6, q, c] + coef[0, q, c] * other[p, r]
    out = out + coef[1, q, c] * other[p + 2, r]
    out = out + coef[2, q, c] * other[p + 1, a - 1 : a - 1 + rows]
    out = out + coef[3, q, c] * other[p + 1, a + 1 : a + 1 + rows]
    out = out + coef[4, q, c] * mid
    return out + coef[5, q, c] * beside(mid, index)


def pairs(start, stop, body, rows):
    count = stop - start
    most = 8 * GROUP if rows < 64 else 16 * GROUP
    width = max(w for w in (2, 4, 8, 16) if w == 2 or (count % w == 0 and w * rows <= most))

    def step(t, carry):
        for n in range(width):
            body(start + t * width + n, n % 2)
        return carry

    if count == width:
        step(0, 0)
    else:
        lax.fori_loop(0, count // width, step, 0)


def update(mine, other, coef, index, start, stop, rows, flip, shift=0):
    def body(p, parity):
        mine[p + 1, 8 : 8 + rows] = relaxed(other, coef, p, index[(parity + flip) % 2], rows, 0, shift)

    pairs(start, stop, body, rows)


def defect(red, black, cr, cb, p, parity, index, rows, first=0, shift=0):
    r = slice(8 + first, 8 + first + rows)
    c = slice(first, first + rows)
    er = cr[7, p - shift, c] * (relaxed(black, cr, p, index[parity], rows, first, shift) - red[p + 1, r])
    eb = cb[7, p - shift, c] * (relaxed(red, cb, p, index[1 - parity], rows, first, shift) - black[p + 1, r])
    return er, eb


def halve_rows(tmp, value, rows):
    tmp[0:rows] = value
    return 0.125 * (tmp[pl.ds(0, rows // 2, 2)] + tmp[pl.ds(1, rows // 2, 2)])


def double_rows(tmp, value, rows):
    tmp[pl.ds(0, rows, 2)] = value
    tmp[pl.ds(1, rows, 2)] = value


def fine_down(
    at, wf, wb, xl, xu, yl, yu, zl, zu, g_ref, cr_out, cb_out, br, bb, fr, fb, cr, cb, vr, vb, tmp, sems
):
    gx, gy, gz = at[0], at[1], at[2]
    lane, row = lanes(48), sublanes(48)
    own = lane < 64
    keep = own | ((lane < 96) & (gz < 7)) | ((lane >= 96) & (gz > 0))
    keep = keep & ((row >= 8) | (gy > 0)) & ((row < 40) | (gy < 3))
    kept = jnp.where(keep, 1.0, 0.0).astype(F32)
    below = jnp.where(gx > 0, 1.0, 0.0).astype(F32)
    above = jnp.where(gx < 3, 1.0, 0.0).astype(F32)
    left = jnp.where(gy > 0, 1.0, 0.0).astype(F32)
    right = jnp.where(gy < 3, 1.0, 0.0).astype(F32)
    vr[...] = jnp.zeros_like(vr)
    vb[...] = jnp.zeros_like(vb)
    edge = jnp.zeros((8, 128), F32)
    for b in (br, bb):
        for q in range(34):
            b[q, 0:8] = edge
            b[q, 56:64] = edge
        for q in (0, 33):
            b[q, 8:56] = jnp.zeros((48, 128), F32)
    for which, width, base in ((0, 16, 0), (1, 16, 48)):
        count = 64 // width
        slot = (lane % 64) // width
        for p in range(32):
            plane = plane_b(wb, xl, xu, p) if which else plane_f(wf, xl, xu, p)
            w = slab(plane, yl, yu, which, p)
            s = p % count
            start = base + 6 * (p // count)
            up = zu[start : start + 6].reshape(48, 128)
            low = zl[start : start + 6].reshape(48, 128)
            both = jnp.where(slot == s, up, low)
            red = jnp.where(own, w, turn(both, 64 - width * s))
            black = jnp.where(own, turn(w, 64), turn(both, -width * s))
            if which:
                k = kept * below if p < 8 else kept * above if p >= 24 else kept
                br[p + 1, 8:56] = red * k
                bb[p + 1, 8:56] = black * k
            else:
                fr[p] = red
                fb[p] = black
    for a in range(2):
        for src, r, ok in ((yl, 7, left), (yu, 56, right)):
            v = src[64 + a] * ok
            t = turn(v, 64)
            for s in range(8):
                br[9 + 8 * a + s, r : r + 1] = v[s : s + 1]
                bb[9 + 8 * a + s, r : r + 1] = t[s : s + 1]
    for v, q in ((xl[8] * below, 0), (xu[16] * above, 33)):
        br[q, 16:48] = v
        bb[q, 16:48] = turn(v, 64)

    index = [side_rule(48, parity) for parity in range(2)]

    def coefs(p, parity):
        make_coefs(br, bb, fr[p], cr, p, index[parity], 1.0, 48)
        make_coefs(bb, br, fb[p], cb, p, index[1 - parity], 1.0, 48)
        vr[p + 1, 8:56] = cr[6, p]

    pairs(0, 32, coefs, 48)
    copies = [
        pltpu.make_async_copy(cr.at[:, pl.ds(4, 24)], cr_out, sems.at[0]),
        pltpu.make_async_copy(cb.at[:, pl.ds(3, 26)], cb_out.at[pl.ds(0, 8)], sems.at[1]),
        pltpu.make_async_copy(vb.at[pl.ds(4, 26), pl.ds(8, 48)], cb_out.at[8], sems.at[2]),
    ]
    copies[0].start()
    copies[1].start()
    update(vb, vr, cb, index, 0, 32, 48, 1)
    update(vr, vb, cr, index, 2, 30, 48, 0)
    update(vb, vr, cb, index, 2, 30, 48, 1)
    copies[2].start()
    inner = [side_rule(32, parity) for parity in range(2)]
    swap = gx >= 2
    lane16 = lanes(16)
    spare = (lane16 % 64 >= 38) & (lane16 % 64 < 58)
    for n in range(8):
        total = coarse = None
        for parity in range(2):
            p = 8 + 2 * n + parity
            er, eb = defect(vr, vb, cr, cb, p, parity, inner, 32, 8)
            b = br[p + 1, 16:48] + bb[p + 1, 16:48]
            total = er + eb if total is None else total + (er + eb)
            coarse = b if coarse is None else coarse + b
        f1 = pick(halve_rows(tmp, total, 32), by_colour(n, swap))
        b1 = halve_rows(tmp, coarse, 32)
        w1 = jnp.where(spare, pick(b1, spared(by_colour(n, swap))), f1)
        for copy in range(16):
            g_ref[copy, 16 * n : 16 * n + 16] = w1
    for c in copies:
        c.wait()


def across(g, a, start):
    r = slice(start, start + 16)
    return jnp.concatenate([g[4 * a + y, r] for y in range(4)], axis=0)


def joined_f(g, p):
    wa, wb = (across(g, p // 8 + up, 16 * (p % 8)) for up in (0, 2))
    half = lanes(64) < 64
    return jnp.where(half, wa, wb), turn(jnp.where(half, wb, wa), 64)


def across_b(gx, gy, held, a, n):
    back = (gx - a + 4) % 4
    r = slice(16 * n, 16 * n + 16)
    out = []
    for y in range(4):
        e = (gy - y + 4) % 4
        v = held[0][e, r]
        for d in range(1, 4):
            v = jnp.where(back == d, held[d][e, r], v)
        out.append(v)
    return jnp.concatenate(out, axis=0)


def joined_b(gx, gy, held, a, n):
    wa, wb = (across_b(gx, gy, held, a + up, n) for up in (0, 2))
    half = lanes(64) < 64
    reds = jnp.where(half, wa, turn(wb, 64)), jnp.where(half, turn(wa, 64), wb)
    return [(red, turn(red, -32)) for red in reds]


def seam(v, rows):
    r = slice(8, 8 + rows)
    half = lanes(rows) < 64
    v[0, r] = jnp.where(half, 0.0, turn(v[16, r], 64))
    v[17, r] = jnp.where(half, turn(v[1, r], 64), 0.0)


def mid_down(at, g, h0, h1, h2, h3, w2_ref, c_out, vb_out, br, bb, fr, fb, cr, cb, vr, vb, tmp, sems):
    gx, gy, gz = at[0], at[1], at[2]
    lane = lanes(64)
    own = lane % 64 < 32
    keep = own | ((lane % 64 < 48) & (gz < 7)) | ((lane % 64 >= 48) & (gz > 0))
    kept = jnp.where(keep, 1.0, 0.0).astype(F32)
    halo = (lane + jnp.where(lane % 64 < 48, 6, -6)) % 128
    for v in (vr, vb):
        v[...] = jnp.zeros_like(v)
    for b in (br, bb):
        b[:, 0:8] = jnp.zeros((18, 8, 128), F32)
        b[:, 72:80] = jnp.zeros((18, 8, 128), F32)
    for p in range(16):
        fr[p], fb[p] = joined_f(g, p)
    for a in range(2):
        for n in range(4):
            for up, (red, black) in enumerate(joined_b(gx, gy, (h0, h1, h2, h3), a, n)):
                p = 8 * a + n + 4 * up
                br[p + 1, 8:72] = kept * jnp.where(own, red, pick(fr[p], halo))
                bb[p + 1, 8:72] = kept * jnp.where(own, black, pick(fb[p], halo))
    seam(br, 64)
    seam(bb, 64)
    index = [side_index(64, parity, 64) for parity in range(2)]

    def coefs(p, parity):
        make_coefs(br, bb, fr[p], cr, p, index[parity], 0.25, 64)
        make_coefs(bb, br, fb[p], cb, p, index[1 - parity], 0.25, 64)
        vr[p + 1, 8:72] = cr[6, p]

    pairs(0, 16, coefs, 64)
    seam(vr, 64)
    window = pl.multiple_of(jnp.clip(gy * 16 - 8, 0, 32), 8)
    copies = [
        pltpu.make_async_copy(cr.at[:, :, pl.ds(window, 32)], c_out.at[0], sems.at[0]),
        pltpu.make_async_copy(cb.at[:, :, pl.ds(window, 32)], c_out.at[1], sems.at[1]),
        pltpu.make_async_copy(vb.at[:, pl.ds(window + 8, 32)], vb_out, sems.at[2]),
    ]
    copies[0].start()
    copies[1].start()
    update(vb, vr, cb, index, 0, 16, 64, 1)
    seam(vb, 64)
    update(vr, vb, cr, index, 0, 16, 64, 0)
    seam(vr, 64)
    update(vb, vr, cb, index, 0, 16, 64, 1)
    seam(vb, 64)
    copies[2].start()
    lane, row = lanes(32), sublanes(32)
    for n in range(8):
        total = coarse = None
        for parity in range(2):
            p = 2 * n + parity
            er, eb = defect(vr, vb, cr, cb, p, parity, index, 64)
            e = er + eb
            b = br[p + 1, 8:72] + bb[p + 1, 8:72]
            total = e if total is None else total + e
            coarse = b if coarse is None else coarse + b
        f2 = halve_rows(tmp, total, 64)
        b2 = halve_rows(tmp, coarse, 64)
        odd = (row + n) % 2
        idx = 64 * ((lane % 64) // 32) + 2 * (lane % 16) + jnp.where(lane % 32 < 16, odd, 1 - odd)
        w2 = jnp.where(lane < 64, pick(f2, idx), pick(b2, idx))
        w2_ref[n] = w2
    for c in copies:
        c.wait()


def transposed(blocks):
    slot = lanes(32) // 16
    for bit in (1, 2, 4):
        out = list(blocks)
        for i in range(8):
            if not i & bit:
                x, y = blocks[i], blocks[i + bit]
                out[i] = jnp.where(slot & bit == 0, x, turn(y, 16 * bit))
                out[i + bit] = jnp.where(slot & bit == 0, turn(x, -16 * bit), y)
        blocks = out
    return blocks


def level_scratch(planes, rows):
    return [pltpu.VMEM((planes + 2, rows + 16, 128), F32)] * 4 + [pltpu.VMEM((8, planes, rows, 128), F32)] * 2


def clear(refs):
    for v in refs:
        v[...] = jnp.zeros_like(v)


def smooth_down(br, bb, vr, vb, cr, cb, f_of, index, scale, planes, rows, inside):
    def coefs(p, parity):
        fr, fb = f_of(p)
        make_coefs(br, bb, fr, cr, p, index[parity], scale, rows, inside and inside[parity])
        make_coefs(bb, br, fb, cb, p, index[1 - parity], scale, rows, inside and inside[1 - parity])
        vr[p + 1, 8 : 8 + rows] = cr[6, p]

    pairs(0, planes, coefs, rows)
    update(vb, vr, cb, index, 0, planes, rows, 1)
    update(vr, vb, cr, index, 0, planes, rows, 0)
    update(vb, vr, cb, index, 0, planes, rows, 1)


def smooth_up(vr, vb, cr, cb, index, planes, rows):
    for _ in range(2):
        update(vr, vb, cr, index, 0, planes, rows, 0)
        update(vb, vr, cb, index, 0, planes, rows, 1)


def restrict(level, tmp, index, planes, rows, cells, put):
    br, bb, vr, vb, cr, cb = level
    lane, row = lanes(rows // 2), sublanes(rows // 2)
    for n in range(planes // 2):
        total = coarse = None
        for parity in range(2):
            p = 2 * n + parity
            er, eb = defect(vr, vb, cr, cb, p, parity, index, rows)
            b = br[p + 1, 8 : 8 + rows] + bb[p + 1, 8 : 8 + rows]
            total = er + eb if total is None else total + (er + eb)
            coarse = b if coarse is None else coarse + b
        f = halve_rows(tmp, total, rows)
        b = halve_rows(tmp, coarse, rows)
        odd = (row + n) % 2
        red = 2 * (lane % 64) + odd
        black = 2 * (lane % 64) + 1 - odd
        inside = lane < cells
        put(n, *[jnp.where(inside, pick(x, i), 0.0) for x in (f, b) for i in (red, black)])


def prolong(vr, vb, out, tmp, planes, rows):
    lane, row = lanes(rows), sublanes(rows)
    r = slice(8, 8 + rows)
    for n in range(planes):
        even = (row + lane + n) % 2 == 0
        c = jnp.where(even, pick(vr[n + 1, r], lane // 2), pick(vb[n + 1, r], lane // 2))
        double_rows(tmp, c, rows)
        for p in (2 * n, 2 * n + 1):
            out[p + 1, 8 : 8 + 2 * rows] += tmp[0 : 2 * rows]


def coarse_up(
    at, m0, m1, m2, m3, q0, q1, q2, q3, c1_in, v1b_in, c0r_in, c0b_in, u_ref, res_ref,
    b2r, b2b, v2r, v2b, c2r, c2b, f2,
    b3r, b3b, v3r, v3b, c3r, c3b, f3,
    b4r, b4b, v4r, v4b, c4r, c4b, f4,
    v1r, v1b, c1r, c1b, v0r, v0b, c0r, c0b, tmp, sems,
):
    gx, gy, gz = at[0], at[1], at[2]
    copies = [
        pltpu.make_async_copy(c1_in.at[0], c1r, sems.at[0]),
        pltpu.make_async_copy(c1_in.at[1], c1b, sems.at[1]),
        pltpu.make_async_copy(v1b_in, v1b.at[:, pl.ds(8, 32)], sems.at[2]),
        pltpu.make_async_copy(c0r_in, c0r, sems.at[3]),
        pltpu.make_async_copy(c0b_in.at[pl.ds(0, 8), pl.ds(1, 24)], c0b, sems.at[4]),
        pltpu.make_async_copy(c0b_in.at[8], v0b.at[pl.ds(4, 26), pl.ds(8, 48)], sems.at[5]),
    ]
    for c in copies:
        c.start()
    clear((b2r, b2b, v2r, v2b, b3r, b3b, v3r, v3b, b4r, b4b, v4r, v4b, v1r, v0r))
    v0b[:, 0:8] = jnp.zeros((34, 8, 128), F32)
    v0b[:, 56:64] = jnp.zeros((34, 8, 128), F32)
    v1b[:, 0:8] = jnp.zeros((18, 8, 128), F32)
    v1b[:, 40:48] = jnp.zeros((18, 8, 128), F32)

    chip = gz // 2
    first = gz % 2 == 0
    for n in range(8):
        near = [(jnp.where(first, a[n], b[n]), jnp.where(first, b[n], a[n])) for a, b in ((m0, q0), (m1, q1), (m2, q2), (m3, q3))]
        blocks = []
        for c in range(4):
            for core in range(2):
                v = near[0][core]
                for back in range(1, 4):
                    v = jnp.where(chip == (c + back) % 4, near[back][core], v)
                blocks.append(v)
        out = transposed(blocks)
        for h in range(2):
            p = n + 8 * h
            f2[0, p] = out[2 * h]
            f2[1, p] = out[2 * h + 1]
            b2r[p + 1, 8:40] = out[4 + 2 * h]
            b2b[p + 1, 8:40] = out[5 + 2 * h]
    lane = lanes(32)
    index2 = [side_rule(32, parity) for parity in range(2)]
    inside2 = [lane != jnp.where(index2[parity], 0, 127) for parity in range(2)]
    smooth_down(b2r, b2b, v2r, v2b, c2r, c2b, lambda p: (f2[0, p], f2[1, p]), index2, 0.25**2, 16, 32, inside2)

    def put3(n, fr, fb, br, bb):
        f3[0, n], f3[1, n] = fr, fb
        b3r[n + 1, 8:24], b3b[n + 1, 8:24] = br, bb

    restrict((b2r, b2b, v2r, v2b, c2r, c2b), tmp, index2, 16, 32, 64, put3)

    index3 = [side_rule(16, parity) for parity in range(2)]
    smooth_down(b3r, b3b, v3r, v3b, c3r, c3b, lambda p: (f3[0, p], f3[1, p]), index3, 0.25**3, 8, 16, None)

    def put4(n, fr, fb, br, bb):
        f4[0, n], f4[1, n] = fr, fb
        b4r[n + 1, 8:16], b4b[n + 1, 8:16] = br, bb

    restrict((b3r, b3b, v3r, v3b, c3r, c3b), tmp, index3, 8, 16, 32, put4)

    index4 = [side_rule(8, parity) for parity in range(2)]

    for p in range(4):
        make_coefs(b4r, b4b, f4[0, p], c4r, p, index4[p % 2], 0.25**4, 8)
        make_coefs(b4b, b4r, f4[1, p], c4b, p, index4[1 - p % 2], 0.25**4, 8)
    row8 = sublanes(8)
    inner = (row8 > 0, row8 < 7)
    cr4 = [[c4r[w, p] for w in range(7)] for p in range(4)]
    cb4 = [[c4b[w, p] for w in range(7)] for p in range(4)]
    for c in cr4 + cb4:
        c[2] = jnp.where(inner[0], c[2], 0.0)
        c[3] = jnp.where(inner[1], c[3], 0.0)

    def half(other, coefs, flip):
        out = []
        for p in range(4):
            c, v = coefs[p], other[p]
            w = c[6] + c[4] * v
            if p > 0:
                w = w + c[0] * other[p - 1]
            if p < 3:
                w = w + c[1] * other[p + 1]
            w = w + c[2] * pltpu.roll(v, 1, 0) + c[3] * pltpu.roll(v, 7, 0)
            out.append(w + c[5] * beside(v, index4[(p + flip) % 2]))
        return out

    def coarse_step(count, state):
        black = list(state)
        red = half(black, cr4, 0)
        return tuple(half(red, cb4, 1))

    black = lax.fori_loop(0, COARSE_ITERS - 1, coarse_step, (jnp.zeros((8, 128), F32),) * 4)
    red = half(black, cr4, 0)
    black = half(red, cb4, 1)
    for p in range(4):
        v4r[p + 1, 8:16] = red[p]
        v4b[p + 1, 8:16] = black[p]

    prolong(v4r, v4b, v3b, tmp, 4, 8)
    smooth_up(v3r, v3b, c3r, c3b, index3, 8, 16)
    prolong(v3r, v3b, v2b, tmp, 8, 16)
    smooth_up(v2r, v2b, c2r, c2b, index2, 16, 32)

    for c in copies[:3]:
        c.wait()
    lane, row = lanes(32), sublanes(32)
    near = lane % 64 - jnp.where(lane % 64 < 48, 0, 64)
    cell = gz * 32 + near
    valid = (cell >= 0) & (cell < 256)
    idx = jnp.clip(cell, 0, 255) // 2
    window = pl.multiple_of(jnp.clip(gy * 16 - 8, 0, 32), 8)
    for n in range(8):
        even = (row + lane + n) % 2 == 0
        parts = []
        for p in (n, n + 8):
            parts.append(jnp.where(even, pick(v2r[p + 1, 8:40], idx), pick(v2b[p + 1, 8:40], idx)))
        c = jnp.where(valid, jnp.where(lane < 64, parts[0], parts[1]), 0.0)
        double_rows(tmp, c, 32)
        for p in (2 * n, 2 * n + 1):
            v1b[p + 1, 8:40] += tmp[pl.ds(window, 32)]
    seam(v1b, 32)
    index1 = [side_index(32, parity, 64) for parity in range(2)]
    for _ in range(2):
        update(v1r, v1b, c1r, index1, 0, 16, 32, 0)
        seam(v1r, 32)
        update(v1b, v1r, c1b, index1, 0, 16, 32, 1)
        seam(v1b, 32)

    for c in copies[3:]:
        c.wait()
    start = pl.multiple_of(gy * 16 - window, 8)
    cell = lane - jnp.where(lane < 96, 0, 128)
    idx = (cell // 2) % 64
    for n in range(-3, 11):
        plane = gx * 8 + n
        held = jnp.clip(plane, 0, 31)
        at_half = idx + 64 * (held // 16)
        even = (row + lane + n) % 2 == 0
        red = v1r[held % 16 + 1, pl.ds(start, 32)]
        black = v1b[held % 16 + 1, pl.ds(start, 32)]
        c = jnp.where(even, pick(red, at_half), pick(black, at_half))
        c = c * jnp.where((plane >= 0) & (plane < 32), 1.0, 0.0).astype(F32)
        tmp[64:96] = c
        double_rows(tmp, tmp[68:92], 24)
        for p in (2 * n + 8, 2 * n + 9):
            v0b[p + 1, 8:56] += tmp[0:48]
    index0 = [side_rule(48, parity) for parity in range(2)]
    update(v0r, v0b, c0r, index0, 4, 28, 48, 0, 4)
    update(v0b, v0r, c0b, index0, 4, 28, 48, 1, 4)
    update(v0r, v0b, c0r, index0, 6, 26, 48, 0, 4)
    update(v0b, v0r, c0b, index0, 6, 26, 48, 1, 4)

    def finish(p, parity):
        even = (row + lane + parity) % 2 == 0
        er, eb = defect(v0r, v0b, c0r, c0b, p, parity, index1_0, 32, 8, 4)
        res_ref[p - 8] = jnp.where(even, pick(er, lane // 2), pick(eb, lane // 2))
        red, black = v0r[p + 1, 16:48], v0b[p + 1, 16:48]
        u_ref[p - 8] = jnp.where(even, pick(red, lane // 2), pick(black, lane // 2))

    index1_0 = [side_rule(32, parity) for parity in range(2)]
    pairs(8, 24, finish, 32)


def around(lo, hi, axis):
    count = lax.axis_size(axis)
    from_above = lax.ppermute(lo, axis, [((i + 1) % count, i) for i in range(count)])
    from_below = lax.ppermute(hi, axis, [(i, (i + 1) % count) for i in range(count)])
    return from_below, from_above


def beyond(x, axis):
    count = lax.axis_size(axis)
    return [lax.ppermute(x, axis, [(i, (i + d) % count) for i in range(count)]) for d in range(1, count)]


def body(source, conductance):
    vmem, smem, hbm = (pl.BlockSpec(memory_space=m) for m in (pltpu.VMEM, pltpu.SMEM, pltpu.HBM))
    at = jnp.stack([lax.axis_index(a) for a in ("gx", "gy", "gz")]).astype(jnp.int32)
    dma = pltpu.SemaphoreType.DMA

    block, x_slab = arr(16, 32, 128), arr(17, 32, 128)
    wf, wb, lo, hi, b1 = call(
        split_fine,
        [(block, block, x_slab, x_slab, arr(64, 128))],
        (jnp.concatenate([source, conductance]),),
        None,
        [pltpu.VMEM((32, 128), F32)],
        8,
    )
    xl, xu = around(lo, hi, "gx")
    b1 = [b1] + beyond(b1, "gy")
    y_slab = arr(66, 8, 128)
    lo, hi, b1 = call(pack_rows, [(y_slab, y_slab, arr(4, 64, 128))], (wf, wb, xl, xu, *b1), limit=8)
    yl, yu = around(lo, hi, "gy")
    b1 = [b1] + beyond(b1, "gx")
    lo, hi = call(pack_lanes, [(arr(96, 8, 128),) * 2], (wf, wb, xl, xu, yl, yu), limit=8)
    zl, zu = around(lo, hi, "gz")
    zl, zu, *b1 = lax.optimization_barrier((zl, zu, *b1))

    colour0 = pltpu.VMEM((34, 64, 128), F32)
    right0 = pltpu.VMEM((32, 48, 128), F32)
    coef0 = pltpu.VMEM((8, 32, 48, 128), F32)
    state0 = (arr(8, 24, 48, 128), arr(9, 26, 48, 128))
    g, c0r, c0b = call(
        fine_down,
        [(arr(16, 128, 128),) + state0, (vmem, hbm, hbm)],
        (at, wf, wb, xl, xu, yl, yu, zl, zu),
        [smem] + [vmem] * 8,
        [colour0, colour0, right0, right0, coef0, coef0, colour0, colour0, pltpu.VMEM((32, 128), F32), dma((3,))],
        LIMIT_FINE,
    )
    g = lax.all_to_all(g, ("gx", "gy"), 0, 0, tiled=True)

    state1 = (arr(2, 8, 16, 32, 128), arr(18, 32, 128))
    colour1 = pltpu.VMEM((18, 80, 128), F32)
    right1 = pltpu.VMEM((16, 64, 128), F32)
    coef1 = pltpu.VMEM((8, 16, 64, 128), F32)
    w2, c1, v1b = call(
        mid_down,
        [(arr(8, 32, 128),) + state1, (vmem, hbm, hbm)],
        (at, g, *b1),
        [smem] + [vmem] * 5,
        [colour1, colour1, right1, right1, coef1, coef1, colour1, colour1, pltpu.VMEM((64, 128), F32), dma((3,))],
        LIMIT_MID,
    )
    mine = [w2] + [lax.ppermute(w2, "gz", [(i, (i + d) % 8) for i in range(8)]) for d in (2, 4, 6)]
    pair = [lax.ppermute(w, "gz", [(i, i ^ 1) for i in range(8)]) for w in mine]

    scratch = []
    for planes, rows in ((16, 32), (8, 16), (4, 8)):
        scratch += level_scratch(planes, rows) + [pltpu.VMEM((2, planes, rows, 128), F32)]
    scratch += [pltpu.VMEM((18, 48, 128), F32)] * 2 + [pltpu.VMEM((8, 16, 32, 128), F32)] * 2
    scratch += [colour0] * 2 + [pltpu.VMEM((8, 24, 48, 128), F32)] * 2
    scratch += [pltpu.VMEM((96, 128), F32), dma((6,))]
    return call(
        coarse_up,
        [(block, block)],
        (at, *mine, *pair, c1, v1b, c0r, c0b),
        [smem] + [vmem] * 8 + [hbm] * 4,
        scratch,
        LIMIT_UP,
    )


def solution(mesh):
    placed = (P("gx", "gy", "gz"), P("gx", "gy", "gz"))
    return jax.shard_map(body, mesh=mesh, in_specs=placed, out_specs=placed, check_vma=False)
```

```python
import functools

import jax
import jax.numpy as jnp
from jax import lax
from jax.experimental import pallas as pl
from jax.experimental.pallas import tpu as pltpu
from jax.sharding import PartitionSpec as P

F32 = jnp.float32
COARSE_ITERS = 20
MIB = 1 << 20
GROUP = 64
LIMIT_FINE = 50
LIMIT_MID = 50
LIMIT_UP = 50


def lanes(rows):
    return lax.broadcasted_iota(jnp.int32, (rows, 128), 1)


def sublanes(rows):
    return lax.broadcasted_iota(jnp.int32, (rows, 128), 0)


def pick(x, idx):
    return jnp.take_along_axis(x, idx, axis=1, mode="promise_in_bounds")


def turn(x, shift):
    shift = shift % 128
    return pltpu.roll(x, shift, 1) if shift else x


def side_index(rows, parity, period):
    lane, row = lanes(rows), sublanes(rows)
    step = 2 * ((row + parity) % 2) - 1
    within = (lane % period + step + period) % period
    return lane - lane % period + within


def side_rule(rows, parity):
    return (sublanes(rows) + parity) % 2 == 0


def beside(x, rule):
    if rule.dtype == jnp.bool_:
        return jnp.where(rule, pltpu.roll(x, 1, 1), pltpu.roll(x, 127, 1))
    return pick(x, rule)


def call(kernel, out, args, specs=None, scratch=(), limit=40):
    vmem = pl.BlockSpec(memory_space=pltpu.VMEM)
    return pl.pallas_call(
        kernel,
        out_shape=out[0],
        in_specs=specs or [vmem] * len(args),
        out_specs=out[1] if len(out) > 1 else jax.tree.map(lambda _: vmem, out[0]),
        scratch_shapes=scratch,
        compiler_params=pltpu.CompilerParams(vmem_limit_bytes=limit * MIB),
        name=kernel.__name__,
    )(*args)


def arr(*shape):
    return jax.ShapeDtypeStruct(shape, F32)


def split_fine(both_ref, wf_ref, wb_ref, lo_ref, hi_ref, b1_ref, tmp):
    lane, row = lanes(32), sublanes(32)
    index = []
    for parity in range(2):
        odd = (row + parity) % 2
        index.append(2 * (lane % 64) + jnp.where(lane < 64, odd, 1 - odd))
    lane16, row16 = lanes(16), sublanes(16)
    own = []
    for n in range(8):
        w = [pick(both_ref[16 + 2 * n + parity], index[parity]) for parity in range(2)]
        for parity in range(2):
            i = 2 * n + parity
            wb_ref[i] = w[parity]
            if i < 9:
                lo_ref[8 + i] = w[parity]
            if i > 6:
                hi_ref[1 + i] = w[parity]
        both = w[0] + w[1]
        odd = (row16 + n) % 2
        cell = 2 * (lane16 % 32) + jnp.where(lane16 % 64 < 32, odd, 1 - odd)
        own.append(pick(halve_rows(tmp, both + turn(both, 64), 32), cell))
    for n in range(4):
        b1_ref[16 * n : 16 * n + 16] = jnp.where(lane16 < 64, own[n], own[n + 4])
    for i in range(16):
        wf = pick(both_ref[i], index[i % 2])
        wf_ref[i] = wf
        if i < 8:
            lo_ref[i] = wf
        else:
            hi_ref[i - 8] = wf


def by_colour(n, swap):
    lane, row = lanes(16), sublanes(16)
    odd = (row + n) % 2
    return (2 * (lane % 64) + jnp.where((lane < 64) != swap, odd, 1 - odd)) % 128


def spared(index):
    return (index + jnp.where(lanes(16) % 64 < 48, -12, 12)) % 128


def plane_f(wf, xl, xu, p):
    return xl.at[p] if p < 8 else wf.at[p - 8] if p < 24 else xu.at[p - 24]


def plane_b(wb, xl, xu, p):
    return xl.at[9 + p] if p < 8 else wb.at[p - 8] if p < 24 else xu.at[8 + p - 24]


def pack_rows(wf, wb, xl, xu, b0, b1, b2, b3, lo_ref, hi_ref, b1_ref):
    for back, b in enumerate((b0, b1, b2, b3)):
        b1_ref[back] = b[...]
    for p in range(32):
        f, b = plane_f(wf, xl, xu, p), plane_b(wb, xl, xu, p)
        lo_ref[p] = f[0:8]
        hi_ref[p] = f[24:32]
        lo_ref[32 + p] = b[0:8]
        hi_ref[32 + p] = b[24:32]
    for i in range(16):
        lo_ref[64 + i // 8, i % 8 : i % 8 + 1] = wb[i, 8:9]
        hi_ref[64 + i // 8, i % 8 : i % 8 + 1] = wb[i, 23:24]


def slab(plane, yl, yu, which, p):
    return jnp.concatenate([yl[32 * which + p], plane[...], yu[32 * which + p]], axis=0)


def pack_lanes(wf, wb, xl, xu, yl, yu, lo_ref, hi_ref):
    slot_of = lanes(48) % 64
    for which, width, base in ((0, 16, 0), (1, 16, 48)):
        count = 64 // width
        slot = slot_of // width
        for group in range(32 // count):
            for s in range(count):
                p = group * count + s
                plane = plane_b(wb, xl, xu, p) if which else plane_f(wf, xl, xu, p)
                v = turn(slab(plane, yl, yu, which, p), width * s)
                if s == 0:
                    low = high = v
                else:
                    low = jnp.where(slot == s, v, low)
                    high = jnp.where(slot == s - 1, v, high)
            start = base + 6 * group
            lo_ref[start : start + 6] = low.reshape(6, 8, 128)
            hi_ref[start : start + 6] = high.reshape(6, 8, 128)


def make_coefs(mine, other, f, coef, p, index, scale, rows, inside=None):
    r = slice(8, 8 + rows)
    centre = mine[p + 1, r]
    mid = other[p + 1, r]
    side = beside(mid, index)
    if inside is not None:
        side = jnp.where(inside, side, 0.0)
    others = (other[p, r], other[p + 2, r], other[p + 1, 7 : 7 + rows], other[p + 1, 9 : 9 + rows], mid, side)
    weights = [centre + b for b in others]
    total = weights[0]
    for w in weights[1:]:
        total = total + w
    inverse = jnp.where(centre > 0.0, 1.0 / jnp.where(centre > 0.0, total, 1.0), 0.0)
    for which in range(6):
        w = weights[which] * inverse
        if which == 5 and inside is not None:
            w = jnp.where(inside, w, 0.0)
        coef[which, p] = w
    coef[6, p] = f * (inverse * (2.0 / scale))
    coef[7, p] = total * (0.5 * scale)


def relaxed(other, coef, p, index, rows, first=0, shift=0):
    a = 8 + first
    r = slice(a, a + rows)
    c = slice(first, first + rows)
    q = p - shift
    mid = other[p + 1, r]
    out = coef[6, q, c] + coef[0, q, c] * other[p, r]
    out = out + coef[1, q, c] * other[p + 2, r]
    out = out + coef[2, q, c] * other[p + 1, a - 1 : a - 1 + rows]
    out = out + coef[3, q, c] * other[p + 1, a + 1 : a + 1 + rows]
    out = out + coef[4, q, c] * mid
    return out + coef[5, q, c] * beside(mid, index)


def pairs(start, stop, body, rows):
    count = stop - start
    most = 8 * GROUP if rows < 64 else 16 * GROUP
    width = max(w for w in (2, 4, 8, 16) if w == 2 or (count % w == 0 and w * rows <= most))

    def step(t, carry):
        for n in range(width):
            body(start + t * width + n, n % 2)
        return carry

    if count == width:
        step(0, 0)
    else:
        lax.fori_loop(0, count // width, step, 0)


def update(mine, other, coef, index, start, stop, rows, flip, shift=0):
    def body(p, parity):
        mine[p + 1, 8 : 8 + rows] = relaxed(other, coef, p, index[(parity + flip) % 2], rows, 0, shift)

    pairs(start, stop, body, rows)


def defect(red, black, cr, cb, p, parity, index, rows, first=0, shift=0):
    r = slice(8 + first, 8 + first + rows)
    c = slice(first, first + rows)
    er = cr[7, p - shift, c] * (relaxed(black, cr, p, index[parity], rows, first, shift) - red[p + 1, r])
    eb = cb[7, p - shift, c] * (relaxed(red, cb, p, index[1 - parity], rows, first, shift) - black[p + 1, r])
    return er, eb


def halve_rows(tmp, value, rows):
    tmp[0:rows] = value
    return 0.125 * (tmp[pl.ds(0, rows // 2, 2)] + tmp[pl.ds(1, rows // 2, 2)])


def double_rows(tmp, value, rows):
    tmp[pl.ds(0, rows, 2)] = value
    tmp[pl.ds(1, rows, 2)] = value


def fine_down(
    at, wf, wb, xl, xu, yl, yu, zl, zu, g_ref, cr_out, cb_out, br, bb, fr, fb, cr, cb, vr, vb, tmp, sems
):
    gx, gy, gz = at[0], at[1], at[2]
    lane, row = lanes(48), sublanes(48)
    own = lane < 64
    keep = own | ((lane < 96) & (gz < 7)) | ((lane >= 96) & (gz > 0))
    keep = keep & ((row >= 8) | (gy > 0)) & ((row < 40) | (gy < 3))
    kept = jnp.where(keep, 1.0, 0.0).astype(F32)
    below = jnp.where(gx > 0, 1.0, 0.0).astype(F32)
    above = jnp.where(gx < 3, 1.0, 0.0).astype(F32)
    left = jnp.where(gy > 0, 1.0, 0.0).astype(F32)
    right = jnp.where(gy < 3, 1.0, 0.0).astype(F32)
    clear((vr, vb))
    edge = jnp.zeros((8, 128), F32)
    for b in (br, bb):
        for q in range(34):
            b[q, 0:8] = edge
            b[q, 56:64] = edge
        for q in (0, 33):
            b[q, 8:56] = jnp.zeros((48, 128), F32)
    for which, width, base in ((0, 16, 0), (1, 16, 48)):
        count = 64 // width
        slot = (lane % 64) // width
        for p in range(32):
            plane = plane_b(wb, xl, xu, p) if which else plane_f(wf, xl, xu, p)
            w = slab(plane, yl, yu, which, p)
            s = p % count
            start = base + 6 * (p // count)
            up = zu[start : start + 6].reshape(48, 128)
            low = zl[start : start + 6].reshape(48, 128)
            both = jnp.where(slot == s, up, low)
            red = jnp.where(own, w, turn(both, 64 - width * s))
            black = jnp.where(own, turn(w, 64), turn(both, -width * s))
            if which:
                k = kept * below if p < 8 else kept * above if p >= 24 else kept
                br[p + 1, 8:56] = red * k
                bb[p + 1, 8:56] = black * k
            else:
                fr[p] = red
                fb[p] = black
    for a in range(2):
        for src, r, ok in ((yl, 7, left), (yu, 56, right)):
            v = src[64 + a] * ok
            t = turn(v, 64)
            for s in range(8):
                br[9 + 8 * a + s, r : r + 1] = v[s : s + 1]
                bb[9 + 8 * a + s, r : r + 1] = t[s : s + 1]
    for v, q in ((xl[8] * below, 0), (xu[16] * above, 33)):
        br[q, 16:48] = v
        bb[q, 16:48] = turn(v, 64)

    index = [side_rule(48, parity) for parity in range(2)]

    def coefs(p, parity):
        make_coefs(br, bb, fr[p], cr, p, index[parity], 1.0, 48)
        make_coefs(bb, br, fb[p], cb, p, index[1 - parity], 1.0, 48)
        vr[p + 1, 8:56] = cr[6, p]

    pairs(0, 32, coefs, 48)
    copies = [
        pltpu.make_async_copy(cr.at[:, pl.ds(4, 24)], cr_out, sems.at[0]),
        pltpu.make_async_copy(cb.at[:, pl.ds(3, 26)], cb_out.at[pl.ds(0, 8)], sems.at[1]),
        pltpu.make_async_copy(vb.at[pl.ds(4, 26), pl.ds(8, 48)], cb_out.at[8], sems.at[2]),
    ]
    copies[0].start()
    copies[1].start()
    update(vb, vr, cb, index, 0, 32, 48, 1)
    update(vr, vb, cr, index, 2, 30, 48, 0)
    update(vb, vr, cb, index, 2, 30, 48, 1)
    copies[2].start()
    inner = [side_rule(32, parity) for parity in range(2)]
    swap = gx >= 2
    lane16 = lanes(16)
    spare = (lane16 % 64 >= 38) & (lane16 % 64 < 58)
    for n in range(8):
        total = coarse = None
        for parity in range(2):
            p = 8 + 2 * n + parity
            er, eb = defect(vr, vb, cr, cb, p, parity, inner, 32, 8)
            b = br[p + 1, 16:48] + bb[p + 1, 16:48]
            total = er + eb if total is None else total + (er + eb)
            coarse = b if coarse is None else coarse + b
        f1 = pick(halve_rows(tmp, total, 32), by_colour(n, swap))
        b1 = halve_rows(tmp, coarse, 32)
        w1 = jnp.where(spare, pick(b1, spared(by_colour(n, swap))), f1)
        for copy in range(16):
            g_ref[copy, 16 * n : 16 * n + 16] = w1
    for c in copies:
        c.wait()


def across(g, a, start):
    r = slice(start, start + 16)
    return jnp.concatenate([g[4 * a + y, r] for y in range(4)], axis=0)


def joined_f(g, p):
    wa, wb = (across(g, p // 8 + up, 16 * (p % 8)) for up in (0, 2))
    half = lanes(64) < 64
    return jnp.where(half, wa, wb), turn(jnp.where(half, wb, wa), 64)


def across_b(gx, gy, held, a, n):
    back = (gx - a + 4) % 4
    r = slice(16 * n, 16 * n + 16)
    out = []
    for y in range(4):
        e = (gy - y + 4) % 4
        v = held[0][e, r]
        for d in range(1, 4):
            v = jnp.where(back == d, held[d][e, r], v)
        out.append(v)
    return jnp.concatenate(out, axis=0)


def joined_b(gx, gy, held, a, n):
    wa, wb = (across_b(gx, gy, held, a + up, n) for up in (0, 2))
    half = lanes(64) < 64
    reds = jnp.where(half, wa, turn(wb, 64)), jnp.where(half, turn(wa, 64), wb)
    return [(red, turn(red, -32)) for red in reds]


def seam(v, rows):
    r = slice(8, 8 + rows)
    half = lanes(rows) < 64
    v[0, r] = jnp.where(half, 0.0, turn(v[16, r], 64))
    v[17, r] = jnp.where(half, turn(v[1, r], 64), 0.0)


def mid_down(at, g, h0, h1, h2, h3, w2_ref, c_out, vb_out, br, bb, fr, fb, cr, cb, vr, vb, tmp, sems):
    gx, gy, gz = at[0], at[1], at[2]
    lane = lanes(64)
    own = lane % 64 < 32
    keep = own | ((lane % 64 < 48) & (gz < 7)) | ((lane % 64 >= 48) & (gz > 0))
    kept = jnp.where(keep, 1.0, 0.0).astype(F32)
    halo = (lane + jnp.where(lane % 64 < 48, 6, -6)) % 128
    clear((vr, vb))
    for b in (br, bb):
        b[:, 0:8] = jnp.zeros((18, 8, 128), F32)
        b[:, 72:80] = jnp.zeros((18, 8, 128), F32)
    for p in range(16):
        fr[p], fb[p] = joined_f(g, p)
    for a in range(2):
        for n in range(4):
            for up, (red, black) in enumerate(joined_b(gx, gy, (h0, h1, h2, h3), a, n)):
                p = 8 * a + n + 4 * up
                br[p + 1, 8:72] = kept * jnp.where(own, red, pick(fr[p], halo))
                bb[p + 1, 8:72] = kept * jnp.where(own, black, pick(fb[p], halo))
    seam(br, 64)
    seam(bb, 64)
    index = [side_index(64, parity, 64) for parity in range(2)]

    def coefs(p, parity):
        make_coefs(br, bb, fr[p], cr, p, index[parity], 0.25, 64)
        make_coefs(bb, br, fb[p], cb, p, index[1 - parity], 0.25, 64)
        vr[p + 1, 8:72] = cr[6, p]

    pairs(0, 16, coefs, 64)
    seam(vr, 64)
    window = pl.multiple_of(jnp.clip(gy * 16 - 8, 0, 32), 8)
    copies = [
        pltpu.make_async_copy(cr.at[:, :, pl.ds(window, 32)], c_out.at[0], sems.at[0]),
        pltpu.make_async_copy(cb.at[:, :, pl.ds(window, 32)], c_out.at[1], sems.at[1]),
        pltpu.make_async_copy(vb.at[:, pl.ds(window + 8, 32)], vb_out, sems.at[2]),
    ]
    copies[0].start()
    copies[1].start()
    update(vb, vr, cb, index, 0, 16, 64, 1)
    seam(vb, 64)
    update(vr, vb, cr, index, 0, 16, 64, 0)
    seam(vr, 64)
    update(vb, vr, cb, index, 0, 16, 64, 1)
    seam(vb, 64)
    copies[2].start()
    lane, row = lanes(32), sublanes(32)
    for n in range(8):
        total = coarse = None
        for parity in range(2):
            p = 2 * n + parity
            er, eb = defect(vr, vb, cr, cb, p, parity, index, 64)
            e = er + eb
            b = br[p + 1, 8:72] + bb[p + 1, 8:72]
            total = e if total is None else total + e
            coarse = b if coarse is None else coarse + b
        f2 = halve_rows(tmp, total, 64)
        b2 = halve_rows(tmp, coarse, 64)
        odd = (row + n) % 2
        idx = 64 * ((lane % 64) // 32) + 2 * (lane % 16) + jnp.where(lane % 32 < 16, odd, 1 - odd)
        w2 = jnp.where(lane < 64, pick(f2, idx), pick(b2, idx))
        w2_ref[n] = w2
    for c in copies:
        c.wait()


def transposed(blocks):
    slot = lanes(32) // 16
    for bit in (1, 2, 4):
        out = list(blocks)
        for i in range(8):
            if not i & bit:
                x, y = blocks[i], blocks[i + bit]
                out[i] = jnp.where(slot & bit == 0, x, turn(y, 16 * bit))
                out[i + bit] = jnp.where(slot & bit == 0, turn(x, -16 * bit), y)
        blocks = out
    return blocks


def level_scratch(planes, rows):
    return [pltpu.VMEM((planes + 2, rows + 16, 128), F32)] * 4 + [pltpu.VMEM((8, planes, rows, 128), F32)] * 2


def clear(refs, ends=1):
    for v in refs:
        planes, rows, _ = v.shape
        v[:, 0:8] = jnp.zeros((planes, 8, 128), F32)
        v[:, rows - 8 : rows] = jnp.zeros((planes, 8, 128), F32)
        v[0:ends] = jnp.zeros((ends, rows, 128), F32)
        v[planes - ends : planes] = jnp.zeros((ends, rows, 128), F32)


def smooth_down(br, bb, vr, vb, cr, cb, f_of, index, scale, planes, rows, inside):
    def coefs(p, parity):
        fr, fb = f_of(p)
        make_coefs(br, bb, fr, cr, p, index[parity], scale, rows, inside and inside[parity])
        make_coefs(bb, br, fb, cb, p, index[1 - parity], scale, rows, inside and inside[1 - parity])
        vr[p + 1, 8 : 8 + rows] = cr[6, p]

    pairs(0, planes, coefs, rows)
    update(vb, vr, cb, index, 0, planes, rows, 1)
    update(vr, vb, cr, index, 0, planes, rows, 0)
    update(vb, vr, cb, index, 0, planes, rows, 1)


def smooth_up(vr, vb, cr, cb, index, planes, rows):
    for _ in range(2):
        update(vr, vb, cr, index, 0, planes, rows, 0)
        update(vb, vr, cb, index, 0, planes, rows, 1)


def restrict(level, tmp, index, planes, rows, cells, put):
    br, bb, vr, vb, cr, cb = level
    lane, row = lanes(rows // 2), sublanes(rows // 2)
    for n in range(planes // 2):
        total = coarse = None
        for parity in range(2):
            p = 2 * n + parity
            er, eb = defect(vr, vb, cr, cb, p, parity, index, rows)
            b = br[p + 1, 8 : 8 + rows] + bb[p + 1, 8 : 8 + rows]
            total = er + eb if total is None else total + (er + eb)
            coarse = b if coarse is None else coarse + b
        f = halve_rows(tmp, total, rows)
        b = halve_rows(tmp, coarse, rows)
        odd = (row + n) % 2
        red = 2 * (lane % 64) + odd
        black = 2 * (lane % 64) + 1 - odd
        inside = lane < cells
        put(n, *[jnp.where(inside, pick(x, i), 0.0) for x in (f, b) for i in (red, black)])


def prolong(vr, vb, out, tmp, planes, rows):
    lane, row = lanes(rows), sublanes(rows)
    r = slice(8, 8 + rows)
    for n in range(planes):
        even = (row + lane + n) % 2 == 0
        c = jnp.where(even, pick(vr[n + 1, r], lane // 2), pick(vb[n + 1, r], lane // 2))
        double_rows(tmp, c, rows)
        for p in (2 * n, 2 * n + 1):
            out[p + 1, 8 : 8 + 2 * rows] += tmp[0 : 2 * rows]


def coarse_up(
    at, m0, m1, m2, m3, q0, q1, q2, q3, c1_in, v1b_in, c0r_in, c0b_in, u_ref, res_ref,
    b2r, b2b, v2r, v2b, c2r, c2b, f2,
    b3r, b3b, v3r, v3b, c3r, c3b, f3,
    b4r, b4b, v4r, v4b, c4r, c4b, f4,
    v1r, v1b, c1r, c1b, v0r, v0b, c0r, c0b, tmp, sems,
):
    gx, gy, gz = at[0], at[1], at[2]
    copies = [
        pltpu.make_async_copy(c1_in.at[0], c1r, sems.at[0]),
        pltpu.make_async_copy(c1_in.at[1], c1b, sems.at[1]),
        pltpu.make_async_copy(v1b_in, v1b.at[:, pl.ds(8, 32)], sems.at[2]),
        pltpu.make_async_copy(c0r_in, c0r, sems.at[3]),
        pltpu.make_async_copy(c0b_in.at[pl.ds(0, 8), pl.ds(1, 24)], c0b, sems.at[4]),
        pltpu.make_async_copy(c0b_in.at[8], v0b.at[pl.ds(4, 26), pl.ds(8, 48)], sems.at[5]),
    ]
    for c in copies:
        c.start()
    clear((b2r, b2b, v2r, v2b, b3r, b3b, v3r, v3b, b4r, b4b, v4r, v4b, v1r))
    clear((v0r,), 5)
    v0b[:, 0:8] = jnp.zeros((34, 8, 128), F32)
    v0b[:, 56:64] = jnp.zeros((34, 8, 128), F32)
    v1b[:, 0:8] = jnp.zeros((18, 8, 128), F32)
    v1b[:, 40:48] = jnp.zeros((18, 8, 128), F32)

    chip = gz // 2
    first = gz % 2 == 0
    for n in range(8):
        near = [(jnp.where(first, a[n], b[n]), jnp.where(first, b[n], a[n])) for a, b in ((m0, q0), (m1, q1), (m2, q2), (m3, q3))]
        blocks = []
        for c in range(4):
            for core in range(2):
                v = near[0][core]
                for back in range(1, 4):
                    v = jnp.where(chip == (c + back) % 4, near[back][core], v)
                blocks.append(v)
        out = transposed(blocks)
        for h in range(2):
            p = n + 8 * h
            f2[0, p] = out[2 * h]
            f2[1, p] = out[2 * h + 1]
            b2r[p + 1, 8:40] = out[4 + 2 * h]
            b2b[p + 1, 8:40] = out[5 + 2 * h]
    lane = lanes(32)
    index2 = [side_rule(32, parity) for parity in range(2)]
    inside2 = [lane != jnp.where(index2[parity], 0, 127) for parity in range(2)]
    smooth_down(b2r, b2b, v2r, v2b, c2r, c2b, lambda p: (f2[0, p], f2[1, p]), index2, 0.25**2, 16, 32, inside2)

    def put3(n, fr, fb, br, bb):
        f3[0, n], f3[1, n] = fr, fb
        b3r[n + 1, 8:24], b3b[n + 1, 8:24] = br, bb

    restrict((b2r, b2b, v2r, v2b, c2r, c2b), tmp, index2, 16, 32, 64, put3)

    index3 = [side_rule(16, parity) for parity in range(2)]
    smooth_down(b3r, b3b, v3r, v3b, c3r, c3b, lambda p: (f3[0, p], f3[1, p]), index3, 0.25**3, 8, 16, None)

    def put4(n, fr, fb, br, bb):
        f4[0, n], f4[1, n] = fr, fb
        b4r[n + 1, 8:16], b4b[n + 1, 8:16] = br, bb

    restrict((b3r, b3b, v3r, v3b, c3r, c3b), tmp, index3, 8, 16, 32, put4)

    index4 = [side_rule(8, parity) for parity in range(2)]

    for p in range(4):
        make_coefs(b4r, b4b, f4[0, p], c4r, p, index4[p % 2], 0.25**4, 8)
        make_coefs(b4b, b4r, f4[1, p], c4b, p, index4[1 - p % 2], 0.25**4, 8)
    row8 = sublanes(8)
    inner = (row8 > 0, row8 < 7)
    cr4 = [[c4r[w, p] for w in range(7)] for p in range(4)]
    cb4 = [[c4b[w, p] for w in range(7)] for p in range(4)]
    for c in cr4 + cb4:
        c[2] = jnp.where(inner[0], c[2], 0.0)
        c[3] = jnp.where(inner[1], c[3], 0.0)

    def half(other, coefs, flip):
        out = []
        for p in range(4):
            c, v = coefs[p], other[p]
            w = c[6] + c[4] * v
            if p > 0:
                w = w + c[0] * other[p - 1]
            if p < 3:
                w = w + c[1] * other[p + 1]
            w = w + c[2] * pltpu.roll(v, 1, 0) + c[3] * pltpu.roll(v, 7, 0)
            out.append(w + c[5] * beside(v, index4[(p + flip) % 2]))
        return out

    def coarse_step(count, state):
        black = list(state)
        red = half(black, cr4, 0)
        return tuple(half(red, cb4, 1))

    black = lax.fori_loop(0, COARSE_ITERS - 1, coarse_step, (jnp.zeros((8, 128), F32),) * 4)
    red = half(black, cr4, 0)
    black = half(red, cb4, 1)
    for p in range(4):
        v4r[p + 1, 8:16] = red[p]
        v4b[p + 1, 8:16] = black[p]

    prolong(v4r, v4b, v3b, tmp, 4, 8)
    smooth_up(v3r, v3b, c3r, c3b, index3, 8, 16)
    prolong(v3r, v3b, v2b, tmp, 8, 16)
    smooth_up(v2r, v2b, c2r, c2b, index2, 16, 32)

    for c in copies[:3]:
        c.wait()
    lane, row = lanes(32), sublanes(32)
    near = lane % 64 - jnp.where(lane % 64 < 48, 0, 64)
    cell = gz * 32 + near
    valid = (cell >= 0) & (cell < 256)
    idx = jnp.clip(cell, 0, 255) // 2
    window = pl.multiple_of(jnp.clip(gy * 16 - 8, 0, 32), 8)
    for n in range(8):
        even = (row + lane + n) % 2 == 0
        parts = []
        for p in (n, n + 8):
            parts.append(jnp.where(even, pick(v2r[p + 1, 8:40], idx), pick(v2b[p + 1, 8:40], idx)))
        c = jnp.where(valid, jnp.where(lane < 64, parts[0], parts[1]), 0.0)
        double_rows(tmp, c, 32)
        for p in (2 * n, 2 * n + 1):
            v1b[p + 1, 8:40] += tmp[pl.ds(window, 32)]
    seam(v1b, 32)
    index1 = [side_index(32, parity, 64) for parity in range(2)]
    for _ in range(2):
        update(v1r, v1b, c1r, index1, 0, 16, 32, 0)
        seam(v1r, 32)
        update(v1b, v1r, c1b, index1, 0, 16, 32, 1)
        seam(v1b, 32)

    for c in copies[3:]:
        c.wait()
    start = pl.multiple_of(gy * 16 - window, 8)
    cell = lane - jnp.where(lane < 96, 0, 128)
    idx = (cell // 2) % 64
    for n in range(-3, 11):
        plane = gx * 8 + n
        held = jnp.clip(plane, 0, 31)
        at_half = idx + 64 * (held // 16)
        even = (row + lane + n) % 2 == 0
        red = v1r[held % 16 + 1, pl.ds(start, 32)]
        black = v1b[held % 16 + 1, pl.ds(start, 32)]
        c = jnp.where(even, pick(red, at_half), pick(black, at_half))
        c = c * jnp.where((plane >= 0) & (plane < 32), 1.0, 0.0).astype(F32)
        tmp[64:96] = c
        double_rows(tmp, tmp[68:92], 24)
        for p in (2 * n + 8, 2 * n + 9):
            v0b[p + 1, 8:56] += tmp[0:48]
    index0 = [side_rule(48, parity) for parity in range(2)]
    update(v0r, v0b, c0r, index0, 4, 28, 48, 0, 4)
    update(v0b, v0r, c0b, index0, 4, 28, 48, 1, 4)
    update(v0r, v0b, c0r, index0, 6, 26, 48, 0, 4)
    update(v0b, v0r, c0b, index0, 6, 26, 48, 1, 4)

    def finish(p, parity):
        even = (row + lane + parity) % 2 == 0
        er, eb = defect(v0r, v0b, c0r, c0b, p, parity, index1_0, 32, 8, 4)
        res_ref[p - 8] = jnp.where(even, pick(er, lane // 2), pick(eb, lane // 2))
        red, black = v0r[p + 1, 16:48], v0b[p + 1, 16:48]
        u_ref[p - 8] = jnp.where(even, pick(red, lane // 2), pick(black, lane // 2))

    index1_0 = [side_rule(32, parity) for parity in range(2)]
    pairs(8, 24, finish, 32)


def around(lo, hi, axis):
    count = lax.axis_size(axis)
    from_above = lax.ppermute(lo, axis, [((i + 1) % count, i) for i in range(count)])
    from_below = lax.ppermute(hi, axis, [(i, (i + 1) % count) for i in range(count)])
    return from_below, from_above


def beyond(x, axis):
    count = lax.axis_size(axis)
    return [lax.ppermute(x, axis, [(i, (i + d) % count) for i in range(count)]) for d in range(1, count)]


def body(source, conductance):
    vmem, smem, hbm = (pl.BlockSpec(memory_space=m) for m in (pltpu.VMEM, pltpu.SMEM, pltpu.HBM))
    at = jnp.stack([lax.axis_index(a) for a in ("gx", "gy", "gz")]).astype(jnp.int32)
    dma = pltpu.SemaphoreType.DMA

    block, x_slab = arr(16, 32, 128), arr(17, 32, 128)
    wf, wb, lo, hi, b1 = call(
        split_fine,
        [(block, block, x_slab, x_slab, arr(64, 128))],
        (jnp.concatenate([source, conductance]),),
        None,
        [pltpu.VMEM((32, 128), F32)],
        8,
    )
    xl, xu = around(lo, hi, "gx")
    b1 = [b1] + beyond(b1, "gy")
    y_slab = arr(66, 8, 128)
    lo, hi, b1 = call(pack_rows, [(y_slab, y_slab, arr(4, 64, 128))], (wf, wb, xl, xu, *b1), limit=8)
    yl, yu = around(lo, hi, "gy")
    b1 = [b1] + beyond(b1, "gx")
    lo, hi = call(pack_lanes, [(arr(96, 8, 128),) * 2], (wf, wb, xl, xu, yl, yu), limit=8)
    zl, zu = around(lo, hi, "gz")
    zl, zu, *b1 = lax.optimization_barrier((zl, zu, *b1))

    colour0 = pltpu.VMEM((34, 64, 128), F32)
    right0 = pltpu.VMEM((32, 48, 128), F32)
    coef0 = pltpu.VMEM((8, 32, 48, 128), F32)
    state0 = (arr(8, 24, 48, 128), arr(9, 26, 48, 128))
    g, c0r, c0b = call(
        fine_down,
        [(arr(16, 128, 128),) + state0, (vmem, hbm, hbm)],
        (at, wf, wb, xl, xu, yl, yu, zl, zu),
        [smem] + [vmem] * 8,
        [colour0, colour0, right0, right0, coef0, coef0, colour0, colour0, pltpu.VMEM((32, 128), F32), dma((3,))],
        LIMIT_FINE,
    )
    g = lax.all_to_all(g, ("gx", "gy"), 0, 0, tiled=True)

    state1 = (arr(2, 8, 16, 32, 128), arr(18, 32, 128))
    colour1 = pltpu.VMEM((18, 80, 128), F32)
    right1 = pltpu.VMEM((16, 64, 128), F32)
    coef1 = pltpu.VMEM((8, 16, 64, 128), F32)
    w2, c1, v1b = call(
        mid_down,
        [(arr(8, 32, 128),) + state1, (vmem, hbm, hbm)],
        (at, g, *b1),
        [smem] + [vmem] * 5,
        [colour1, colour1, right1, right1, coef1, coef1, colour1, colour1, pltpu.VMEM((64, 128), F32), dma((3,))],
        LIMIT_MID,
    )
    mine = [w2] + [lax.ppermute(w2, "gz", [(i, (i + d) % 8) for i in range(8)]) for d in (2, 4, 6)]
    pair = [lax.ppermute(w, "gz", [(i, i ^ 1) for i in range(8)]) for w in mine]

    scratch = []
    for planes, rows in ((16, 32), (8, 16), (4, 8)):
        scratch += level_scratch(planes, rows) + [pltpu.VMEM((2, planes, rows, 128), F32)]
    scratch += [pltpu.VMEM((18, 48, 128), F32)] * 2 + [pltpu.VMEM((8, 16, 32, 128), F32)] * 2
    scratch += [colour0] * 2 + [pltpu.VMEM((8, 24, 48, 128), F32)] * 2
    scratch += [pltpu.VMEM((96, 128), F32), dma((6,))]
    return call(
        coarse_up,
        [(block, block)],
        (at, *mine, *pair, c1, v1b, c0r, c0b),
        [smem] + [vmem] * 8 + [hbm] * 4,
        scratch,
        LIMIT_UP,
    )


def solution(mesh):
    placed = (P("gx", "gy", "gz"), P("gx", "gy", "gz"))
    return jax.shard_map(body, mesh=mesh, in_specs=placed, out_specs=placed, check_vma=False)
```
